32 devices in a mesh: row: 8 (over y, x, core), col: 4 (over z).
Axes of the slice: x: 2, y: 2, z: 4, core: 2. Of those that a mesh axis runs over, the one named last changes fastest.
Arguments:
- layer_in: bfloat16 [2, 1024, 2048], P(None, 'row', 'col'), may hold values from -6 to 6
- out_grad: bfloat16 [2, 1024, 2048], P(None, 'row', 'col'), may hold values from -6 to 6
- lengths: int32 [2, 4], replicated, may hold values from 1 to 682, 1024 in all within a row
- token_order: int32 [2, 1024], replicated, may hold values from 0 to 1023, each once within a row
- choices: int32 [2, 1024, 8], P(None, 'row'), may hold values from 0 to 15, all different within a row
- norm_gain: float32 [2048], replicated, may hold values from 0.5 to 1.5
- w_query: bfloat16 [2048, 4096], P('row', 'col'), may hold values from -0.125 to 0.125
- w_key: bfloat16 [2048, 512], P('row', 'col'), may hold values from -0.125 to 0.125
- w_value: bfloat16 [2048, 512], P('row', 'col'), may hold values from -0.125 to 0.125
- query_gain: float32 [128], replicated, may hold values from 0.5 to 1.5
- key_gain: float32 [128], replicated, may hold values from 0.5 to 1.5
- w_out: bfloat16 [2048, 4096], P('row', 'col'), may hold values from -0.75 to 0.75
- ffn_gain: float32 [2048], replicated, may hold values from 0.5 to 1.5
- w_router: bfloat16 [2048, 16], P('row'), may hold values from -0.0625 to 0.0625
- w_gate: bfloat16 [2048, 12288], P('row', 'col'), may hold values from -0.125 to 0.125
- w_up: bfloat16 [2048, 12288], P('row', 'col'), may hold values from -0.125 to 0.125
- w_down: bfloat16 [2048, 12288], P('row', 'col'), may hold values from -0.875 to 0.875
Outputs:
- layer_out: bfloat16 [2, 1024, 2048], P(None, 'row', 'col')
- input_grad: bfloat16 [2, 1024, 2048], P(None, 'row', 'col')
- grad_norm_gain: float32 [2048], replicated
- grad_w_query: float32 [2048, 4096], P('row', 'col')
- grad_w_key: float32 [2048, 512], P('row', 'col')
- grad_w_value: float32 [2048, 512], P('row', 'col')
- grad_query_gain: float32 [128], replicated
- grad_key_gain: float32 [128], replicated
- grad_w_out: float32 [2048, 4096], P('row', 'col')
- grad_ffn_gain: float32 [2048], replicated
- grad_w_router: float32 [2048, 16], P('row')
- grad_w_gate: float32 [2048, 12288], P('row', 'col')
- grad_w_up: float32 [2048, 12288], P('row', 'col')
- grad_w_down: float32 [2048, 12288], P('row', 'col')
The draws below stay inside these ranges and needn't reach their ends.
Inputs may be any that keep to these rules, and one draw needn't show every extreme that they name: `lengths`: each row sums to 1024 and its largest entry is 682. `token_order`: each row holds every number from 0 to 1023 once. `choices`: the 8 entries of a token are distinct.
All inputs are finite; a program needn't handle non-finite values.
Results may differ from the reference program's by a relative error of at most 0.015.
Values may be sent and summed in bfloat16 or wider, within the bound.
No kernel may reach another device: no remote copies, remote signals or barrier semaphores. Data moves between devices by JAX's collectives and lax.ppermute only.
A program may use at most 576 MiB of HBM per device.

```python
import math
import jax
import jax.numpy as jnp
import numpy as np
from jax import lax

D = 2048
HEADS = 32
KV = 4
HEAD = 128
FF = 768
TOPK = 8
EXPERTS = 16
MICRO = 2
SEQS = 4
TOKENS = 1024
SEQ_MAX = 682


def steps_of(stream_key, extent, shards, smallest, largest):
    def one(position, blocks):
        draws = jax.random.uniform(jax.random.fold_in(jax.random.fold_in(stream_key, 6), position), (blocks,), jnp.float32, smallest / len(shards), largest / len(shards))
        return jnp.repeat(jnp.exp(draws), extent[position] // blocks).reshape((-1,) + (1,) * (len(extent) - position - 1))

    level = one(*shards[0])
    for cut in shards[1:]:
        level = level * one(*cut)
    return level


def picks_of(own_key, rows, amount, top, lift):
    sequence = jax.random.permutation(jax.random.fold_in(own_key, 1), amount)
    pull = sequence
    for power in range(3):
        pull = pull * pull // amount
    pull = pull * lift // amount
    chance = jax.random.randint(jax.random.fold_in(own_key, 2), (rows, amount), 0, 4096) + pull
    sure = jax.random.permutation(jax.random.fold_in(own_key, 3), rows)[jnp.arange(amount) % rows]
    chance = jnp.where(jnp.arange(rows)[:, None] == sure[None, :], 1 << 14, chance)
    merit = chance * amount + jnp.arange(amount)
    return lax.top_k(merit.astype(jnp.int32), top)[1].astype(jnp.int32)


def split_up(count, total, reach, lean):
    weights = [(1 << 20) // math.isqrt(standing ** lean) + 1 for standing in range(2, count + 1)]
    rest, counts = total - reach - (count - 1), [1] * (count - 1)
    while rest > 0:
        movable = [i for i in range(count - 1) if counts[i] < reach]
        pool, budget = sum([weights[i] for i in movable]), rest
        for i in movable:
            extra = min(reach - counts[i], max(1, budget * weights[i] // pool), rest)
            counts[i] = counts[i] + extra
            rest = rest - extra
    return np.array([reach] + counts)


def ragged_sizes(stream_key, amount, total, reach, slope):
    if amount == 2:
        one = jax.random.randint(stream_key, (), max(1, total - reach), min(reach, total - 1) + 1)
        return jnp.stack([one, total - one])
    sizes = jnp.asarray(split_up(amount, total, reach, slope), jnp.int32)
    couples = (amount - 1) // 2
    donor, sink = sizes[1:1 + 2 * couples:2], sizes[2:2 + 2 * couples:2]
    room = jnp.minimum(donor - 1, reach - sink)
    moved = jax.random.randint(jax.random.fold_in(stream_key, 1), (couples,), 0, 1 << 20) % (room + 1)
    sizes = sizes.at[1:1 + 2 * couples:2].set(donor - moved).at[2:2 + 2 * couples:2].set(sink + moved)
    return sizes[jax.random.permutation(jax.random.fold_in(stream_key, 2), amount)]


def centred(key, dims, spread, bound, cuts=(), held_as=jnp.bfloat16):
    values = jax.random.normal(key, dims, jnp.float32) * spread
    if len(cuts) > 0:
        values = steps_of(key, dims, cuts, -0.22, 0.18) * values
    return jnp.clip(values, min=-bound, max=bound).astype(held_as)


def setup_inputs(seed: int = 0) -> dict:
    arg_keys = jax.random.split(jax.random.key(seed), 18)
    return {
        "layer_in": centred(arg_keys[0], (MICRO, TOKENS, D), 1.0, 6.0, ((1, 8), (2, 4))),
        "out_grad": centred(arg_keys[1], (MICRO, TOKENS, D), 1.0, 6.0, ((1, 8), (2, 4))),
        "lengths": jax.vmap(lambda own: ragged_sizes(own, SEQS, TOKENS, SEQ_MAX, 1))(jax.random.split(arg_keys[2], MICRO)).reshape((MICRO, SEQS)).astype(jnp.int32),
        "token_order": jax.vmap(lambda own: jax.random.permutation(own, TOKENS))(jax.random.split(arg_keys[3], MICRO)).reshape((MICRO, TOKENS)).astype(jnp.int32),
        "choices": picks_of(arg_keys[4], MICRO * TOKENS, EXPERTS, TOPK, 4096).reshape((MICRO, TOKENS, TOPK)),
        "norm_gain": jnp.clip(1.0 + 0.1 * jax.random.normal(arg_keys[5], (D,), jnp.float32), 0.5, 1.5),
        "w_query": centred(arg_keys[6], (D, HEADS * HEAD), D ** -0.5, 0.125, ((0, 8), (1, 4))),
        "w_key": centred(arg_keys[7], (D, KV * HEAD), D ** -0.5, 0.125, ((0, 8), (1, 4))),
        "w_value": centred(arg_keys[8], (D, KV * HEAD), D ** -0.5, 0.125, ((0, 8), (1, 4))),
        "query_gain": jnp.clip(1.0 + 0.1 * jax.random.normal(arg_keys[9], (HEAD,), jnp.float32), 0.5, 1.5),
        "key_gain": jnp.clip(1.0 + 0.1 * jax.random.normal(arg_keys[10], (HEAD,), jnp.float32), 0.5, 1.5),
        "w_out": centred(arg_keys[11], (D, HEADS * HEAD), (HEADS * HEAD // 64) ** -0.5, 0.75, ((0, 8), (1, 4))),
        "ffn_gain": jnp.clip(1.0 + 0.1 * jax.random.normal(arg_keys[12], (D,), jnp.float32), 0.5, 1.5),
        "w_router": centred(arg_keys[13], (D, EXPERTS), (4 * D) ** -0.5, 0.0625, ((0, 8),)),
        "w_gate": centred(arg_keys[14], (D, FF * EXPERTS), D ** -0.5, 0.125, ((0, 8), (1, 4))),
        "w_up": centred(arg_keys[15], (D, FF * EXPERTS), D ** -0.5, 0.125, ((0, 8), (1, 4))),
        "w_down": centred(arg_keys[16], (D, FF * EXPERTS), (FF // 16) ** -0.5, 0.875, ((0, 8), (1, 4))),
    }


EPS = 1e-06
THETA = 1000000.0
NEGATIVE = -1e+30
HIGH = lax.Precision.HIGHEST

@jax.custom_vjp
def low(v):
    return lax.optimization_barrier(v.astype(jnp.bfloat16)).astype(jnp.float32)

@jax.custom_vjp
def low_back(v):
    return v

def low_keep(v):
    return (low(v), None)

def low_pass(kept, grad):
    return (grad,)

def back_keep(v):
    return (v, None)

def back_low(kept, grad):
    return (low(grad),)
low.defvjp(low_keep, low_pass)
low_back.defvjp(back_keep, back_low)

def normed(tensor, gain_row):
    return tensor * lax.rsqrt(lax.optimization_barrier(jnp.mean(tensor * tensor, axis=-1, keepdims=True)) + EPS) * gain_row

def rotated(tensor, places):
    half_size = tensor.shape[-1] // 2
    frequency = jnp.exp(jnp.arange(half_size, dtype=jnp.float32) * (-2.0 * math.log(THETA) / tensor.shape[-1]))
    angles = places.astype(jnp.float32)[:, None] * frequency[None, :]
    cosine = jnp.cos(angles)[:, None, :]
    sine_part = jnp.sin(angles)[:, None, :]
    first_half = tensor[..., :half_size]
    second = tensor[..., half_size:]
    return jnp.concatenate([first_half * cosine - second * sine_part, second * cosine + first_half * sine_part], axis=-1)

def token_places(lengths, token_order):
    seq_ends = jnp.cumsum(lengths).astype(jnp.int32)
    passed = token_order[:, None] >= seq_ends[None, :]
    seq_of = lax.optimization_barrier(jnp.sum(passed.astype(jnp.int32), axis=1)).astype(jnp.int32)
    start_of = lax.optimization_barrier(jnp.sum(jnp.where(passed, lengths[None, :], 0), axis=1)).astype(jnp.int32)
    return (seq_of, (token_order - start_of).astype(jnp.int32))

def layer(hidden_in, params, seq_of, packed, places, chosen):
    norm_gain, w_query, w_key, w_value, query_gain, key_gain, w_out, ffn_gain, w_router, w_gate, w_up, w_down = params
    tokens = hidden_in.shape[0]
    head_size = query_gain.shape[0]
    num_heads = w_query.shape[1] // head_size
    kv_heads = w_key.shape[1] // head_size
    group_size = num_heads // kv_heads
    expert_count = w_router.shape[1]
    width = w_gate.shape[0]
    gate_cube = w_gate.reshape(width, -1, expert_count)
    up_cube = w_up.reshape(width, -1, expert_count)
    down_cube = w_down.reshape(width, -1, expert_count)
    block_rows = math.gcd(tokens, 512)
    score_scale = 1.0 / math.sqrt(head_size)
    normed_one = low(normed(hidden_in, norm_gain))
    queries = low_back(jnp.dot(normed_one, w_query, precision=HIGH)).reshape(tokens, num_heads, head_size)
    key_rows = low_back(jnp.dot(normed_one, w_key, precision=HIGH)).reshape(tokens, kv_heads, head_size)
    values = low(low_back(jnp.dot(normed_one, w_value, precision=HIGH))).reshape(tokens, kv_heads, head_size)
    queries = low(rotated(normed(queries, query_gain), places)).reshape(tokens, kv_heads, group_size, head_size)
    key_rows = low(rotated(normed(key_rows, key_gain), places))

    def attend(pieces):
        query_block, seq_block, pack_block = pieces
        scores = low_back(jnp.einsum('qgjd,kgd->gjqk', query_block, key_rows, precision=HIGH) * score_scale)
        allowed = (seq_block[:, None] == seq_of[None, :]) & (packed[None, :] <= pack_block[:, None])
        scores = jnp.where(allowed[None, None], scores, NEGATIVE)
        weights = low(jax.nn.softmax(scores, axis=-1))
        return jnp.einsum('gjqk,kgd->qgjd', weights, values, precision=HIGH)
    mixed = lax.map(jax.checkpoint(attend), (queries.reshape(tokens // block_rows, block_rows, kv_heads, group_size, head_size), seq_of.reshape(-1, block_rows), packed.reshape(-1, block_rows)))
    attended = low(low_back(mixed.reshape(tokens, num_heads * head_size)))
    residual = hidden_in + low_back(jnp.dot(attended, w_out.T, precision=HIGH))
    normed_two = low(normed(residual, ffn_gain))
    logits = low_back(jnp.dot(normed_two, w_router, precision=HIGH))
    gate_probs = jax.nn.softmax(jnp.where(chosen, logits, NEGATIVE), axis=-1)

    def experts(pieces):
        token_block, prob_block = pieces
        gate_pre = low_back(jnp.einsum('td,dfe->tfe', token_block, gate_cube, precision=HIGH))
        up_pre = low_back(jnp.einsum('td,dfe->tfe', token_block, up_cube, precision=HIGH))
        weighted = low(prob_block[:, None, :] * jax.nn.silu(gate_pre) * up_pre)
        return jnp.einsum('tfe,dfe->td', weighted, down_cube, precision=HIGH)
    expert_sum = lax.map(jax.checkpoint(experts), (normed_two.reshape(-1, block_rows, normed_two.shape[1]), gate_probs.reshape(-1, block_rows, gate_probs.shape[1])))
    return residual + low_back(expert_sum.reshape(tokens, -1))

def reference(layer_in, out_grad, lengths, token_order, choices, norm_gain, w_query, w_key, w_value, query_gain, key_gain, w_out, ffn_gain, w_router, w_gate, w_up, w_down):
    params = tuple((weight.astype(jnp.float32) for weight in (norm_gain, w_query, w_key, w_value, query_gain, key_gain, w_out, ffn_gain, w_router, w_gate, w_up, w_down)))
    expert_count = w_router.shape[1]
    totals = None
    layer_outs = []
    input_grads = []
    for batch_index in range(layer_in.shape[0]):
        seq_of, places = token_places(lengths[batch_index], token_order[batch_index])
        chosen = jnp.any(choices[batch_index][:, :, None] == jnp.arange(expert_count, dtype=jnp.int32)[None, None, :], axis=1)
        packed = token_order[batch_index]

        def run(hidden_in, weights):
            return layer(hidden_in, weights, seq_of, packed, places, chosen)
        result, pullback = jax.vjp(run, layer_in[batch_index].astype(jnp.float32), params)
        grad_in, grad_weights = pullback(out_grad[batch_index].astype(jnp.float32))
        layer_outs.append(result.astype(jnp.bfloat16))
        input_grads.append(grad_in.astype(jnp.bfloat16))
        totals = grad_weights if totals is None else jax.tree.map(jnp.add, totals, grad_weights)
    return (jnp.stack(layer_outs), jnp.stack(input_grads), totals[0], totals[1], totals[2], totals[3], totals[4], totals[5], totals[6], totals[7], totals[8], totals[9], totals[10], totals[11])
```

```python
import functools
import math

import jax
import jax.numpy as jnp
from jax import lax
from jax.experimental import pallas as pl
from jax.experimental.pallas import tpu as pltpu
from jax.sharding import Mesh
from jax.sharding import PartitionSpec as P

EPS = 1e-06
THETA = 1000000.0
NEGATIVE = -1e30
F32 = jnp.float32
BF16 = jnp.bfloat16
VMEM_BYTES = 56 * 1024 * 1024
LANES = 128
ROW = ("outer", "core")


def angles_of(places, head_size):
    half_size = head_size // 2
    frequency = jnp.exp(jnp.arange(half_size, dtype=F32) * (-2.0 * math.log(THETA) / head_size))
    angles = places.astype(F32)[:, None] * frequency[None, :]
    cosine, sine = jnp.cos(angles), jnp.sin(angles)
    return jnp.concatenate([cosine, cosine], axis=1), jnp.concatenate([-sine, sine], axis=1)


def token_places(lengths, token_order):
    seq_ends = jnp.cumsum(lengths)
    passed = token_order[:, None] >= seq_ends[None, :]
    seq_of = jnp.sum(passed.astype(jnp.int32), axis=1)
    start_of = jnp.sum(jnp.where(passed, lengths[None, :], 0), axis=1)
    return (seq_of, token_order - start_of)


def dot(a, b):
    return jnp.dot(a, b, preferred_element_type=F32)


def dot_bt(a, b):
    return lax.dot_general(a, b, (((1,), (1,)), ((), ())), preferred_element_type=F32)


def dot_at(a, b):
    return lax.dot_general(a, b, (((0,), (0,)), ((), ())), preferred_element_type=F32)


def two_parts(a):
    high = a.astype(BF16)
    return high, (a - high.astype(F32)).astype(BF16)


ANY = pl.BlockSpec(memory_space=pl.ANY)
SMEM = pl.BlockSpec(memory_space=pltpu.SMEM)


def whole(shape):
    return pl.BlockSpec(shape, lambda *_: (0,) * len(shape))


def params(steps=1):
    return pltpu.CompilerParams(
        dimension_semantics=("arbitrary",) * steps, vmem_limit_bytes=VMEM_BYTES
    )


def cost(flops, moved):
    return pl.CostEstimate(flops=int(flops), bytes_accessed=int(moved), transcendentals=0)


def nbytes(arrays):
    return sum(math.prod(a.shape) * a.dtype.itemsize for a in arrays)


def struct(shape, dtype):
    return jax.ShapeDtypeStruct(shape, dtype)


def weight_copies(at, pairs, fulls, sems, firsts=None):
    copies = []
    for i, ((own, other), full) in enumerate(zip(pairs, fulls)):
        cols, half = own.shape[0], own.shape[1]
        first = firsts[i] if firsts else 0
        for k in range(cols):
            for h, source in enumerate((own, other)):
                copies.append(
                    pltpu.make_async_copy(
                        source.at[at ^ k, :, pl.ds(first, full.shape[1])],
                        full.at[pl.ds((2 * k + h) * half, half)],
                        sems.at[len(copies)],
                    )
                )
    return copies


def load_weights(at, pairs, fulls, sems, firsts=None):
    copies = weight_copies(at, pairs, fulls, sems, firsts)
    for copy in copies:
        copy.start()
    for copy in copies:
        copy.wait()


def full_weight(pair, n=None):
    cols, half, _ = pair[0].shape
    n = n or pair[0].shape[2]
    return pltpu.VMEM((2 * cols * half, n), BF16)


def weight_sems(*pairs):
    return pltpu.SemaphoreType.DMA((sum(2 * pair[0].shape[0] for pair in pairs),))


def rms_scale(pieces, width):
    total = sum(jnp.sum(piece * piece, axis=1, keepdims=True) for piece in pieces)
    return lax.rsqrt(total / width + EPS)


def project(at, pieces, gain, pair, query_gain, key_gain, cosine, sine, heads, kv_heads):
    parts = len(pieces)
    tokens, part = pieces[0].shape
    width = parts * part
    n = pair[0].shape[2]
    size = query_gain.shape[1]

    def kernel(at_ref, *refs):
        ins, refs = refs[:parts], refs[parts:]
        gain_ref, own, other, qg, kg, cos_ref, sin_ref, normed, pre, ready, full, sems = refs
        copies = weight_copies(at_ref[0], [(own, other)], [full], sems)
        for copy in copies:
            copy.start()
        values = [ref[...].astype(F32) for ref in ins]
        scale = rms_scale(values, width)
        for k, value in enumerate(values):
            cut = slice(k * part, (k + 1) * part)
            normed[:, cut] = (value * scale * gain_ref[:, cut]).astype(BF16)
        for copy in copies:
            copy.wait()
        pre[...] = dot(normed[...], full[...])
        cosine, sine = cos_ref[...], sin_ref[...]
        for i in range(n // size):
            cut = slice(i * size, (i + 1) * size)
            head = pre[:, cut]
            if i < heads + kv_heads:
                head_gain = qg[...] if i < heads else kg[...]
                head = (
                    head
                    * lax.rsqrt(jnp.mean(head * head, axis=1, keepdims=True) + EPS)
                    * head_gain
                )
                head = head * cosine + pltpu.roll(head, size // 2, 1) * sine
            ready[:, cut] = head.astype(BF16)

    outs = (
        struct((tokens, width), BF16),
        struct((tokens, n), F32),
        struct((tokens, n), BF16),
    )
    ins = (*pieces, gain, *pair, query_gain, key_gain, cosine, sine)
    return pl.pallas_call(
        kernel,
        out_shape=outs,
        in_specs=[SMEM]
        + [whole(a.shape) for a in pieces]
        + [whole(gain.shape), ANY, ANY]
        + [whole(a.shape) for a in (query_gain, key_gain, cosine, sine)],
        out_specs=[whole(o.shape) for o in outs],
        scratch_shapes=[full_weight(pair), weight_sems(pair)],
        grid=(1,),
        compiler_params=params(),
        cost_estimate=cost(2 * tokens * width * n, nbytes(ins + outs)),
        name="project",
    )(at, *ins)


def attend(ready, own, other, bias, heads, kv_heads, size):
    micro, keys, tok = bias.shape
    group = heads // kv_heads
    outer = own.shape[0]
    scale = 1.0 / math.sqrt(size)

    def kernel(q_ref, k0, k1, v0, v1, bias_ref, out_ref, lse_ref):
        key = jnp.concatenate([r[...].reshape(outer * tok, size) for r in (k0, k1)], axis=0)
        value = jnp.concatenate([r[...].reshape(outer * tok, size) for r in (v0, v1)], axis=0)
        scores = dot_bt(key, q_ref[...]) * scale + bias_ref[0]
        peak = jnp.max(scores, axis=0, keepdims=True)
        powers = jnp.exp(scores - peak)
        total = jnp.sum(powers, axis=0, keepdims=True)
        probs = (powers * (1.0 / total)).astype(BF16)
        out_ref[...] = dot_at(probs, value).astype(BF16)
        lse_ref[0, 0] = peak + jnp.log(total)

    def kv_spec(first):
        return pl.BlockSpec((outer, tok, size), lambda m, h: (0, m, first + h // group))

    outs = (struct((micro * tok, heads * size), BF16), struct((micro, heads, 1, tok), F32))
    return pl.pallas_call(
        kernel,
        out_shape=outs,
        grid=(micro, heads),
        in_specs=[
            pl.BlockSpec((tok, size), lambda m, h: (m, h)),
            kv_spec(0),
            kv_spec(0),
            kv_spec(kv_heads),
            kv_spec(kv_heads),
            pl.BlockSpec((1, keys, tok), lambda m, h: (m, 0, 0)),
        ],
        out_specs=[
            pl.BlockSpec((tok, size), lambda m, h: (m, h)),
            pl.BlockSpec((1, 1, 1, tok), lambda m, h: (m, h, 0, 0)),
        ],
        compiler_params=params(2),
        cost_estimate=cost(4 * micro * heads * keys * tok * size, nbytes((ready, own, other, bias))),
        name="attend",
    )(ready, own, other, own, other, bias)


def attend_back(ready, own, other, bias, lse, grad, heads, kv_heads, size):
    micro, keys, tok = bias.shape
    group = heads // kv_heads
    outer = own.shape[0]
    scale = 1.0 / math.sqrt(size)
    mid = keys // 2

    def kernel(q_ref, k0, k1, v0, v1, bias_ref, lse_ref, g_ref, gq, gk0, gk1, gv0, gv1):
        first = pl.program_id(1) % group == 0
        key = jnp.concatenate([r[...].reshape(outer * tok, size) for r in (k0, k1)], axis=0)
        value = jnp.concatenate([r[...].reshape(outer * tok, size) for r in (v0, v1)], axis=0)
        query, out_grad = q_ref[...], g_ref[...]
        scores = dot_bt(key, query) * scale + bias_ref[0]
        probs = jnp.exp(scores - lse_ref[0, 0])
        back = dot_bt(value, out_grad)
        centre = jnp.sum(probs * back, axis=0, keepdims=True)
        slope = (probs * (back - centre)).astype(BF16)
        gq[...] = dot_at(slope, key) * scale
        key_part = dot(slope, query) * scale
        value_part = dot(probs.astype(BF16), out_grad)
        for ref, part in (
            (gk0, key_part[:mid]),
            (gk1, key_part[mid:]),
            (gv0, value_part[:mid]),
            (gv1, value_part[mid:]),
        ):
            part = part.reshape(outer, tok, size)
            before = jnp.where(first, 0.0, ref[...])
            ref[...] = before + part

    def kv_spec(start):
        return pl.BlockSpec((outer, tok, size), lambda m, h: (0, m, start + h // group))

    head_spec = pl.BlockSpec((tok, size), lambda m, h: (m, h))
    kv_shape = struct((outer, micro * tok, kv_heads * size), F32)
    outs = (struct((micro * tok, heads * size), F32), kv_shape, kv_shape, kv_shape, kv_shape)
    return pl.pallas_call(
        kernel,
        out_shape=outs,
        grid=(micro, heads),
        in_specs=[
            head_spec,
            kv_spec(0),
            kv_spec(0),
            kv_spec(kv_heads),
            kv_spec(kv_heads),
            pl.BlockSpec((1, keys, tok), lambda m, h: (m, 0, 0)),
            pl.BlockSpec((1, 1, 1, tok), lambda m, h: (m, h, 0, 0)),
            head_spec,
        ],
        out_specs=[head_spec] + [kv_spec(0)] * 4,
        compiler_params=params(2),
        cost_estimate=cost(
            10 * micro * heads * keys * tok * size, nbytes((ready, own, other, bias) + outs)
        ),
        name="attend_back",
    )(ready, own, other, own, other, bias, lse, grad)


def expand(at, a, pair, part):
    tokens, n = a.shape
    cols = pair[0].shape[0]
    outs = [struct((tokens, part), F32 if k == 0 else BF16) for k in range(cols)]

    def kernel(at_ref, a_ref, own, other, *refs):
        outs, (full, sems) = refs[:cols], refs[cols:]
        load_weights(at_ref[0], [(own, other)], [full], sems)
        for k, out in enumerate(outs):
            out[...] = dot_bt(a_ref[...], full[k * part : (k + 1) * part]).astype(out.dtype)

    return pl.pallas_call(
        kernel,
        out_shape=outs,
        in_specs=[SMEM, whole(a.shape), ANY, ANY],
        out_specs=[whole(o.shape) for o in outs],
        scratch_shapes=[full_weight(pair, n), weight_sems(pair)],
        grid=(1,),
        compiler_params=params(),
        cost_estimate=cost(2 * tokens * n * part * cols, nbytes((a, *pair))),
        name="expand",
    )(at, a, *pair)


def contract(at, pieces, pair, n):
    parts = len(pieces)
    tokens, part = pieces[0].shape
    outs = struct((tokens, n), BF16)

    def kernel(at_ref, *refs):
        ins, (own, other, out, full, sems) = refs[:parts], refs[parts:]
        load_weights(at_ref[0], [(own, other)], [full], sems)
        joined = jnp.concatenate([ref[...] for ref in ins], axis=1)
        out[...] = dot(joined, full[...]).astype(BF16)

    return pl.pallas_call(
        kernel,
        out_shape=outs,
        in_specs=[SMEM] + [whole(a.shape) for a in pieces] + [ANY, ANY],
        out_specs=whole(outs.shape),
        scratch_shapes=[full_weight(pair, n), weight_sems(pair)],
        grid=(1,),
        compiler_params=params(),
        cost_estimate=cost(2 * tokens * n * part * parts, nbytes((*pieces, *pair))),
        name="contract",
    )(at, *pieces, *pair)


def second_norm(pieces, gain):
    parts = len(pieces)
    tokens, part = pieces[0].shape
    width = parts * part
    out = struct((tokens, width), BF16)

    def kernel(*refs):
        ins, (gain_ref, out_ref) = refs[:parts], refs[parts:]
        values = [ref[...].astype(F32) for ref in ins]
        scale = rms_scale(values, width)
        for k, value in enumerate(values):
            cut = slice(k * part, (k + 1) * part)
            out_ref[:, cut] = (value * scale * gain_ref[:, cut]).astype(BF16)

    return pl.pallas_call(
        kernel,
        out_shape=out,
        in_specs=[whole(a.shape) for a in pieces] + [whole(gain.shape)],
        out_specs=whole(out.shape),
        grid=(1,),
        compiler_params=params(),
        cost_estimate=cost(tokens * width * 4, nbytes((*pieces, out))),
        name="second_norm",
    )(*pieces, gain)


def run_experts(at, first, tokens_in, grads, spread, high, low, router, router_at, before):
    count = len(tokens_in)
    tokens, width = tokens_in[0].shape
    hidden = low[0].shape[2]
    parts = low[0].shape[0]
    part = width // parts

    def kernel(at_ref, g_ref, c_ref, s_ref, *refs):
        x_refs, refs = refs[:count], refs[count:]
        pairs, refs = [refs[:2], refs[2:4], refs[4:6]], refs[6 + len(before) :]
        weighted, d_high, logit, dx, lo, full_high, full_low, r_ref, x_now, sems, x_sems = refs
        step = pl.program_id(0)
        fulls = [full_high, full_low, r_ref]
        copies = weight_copies(at_ref[0], pairs, fulls, sems, (0, 0, router_at))
        arrivals = [
            pltpu.make_async_copy(ref, x_now.at[i % 2], x_sems.at[i % 2])
            for i, ref in enumerate(x_refs)
        ]

        @pl.when(step == 0)
        def _():
            arrivals[0].start()
            for k in range(parts):
                for i in range(3):
                    for h in range(2):
                        copies[2 * parts * i + 2 * k + h].start()

        for i in range(count):

            @pl.when(step == i)
            def _(i=i):
                arrivals[i].wait()
                if i + 1 < count:
                    arrivals[i + 1].start()

        slot = lax.rem(step, 2)
        pre, back, logits = 0.0, 0.0, 0.0
        for k in range(parts):

            @pl.when(step == 0)
            def _(k=k):
                for i in range(3):
                    for h in range(2):
                        copies[2 * parts * i + 2 * k + h].wait()

            cut = slice(k * part, (k + 1) * part)
            x = x_now[slot, :, cut]
            pre = pre + dot(x, full_high[cut])
            back = back + dot(g_ref[0, :, cut], full_low[cut])
            logits = logits + dot(x, r_ref[cut])
        logits = jnp.where(c_ref[0] > 0, logits, NEGATIVE)
        peak = jnp.max(logits, axis=1, keepdims=True)
        powers = jnp.exp(logits - peak)
        gate_probs = powers / jnp.sum(powers, axis=1, keepdims=True)
        spread = s_ref[...]
        one, two = two_parts(gate_probs)
        probs_wide = dot(one, spread) + dot(two, spread)
        gate_pre, up_pre = pre[:, :hidden], pre[:, hidden:]
        sigmoid = 0.5 + 0.5 * jnp.tanh(0.5 * gate_pre)
        swish = gate_pre * sigmoid
        active = swish * up_pre
        weighted_now = (probs_wide * active).astype(BF16)
        weighted[...] = weighted_now
        gate_grad = dot_bt((active * back).astype(BF16), spread)
        logit_low = (
            gate_probs * (gate_grad - jnp.sum(gate_probs * gate_grad, axis=1, keepdims=True))
        ).astype(BF16)
        logit[...] = logit_low
        back = probs_wide * back
        d_high[:, :hidden] = (back * up_pre * (sigmoid + swish * (1.0 - sigmoid))).astype(BF16)
        d_high[:, hidden:] = (back * swish).astype(BF16)
        dx[0] = (dot_bt(d_high[...], full_high[...]) + dot_bt(logit_low, r_ref[...])).astype(BF16)
        lo[0] = dot_bt(weighted_now, full_low[...]).astype(BF16)

    def rows(n):
        return pl.BlockSpec((tokens, n), lambda i, at_ref: (i, 0))

    def owner(n, lane):
        return pl.BlockSpec(
            (1, tokens, n), lambda i, at_ref: (at_ref[1] ^ (i + first), 0, lane)
        )

    outs = [struct((count * tokens, n), BF16) for n in (hidden, 2 * hidden, LANES)]
    outs += [struct((grads.shape[0], tokens, width), BF16)] * 2
    ins = (grads, grads, spread, *tokens_in, *high, *low, *router, *before)
    return pl.pallas_call(
        kernel,
        out_shape=outs,
        grid_spec=pltpu.PrefetchScalarGridSpec(
            num_scalar_prefetch=1,
            grid=(count,),
            in_specs=[owner(width, 0), owner(LANES, width // LANES), whole(spread.shape)]
            + [ANY] * (count + 6 + len(before)),
            out_specs=[rows(hidden), rows(2 * hidden), rows(LANES)] + [owner(width, 0)] * 2,
            scratch_shapes=[
                full_weight(high),
                full_weight(low),
                full_weight(router, LANES),
                pltpu.VMEM((2, tokens, width), BF16),
                weight_sems(high, low, router),
                pltpu.SemaphoreType.DMA((2,)),
            ],
        ),
        input_output_aliases={len(ins) - 1: 3, len(ins): 4} if before else {},
        compiler_params=params(),
        cost_estimate=cost(12 * count * tokens * width * hidden, nbytes([*high, *low, *outs])),
        name="run_experts",
    )(at, *ins)


def weight_grads(at, half_at, lefts, rights, cols, add=None):
    flat = [r for group in rights for stack in group for r in stack]
    lefts = [[a] * a.shape[0] if not isinstance(a, list) else a for a in lefts]
    left_flat = [a for group in lefts for a in group]
    stacks = [stack for group in rights for stack in group]
    tokens = sum(r.shape[0] for r in stacks[0])
    by_part = [group[0].shape[0] == tokens and len(group) > 1 for group in lefts]
    width = lefts[0][0].shape[1] * (cols if by_part[0] else 1)
    half = width // cols // 2
    n = sum(stack[0].shape[1] for stack in stacks)
    apart = add is None
    outs = [struct((half, n), BF16)] * cols if apart else struct((cols, half, n), BF16)
    joins = [stack for stack in stacks if len(stack) > 1]
    extra = [] if apart else list(add)

    def kernel(at_ref, *refs):
        left_refs, refs = refs[: len(left_flat)], refs[len(left_flat) :]
        right_refs, refs = refs[: len(flat)], refs[len(flat) :]
        added, refs = refs[: len(extra)], refs[len(extra) :]
        out_refs, joined = refs[: cols if apart else 1], refs[cols if apart else 1 :]
        step = pl.program_id(0)
        stacked = []
        for stack in stacks:
            stack_refs, right_refs = right_refs[: len(stack)], right_refs[len(stack) :]
            if len(stack) == 1:
                stacked.append(stack_refs[0])
            else:
                full, joined = joined[0], joined[1:]
                stacked.append(full)

                @pl.when(step == 0)
                def _(full=full, stack_refs=stack_refs):
                    row = 0
                    for ref in stack_refs:
                        full[row : row + ref.shape[0]] = ref[...]
                        row += ref.shape[0]

        def write(k):
            column, group_lefts, rest = 0, left_refs, stacked
            for group, is_part, group_rights in zip(lefts, by_part, rights):
                group_refs, group_lefts = group_lefts[: len(group)], group_lefts[len(group) :]
                now, rest = rest[: len(group_rights)], rest[len(group_rights) :]
                if is_part:
                    left = group_refs[k][...]
                else:
                    blocks = [ref[...] if len(ref.shape) == 2 else ref[0] for ref in group_refs]
                    left = jnp.concatenate(blocks, axis=0)
                left = left.T
                for right in now:
                    cut = slice(column, column + right.shape[1])
                    value = dot(left, right[...])
                    if apart:
                        out_refs[k][:, cut] = value.astype(BF16)
                    else:
                        out_refs[0][0, :, cut] = (value + added[k][:, cut].astype(F32)).astype(BF16)
                    column = cut.stop

        for k in range(cols):
            pl.when(step == k)(functools.partial(write, k))

    def left_spec(a, i, is_part):
        if a.ndim == 3:
            return pl.BlockSpec(
                (1, a.shape[1], half), lambda k, at_ref: (at_ref[1] ^ i, 0, 2 * k + half_at)
            )
        shape = (a.shape[0], half)
        if is_part:
            return pl.BlockSpec(shape, lambda k, at_ref: (0, half_at))
        return pl.BlockSpec(shape, lambda k, at_ref: (0, 2 * k + half_at))

    ins = (*left_flat, *flat, *extra)
    return pl.pallas_call(
        kernel,
        out_shape=outs,
        grid_spec=pltpu.PrefetchScalarGridSpec(
            num_scalar_prefetch=1,
            grid=(cols,),
            in_specs=[
                left_spec(a, i, p) for group, p in zip(lefts, by_part) for i, a in enumerate(group)
            ]
            + [whole(a.shape) for a in flat + extra],
            out_specs=[whole((half, n))] * cols
            if apart
            else pl.BlockSpec((1, half, n), lambda k, at_ref: (at_ref[0] ^ k, 0, 0)),
            scratch_shapes=[pltpu.VMEM((tokens, stack[0].shape[1]), BF16) for stack in joins],
        ),
        compiler_params=params(),
        cost_estimate=cost(2 * tokens * cols * half * n, nbytes(ins)),
        name="weight_grads",
    )(at, *ins)


def by_owner(weights, outer):
    unit, hidden = weights[0].shape[0], weights[0].shape[1] // outer
    if hidden % LANES:
        return jnp.concatenate(
            [w.reshape(unit, outer, hidden).transpose(1, 0, 2) for w in weights], axis=2
        )

    def kernel(*refs):
        for i, ref in enumerate(refs[:-1]):
            refs[-1][0, :, i * hidden : (i + 1) * hidden] = ref[...]

    out = struct((outer, unit, hidden * len(weights)), BF16)
    return pl.pallas_call(
        kernel,
        out_shape=out,
        grid=(outer,),
        in_specs=[pl.BlockSpec((unit, hidden), lambda i: (0, i)) for _ in weights],
        out_specs=pl.BlockSpec((1,) + out.shape[1:], lambda i: (i, 0, 0)),
        compiler_params=params(),
        cost_estimate=cost(1, 1),
        name="by_owner",
    )(*weights)


def by_columns(grads, hidden):
    outer, unit, n = grads.shape
    starts = (0, hidden, 2 * hidden + LANES)
    if hidden % LANES:
        return [
            grads[:, :, start : start + hidden]
            .transpose(1, 0, 2)
            .reshape(unit, outer * hidden)
            .astype(F32)
            for start in starts
        ] + [jnp.sum(grads[:, :, 2 * hidden : 2 * hidden + LANES].astype(F32), axis=0)]

    def kernel(ref, *outs):
        for start, out in zip(starts, outs):
            out[...] = ref[0, :, start : start + hidden].astype(F32)
        rest = ref[0, :, 2 * hidden : 2 * hidden + LANES].astype(F32)
        before = jnp.where(pl.program_id(0) == 0, 0.0, outs[-1][...])
        outs[-1][...] = before + rest

    outs = [struct((unit, outer * hidden), F32) for _ in starts] + [struct((unit, LANES), F32)]
    return pl.pallas_call(
        kernel,
        out_shape=outs,
        grid=(outer,),
        in_specs=[pl.BlockSpec((1, unit, n), lambda i: (i, 0, 0))],
        out_specs=[pl.BlockSpec((unit, hidden), lambda i: (0, i)) for _ in starts]
        + [whole((unit, LANES))],
        compiler_params=params(),
        cost_estimate=cost(0, nbytes([grads, *outs])),
        name="by_columns",
    )(grads)


def norm_back(values, pieces, scale, gain, gain_grad, outs, width):
    part = pieces[0].shape[1]
    cuts = [slice(k * part, (k + 1) * part) for k in range(len(pieces))]
    inner = 0.0
    for value, piece, cut in zip(values, pieces, cuts):
        gain_grad[:, cut] = jnp.sum(value * (piece * scale), axis=0, keepdims=True)
        inner = inner + jnp.sum(value * gain[:, cut] * piece, axis=1, keepdims=True)
    inner = inner * (scale * scale * scale / width)
    for value, piece, cut, out in zip(values, pieces, cuts, outs):
        out[...] = (value * gain[:, cut] * scale - piece * inner).astype(out.dtype)


def second_norm_back(received, pieces, gain):
    parts = len(pieces)
    blocks, tokens, width = received.shape
    part = width // parts
    outs = [struct((tokens, part), F32 if k == 0 else BF16) for k in range(parts)]
    outs.append(struct((1, width), F32))

    def kernel(*refs):
        got, *refs = refs
        ins, (gain_ref, *outs, gain_grad) = refs[:parts], refs[parts:]
        values = []
        for k in range(parts):
            cut = slice(k * part, (k + 1) * part)
            values.append(sum(got[i, :, cut].astype(F32) for i in range(blocks)))
        pieces = [ref[...].astype(F32) for ref in ins]
        scale = rms_scale(pieces, width)
        norm_back(values, pieces, scale, gain_ref, gain_grad, outs, width)

    ins = (received, *pieces, gain)
    return pl.pallas_call(
        kernel,
        out_shape=outs,
        in_specs=[whole(a.shape) for a in ins],
        out_specs=[whole(o.shape) for o in outs],
        grid=(1,),
        compiler_params=params(),
        cost_estimate=cost(tokens * width * 20, nbytes(ins)),
        name="second_norm_back",
    )(*ins)


def project_back(
    at, grad_q, grad_kv, pre, pieces, gain, pair, query_gain, key_gain, cosine, sine, heads, kv_heads
):
    parts = len(pieces)
    tokens, part = pieces[0].shape
    width = parts * part
    n = pair[0].shape[2]
    size = query_gain.shape[1]
    blocks = len(grad_kv)
    outs = [struct((tokens, part), F32 if k == 0 else BF16) for k in range(parts)]
    outs += [struct((1, width), F32), struct((tokens, n), BF16), struct((2, size), F32)]

    def kernel(at_ref, gq, pre_ref, *refs):
        gkv, refs = refs[:blocks], refs[blocks:]
        ins, refs = refs[:parts], refs[parts:]
        gain_ref, own, other, qg, kg, cos_ref, sin_ref, *refs = refs
        outs, (gain_grad, d_wide, head_gain, full, sems) = refs[:parts], refs[parts:]
        copies = weight_copies(at_ref[0], [(own, other)], [full], sems)
        for copy in copies:
            copy.start()
        cosine, sine = cos_ref[...], sin_ref[...]
        totals = [jnp.zeros((1, size), F32), jnp.zeros((1, size), F32)]
        for i in range(n // size):
            cut = slice(i * size, (i + 1) * size)
            if i < heads:
                grad = gq[:, cut]
            else:
                kv_cut = slice((i - heads) * size, (i - heads + 1) * size)
                grad = sum(ref[:, kv_cut].astype(F32) for ref in gkv)
            if i < heads + kv_heads:
                which = 0 if i < heads else 1
                gain_row = (qg, kg)[which][...]
                grad = grad * cosine + pltpu.roll(grad * sine, size // 2, 1)
                head = pre_ref[:, cut]
                scale = lax.rsqrt(jnp.mean(head * head, axis=1, keepdims=True) + EPS)
                unit = head * scale
                totals[which] = totals[which] + jnp.sum(grad * unit, axis=0, keepdims=True)
                grad = grad * gain_row
                grad = scale * (grad - unit * jnp.mean(grad * unit, axis=1, keepdims=True))
            d_wide[:, cut] = grad.astype(BF16)
        head_gain[0:1] = totals[0]
        head_gain[1:2] = totals[1]
        for copy in copies:
            copy.wait()
        values = [
            dot_bt(d_wide[...], full[k * part : (k + 1) * part]) for k in range(parts)
        ]
        pieces = [ref[...].astype(F32) for ref in ins]
        scale = rms_scale(pieces, width)
        norm_back(values, pieces, scale, gain_ref, gain_grad, outs, width)

    ins = (grad_q, pre, *grad_kv, *pieces, gain, *pair, query_gain, key_gain, cosine, sine)
    return pl.pallas_call(
        kernel,
        out_shape=outs,
        in_specs=[SMEM]
        + [whole(a.shape) for a in (grad_q, pre, *grad_kv, *pieces, gain)]
        + [ANY, ANY]
        + [whole(a.shape) for a in (query_gain, key_gain, cosine, sine)],
        out_specs=[whole(o.shape) for o in outs],
        scratch_shapes=[full_weight(pair), weight_sems(pair)],
        grid=(1,),
        compiler_params=params(),
        cost_estimate=cost(2 * tokens * width * n, nbytes(ins)),
        name="project_back",
    )(at, *ins)


def per_device(
    layer_in,
    out_grad,
    lengths,
    token_order,
    choices,
    norm_gain,
    w_query,
    w_key,
    w_value,
    query_gain,
    key_gain,
    w_out,
    ffn_gain,
    w_router,
    w_gate,
    w_up,
    w_down,
):
    micro, tok, part = layer_in.shape
    outer, cols = lax.axis_size("outer"), lax.axis_size("col")
    rows = 2 * outer
    tokens = micro * tok
    width = part * cols
    outer_at, core_at, col_at = (lax.axis_index(name) for name in ("outer", "core", "col"))
    row_at = outer_at * 2 + core_at
    at = jnp.stack([col_at, outer_at]).astype(jnp.int32)
    low = outer // cols
    unit = width // rows
    half = part // 2
    size = query_gain.shape[0]
    heads = w_query.shape[1] // size
    kv_heads = w_key.shape[1] // size
    experts = w_router.shape[1]
    hidden = w_gate.shape[1] // outer
    repeats = hidden // experts

    def core_swap(a):
        return lax.ppermute(a, "core", [(0, 1), (1, 0)])

    def col_swap(a, mask):
        return lax.ppermute(a, "col", [(i, i ^ mask) for i in range(cols)])

    def exchange(a):
        return lax.all_to_all(a, "outer", 0, 0, tiled=True)

    def after(a, b):
        return lax.optimization_barrier((a, b))[0]

    def spread_out(a):
        return exchange(jnp.broadcast_to(a[None], (outer,) + a.shape))

    def to_halves(a):
        blocks = a.reshape(a.shape[:-1] + (low, 2, unit))
        first = blocks[..., 0, :].reshape(a.shape[:-1] + (half,))
        second = blocks[..., 1, :].reshape(a.shape[:-1] + (half,))
        even = core_at == 0
        return jnp.concatenate(
            [jnp.where(even, first, second), jnp.where(even, second, first)], axis=-1
        )

    def from_halves(a):
        even = core_at == 0
        first = jnp.where(even, a[..., :half], a[..., half:]).reshape(a.shape[:-1] + (low, unit))
        second = jnp.where(even, a[..., half:], a[..., :half]).reshape(a.shape[:-1] + (low, unit))
        return jnp.stack([first, second], axis=-2).reshape(a.shape)

    def relative(a):
        return jnp.stack(
            [lax.dynamic_index_in_dim(a, col_at ^ k, 0, keepdims=False) for k in range(cols)]
        )

    def order_rows(a):
        blocks = relative(a.reshape((cols, low, 2, unit) + a.shape[1:]))
        blocks = jnp.where(core_at == 0, blocks, blocks[:, :, ::-1])
        return jnp.moveaxis(blocks, 2, 1).reshape(a.shape)

    def unorder_rows(a):
        blocks = jnp.moveaxis(a.reshape((cols, 2, low, unit) + a.shape[1:]), 1, 2)
        blocks = jnp.where(core_at == 0, blocks, blocks[:, :, ::-1])
        return relative(blocks).reshape(a.shape)

    def col_gather(a):
        return [a] + [col_swap(a, k) for k in range(1, cols)]

    def col_total(pieces):
        total = pieces[0]
        for k in range(1, cols):
            total = total + col_swap(pieces[k], k).astype(F32)
        return total

    def both_cores(a):
        own = a.reshape(cols, half, a.shape[-1])
        return own, core_swap(own)

    def swap(a, mask):
        return lax.ppermute(a, "outer", [(i, i ^ mask) for i in range(outer)])

    def gather(a):
        return [a] + [swap(a, j) for j in range(1, outer)]

    def scatter(blocks):
        return [blocks[0]] + [swap(blocks[j], j) for j in range(1, outer)]

    own_in = to_halves(layer_in).reshape(tokens, part)
    own_grad = to_halves(out_grad).reshape(tokens, part)
    w_in = spread_out(jnp.concatenate([w_query, w_key, w_value], axis=1))
    full_in = col_gather(own_in)
    chosen = jnp.any(
        choices.reshape(tokens, -1)[..., None] == jnp.arange(LANES, dtype=jnp.int32), axis=1
    ).astype(BF16)
    own_grads = col_gather(own_grad)
    back_now = jnp.concatenate([w_out, jnp.pad(w_router, ((0, 0), (0, LANES - experts)))], axis=1)
    back_now = jnp.broadcast_to(back_now[None], (outer,) + back_now.shape)
    low_now, high_now = by_owner([w_down], outer), by_owner([w_gate, w_up], outer)
    grads = jnp.concatenate(own_grads + [chosen], axis=1)
    grads = jnp.broadcast_to(grads[None], (outer,) + grads.shape)
    gain_one = order_rows(norm_gain)[None, :]
    gain_two = order_rows(ffn_gain)[None, :]
    q_gain, k_gain = query_gain[None, :], key_gain[None, :]
    spread = (
        jnp.arange(hidden)[None, :] % experts == jnp.arange(LANES)[:, None]
    ).astype(BF16)

    biases, cosines, sines = [], [], []
    for b in range(micro):
        dealt = token_order[b]
        seq_of, places = token_places(lengths[b], dealt)
        own_order = lax.dynamic_slice_in_dim(dealt, row_at * tok, tok)
        own_seq = lax.dynamic_slice_in_dim(seq_of, row_at * tok, tok)
        own_places = lax.dynamic_slice_in_dim(places, row_at * tok, tok)

        def by_core(a):
            blocks = a.reshape(outer, 2, tok)
            blocks = jnp.where(core_at == 0, blocks, blocks[:, ::-1])
            blocks = jnp.stack(
                [
                    lax.dynamic_index_in_dim(blocks, outer_at ^ j, 0, keepdims=False)
                    for j in range(outer)
                ]
            )
            return blocks.transpose(1, 0, 2).reshape(-1)

        allowed = (own_seq[None, :] == by_core(seq_of)[:, None]) & (
            by_core(dealt)[:, None] <= own_order[None, :]
        )
        biases.append(jnp.where(allowed, 0.0, NEGATIVE))
        cosine, sine = angles_of(own_places, size)
        cosines.append(cosine)
        sines.append(sine)
    bias = jnp.stack(biases)
    cosine, sine = jnp.concatenate(cosines), jnp.concatenate(sines)

    w_in, *_ = lax.optimization_barrier(
        (w_in, full_in, grads, back_now, low_now, high_now, bias, cosine, sine, gain_one, gain_two, spread)
    )
    w_back = exchange(after(back_now, w_in))
    w_in = both_cores(w_in)
    normed_one, pre, ready = project(
        at, full_in, gain_one, w_in, q_gain, k_gain, cosine, sine, heads, kv_heads
    )
    kv_own = jnp.stack(gather(ready[:, heads * size :]))
    kv_other = core_swap(kv_own)
    kv_other, w_back = lax.optimization_barrier((kv_other, w_back))
    w_low = exchange(after(low_now, w_back))
    w_back = both_cores(w_back)
    attended, lse = attend(ready, kv_own, kv_other, bias, heads, kv_heads, size)
    attended, w_low = lax.optimization_barrier((attended, w_low))
    w_high = exchange(after(high_now, w_low))
    attn_parts = expand(at, attended, w_back, part)
    residual = own_in.astype(F32) + col_total(attn_parts)
    residual, w_high = lax.optimization_barrier((residual, w_high))
    grads = exchange(after(grads, w_high))
    w_low = both_cores(w_low)
    full_res = col_gather(residual.astype(BF16))

    full_res, grads = lax.optimization_barrier((full_res, grads))
    normed_two = second_norm(full_res, gain_two)
    expert_in = gather(normed_two)
    w_high = both_cores(w_high)
    weights = (spread, w_high, w_low, w_back, w_out.shape[1])
    weighted_0, d_high_0, logit_0, *before = run_experts(
        at, 0, expert_in[:1], grads, *weights, ()
    )
    weighted, d_high, logit_low, dx, lo = run_experts(
        at, 1, expert_in[1:], grads, *weights, before
    )
    weighted, d_high, logit_low = [weighted_0, weighted], [d_high_0, d_high], [logit_0, logit_low]
    dx = exchange(dx)

    def both_halves(lefts, rights):
        other = weight_grads(at, 1, lefts, rights, cols)
        own = weight_grads(at, 0, lefts, rights, cols, [core_swap(a) for a in other])
        return own.reshape(outer, unit, own.shape[-1])

    expert_grads = both_halves([expert_in, grads], [[d_high, logit_low], [weighted]])
    dx, expert_grads = lax.optimization_barrier((dx, expert_grads))
    expert_grads = exchange(expert_grads)
    *spread_two, gain_grad_two = second_norm_back(dx, full_res, gain_two)
    grad_residual = own_grad.astype(F32) + col_total(spread_two)
    grad_feats = col_gather(grad_residual.astype(BF16))

    grad_feats, expert_grads = lax.optimization_barrier((grad_feats, expert_grads))
    lo = exchange(after(lo, expert_grads))
    back_attended = contract(at, grad_feats, w_back, heads * size)
    grad_q, *kv_grads = attend_back(
        ready, kv_own, kv_other, bias, lse, back_attended, heads, kv_heads, size
    )
    kv_mine = jnp.concatenate([kv_grads[0], kv_grads[2]], axis=2)
    kv_theirs = jnp.concatenate([kv_grads[1], kv_grads[3]], axis=2).astype(BF16)
    kv_mine = (kv_mine + core_swap(kv_theirs).astype(F32)).astype(BF16)
    grad_kv = scatter([kv_mine[j] for j in range(outer)])
    out_grads = both_halves([grad_feats], [[[attended]]])
    grad_kv, out_grads, lo = lax.optimization_barrier((grad_kv, out_grads, lo))
    out_grads = exchange(out_grads)
    *spread_one, gain_grad_one, d_wide, head_gains = project_back(
        at, grad_q, grad_kv, pre, full_in, gain_one, w_in, q_gain, k_gain, cosine, sine, heads, kv_heads
    )
    sums = jnp.concatenate(
        [unorder_rows(gain_grad_one[0]), unorder_rows(gain_grad_two[0]), head_gains.reshape(-1)]
    ).reshape(-1, LANES)
    sums = sums + sum(col_swap(sums, k) for k in range(1, cols))
    sums = sums + core_swap(sums)
    wide_grads = both_halves([[normed_one]], [[[d_wide]]])
    out_grads, wide_grads, sums = lax.optimization_barrier((out_grads, wide_grads, sums))
    wide_grads = exchange(wide_grads)
    sums = sum(gather(sums)).reshape(-1)
    expert_grads, lo = lax.optimization_barrier((expert_grads, lo, out_grads))[:2]
    layer_sum = jnp.sum(lo.astype(F32), axis=0)
    layer_out = residual + col_total(
        [
            layer_sum[:, k * part : (k + 1) * part].astype(F32 if k == 0 else BF16)
            for k in range(cols)
        ]
    )
    input_grad = grad_residual + col_total(spread_one)
    grad_gate_w, grad_up_w, grad_down_w, router_part = by_columns(expert_grads, hidden)
    grad_router = router_part
    for k in range(1, cols):
        grad_router = grad_router + col_swap(router_part, k)
    grad_out_w = jnp.sum(out_grads.astype(F32), axis=0)
    wide_grads, input_grad, layer_out, grad_out_w, sums, grad_router, grad_gate_w = (
        lax.optimization_barrier(
            (wide_grads, input_grad, layer_out, grad_out_w, sums, grad_router, grad_gate_w)
        )
    )
    grad_wide = jnp.sum(wide_grads.astype(F32), axis=0)
    query_cols, key_cols = w_query.shape[1], w_key.shape[1]
    return (
        from_halves(layer_out.astype(BF16)).reshape(micro, tok, part),
        from_halves(input_grad.astype(BF16)).reshape(micro, tok, part),
        sums[:width],
        grad_wide[:, :query_cols],
        grad_wide[:, query_cols : query_cols + key_cols],
        grad_wide[:, query_cols + key_cols :],
        sums[2 * width : 2 * width + size],
        sums[2 * width + size :],
        grad_out_w,
        sums[width : 2 * width],
        grad_router[:, :experts],
        grad_gate_w,
        grad_up_w,
        grad_down_w,
    )


def solution(mesh):
    rows, cols = mesh.devices.shape
    split = Mesh(mesh.devices.reshape(rows // 2, 2, cols), ("outer", "core", "col"))
    tokens_placed = P(None, ROW, "col")
    weight_placed = P(ROW, "col")
    return jax.shard_map(
        per_device,
        mesh=split,
        in_specs=(
            tokens_placed,
            tokens_placed,
            P(),
            P(),
            P(None, ROW, None),
            P(),
            weight_placed,
            weight_placed,
            weight_placed,
            P(),
            P(),
            weight_placed,
            P(),
            P(ROW, None),
            weight_placed,
            weight_placed,
            weight_placed,
        ),
        out_specs=(
            tokens_placed,
            tokens_placed,
            P(),
            weight_placed,
            weight_placed,
            weight_placed,
            P(),
            P(),
            weight_placed,
            P(),
            P(ROW, None),
            weight_placed,
            weight_placed,
            weight_placed,
        ),
        check_vma=False,
    )
```

```python
import functools
import math

import jax
import jax.numpy as jnp
from jax import lax
from jax.experimental import pallas as pl
from jax.experimental.pallas import tpu as pltpu
from jax.sharding import Mesh
from jax.sharding import PartitionSpec as P

EPS = 1e-06
THETA = 1000000.0
NEGATIVE = -1e30
F32 = jnp.float32
BF16 = jnp.bfloat16
VMEM_BYTES = 56 * 1024 * 1024
LANES = 128
ROW = ("outer", "core")


def dot(a, b):
    return jnp.dot(a, b, preferred_element_type=F32)


def dot_bt(a, b):
    return lax.dot_general(a, b, (((1,), (1,)), ((), ())), preferred_element_type=F32)


def dot_at(a, b):
    return lax.dot_general(a, b, (((0,), (0,)), ((), ())), preferred_element_type=F32)


def two_parts(a):
    high = a.astype(BF16)
    return high, (a - high.astype(F32)).astype(BF16)


ANY = pl.BlockSpec(memory_space=pl.ANY)
SMEM = pl.BlockSpec(memory_space=pltpu.SMEM)


def whole(shape):
    return pl.BlockSpec(shape, lambda *_: (0,) * len(shape))


def params(steps=1):
    return pltpu.CompilerParams(
        dimension_semantics=("arbitrary",) * steps, vmem_limit_bytes=VMEM_BYTES
    )


def cost(flops, moved):
    return pl.CostEstimate(flops=int(flops) // 64, bytes_accessed=int(moved) // 64, transcendentals=0)


def nbytes(arrays):
    return sum(math.prod(a.shape) * a.dtype.itemsize for a in arrays)


def struct(shape, dtype):
    return jax.ShapeDtypeStruct(shape, dtype)


def block_count(pair):
    return len(pair[0]) if isinstance(pair[0], list) else pair[0].shape[0]


def weight_copies(at_ref, pairs, fulls, sems, parts, firsts=None):
    copies, base = [], 0
    for i, (pair, full) in enumerate(zip(pairs, fulls)):
        first = firsts[i] if firsts else 0
        blocks = block_count(pair)
        low = blocks // parts
        unit = full.shape[0] // blocks // 2
        for h, sources in enumerate(pair):
            listed = isinstance(sources, list)
            for j in range(blocks):
                to = at_ref[0 if listed else 2] ^ j
                source = sources[j] if listed else sources.at[j]
                row = (2 * (to // low) + h) * (low * unit) + lax.rem(to, low) * unit
                copies.append(
                    pltpu.make_async_copy(
                        source.at[:, pl.ds(first, full.shape[1])],
                        full.at[pl.ds(pl.multiple_of(row, unit), unit)],
                        sems.at[base + h * blocks + to],
                    )
                )
        base += 2 * blocks
    return copies


def weight_wait(pairs, fulls, sems, parts, part=None):
    base = 0
    for pair, full in zip(pairs, fulls):
        blocks = block_count(pair)
        low = blocks // parts
        unit = full.shape[0] // blocks // 2
        for h in range(2):
            for to in range(blocks):
                if part is None or to // low == part:
                    row = (2 * (to // low) + h) * (low * unit) + to % low * unit
                    source = pair[h][0] if isinstance(pair[h], list) else pair[h].at[0]
                    pltpu.make_async_copy(
                        source.at[:, pl.ds(0, full.shape[1])],
                        full.at[pl.ds(row, unit)],
                        sems.at[base + h * blocks + to],
                    ).wait()
        base += 2 * blocks


def full_weight(pair, n=None):
    unit, width = (pair[0][0] if isinstance(pair[0], list) else pair[0]).shape[-2:]
    return pltpu.VMEM((2 * block_count(pair) * unit, n or width), BF16)


def weight_sems(*pairs):
    return pltpu.SemaphoreType.DMA((sum(2 * block_count(pair) for pair in pairs),))


def flat_pair(pair):
    return [a for half in pair for a in (half if isinstance(half, list) else [half])]


def taken(refs, pair):
    halves = []
    for half in pair:
        if isinstance(half, list):
            halves.append(list(refs[: len(half)]))
            refs = refs[len(half) :]
        else:
            halves.append(refs[0])
            refs = refs[1:]
    return tuple(halves), refs


def rms_scale(pieces, width):
    total = sum(jnp.sum(piece * piece, axis=1, keepdims=True) for piece in pieces)
    return lax.rsqrt(total / width + EPS)


def prepare(at, lengths, order, choices, frequency, gains, low, hidden, experts):
    micro, rows, tok = order.shape
    tokens, top = choices.shape
    _, cols, part = gains.shape
    unit = part // 2 // low
    outer, seqs, size = rows // 2, lengths.shape[1], frequency.shape[1]

    def kernel(at_ref, len_ref, order_ref, choice_ref, freq_ref, gain_ref, bias, angles, chosen, spread, *ordered):
        outer_at, core, col = at_ref[1], at_ref[3], at_ref[4]
        for b in range(micro):

            def seq_of(value):
                seq, start, end = jnp.zeros_like(value), jnp.zeros_like(value), 0
                for i in range(seqs):
                    end = end + len_ref[b, i]
                    passed = value >= end
                    seq = seq + jnp.where(passed, 1, 0)
                    start = start + jnp.where(passed, len_ref[b, i], 0)
                return seq, start

            def row(at):
                return order_ref[b, pl.ds(at, 1), :]

            own = row(2 * outer_at + core)
            own_seq, own_start = seq_of(own)
            keys = jnp.concatenate(
                [row(2 * (outer_at ^ j) + (core ^ h)) for h in range(2) for j in range(outer)], axis=0
            )
            key_seq, _ = seq_of(keys)
            lines = [keys, key_seq, own - own_start]
            lines.append(jnp.zeros((tok - 2 * rows - 1, tok), jnp.int32))
            turned = jnp.concatenate(lines, axis=0).astype(F32).T
            own, own_seq = own.astype(F32), own_seq.astype(F32)
            for i in range(rows):
                allowed = (turned[:, rows + i : rows + i + 1] == own_seq) & (
                    turned[:, i : i + 1] <= own
                )
                bias[b, i * tok : (i + 1) * tok] = jnp.where(allowed, 0.0, NEGATIVE)
            angles[b * tok : (b + 1) * tok] = turned[:, 2 * rows : 2 * rows + 1] * freq_ref[...]
        lanes = lax.broadcasted_iota(jnp.int32, (tokens, LANES), 1)
        hits = jnp.zeros((tokens, LANES), F32)
        for i in range(top):
            hits = hits + jnp.where(choice_ref[:, i : i + 1] == lanes, 1.0, 0.0)
        chosen[...] = hits.astype(BF16)
        units = lax.broadcasted_iota(jnp.int32, (LANES, hidden), 1)
        owners = lax.broadcasted_iota(jnp.int32, (LANES, hidden), 0)
        spread[...] = jnp.where(lax.rem(units, experts) == owners, 1.0, 0.0).astype(BF16)
        for i, out in enumerate(ordered):
            for k in range(cols):
                line = gain_ref[i, pl.ds(col ^ k, 1), :]
                for n in range(low):
                    first = line[:, 2 * n * unit : (2 * n + 1) * unit]
                    second = line[:, (2 * n + 1) * unit : (2 * n + 2) * unit]
                    start = k * part + n * unit
                    out[:, start : start + unit] = jnp.where(core == 0, first, second)
                    start = start + part // 2
                    out[:, start : start + unit] = jnp.where(core == 0, second, first)

    outs = (
        struct((micro, rows * tok, tok), F32),
        struct((tokens, size), F32),
        struct((tokens, LANES), BF16),
        struct((LANES, hidden), BF16),
        struct((1, cols * part), F32),
        struct((1, cols * part), F32),
    )
    ins = (order, choices, frequency, gains)
    return pl.pallas_call(
        kernel,
        out_shape=outs,
        grid=(1,),
        in_specs=[SMEM, SMEM] + [whole(a.shape) for a in ins],
        out_specs=[whole(o.shape) for o in outs],
        compiler_params=params(),
        cost_estimate=cost(1, 1),
        name="prepare",
    )(at, lengths, *ins)


def project(at, pieces, part, gain, pair, query_gain, key_gain, cosine, sine, heads, kv_heads):
    parts = len(pieces)
    tokens = cosine.shape[0]
    width = parts * part
    n = flat_pair(pair)[0].shape[-1]
    size = query_gain.shape[1]

    def kernel(at_ref, *refs):
        ins, refs = refs[:parts], refs[parts:]
        weights, refs = taken(refs, pair)
        gain_ref, qg, kg, cos_ref, sin_ref, normed, pre, ready, kv, full, sems = refs
        for copy in weight_copies(at_ref, [weights], [full], sems, parts):
            copy.start()
        values = [ref[...].astype(F32) for ref in ins]
        scale = rms_scale(values, width)
        for k, value in enumerate(values):
            cut = slice(k * part, (k + 1) * part)
            normed[:, cut] = (value * scale * gain_ref[:, cut]).astype(BF16)
        weight_wait([weights], [full], sems, parts)
        pre[...] = dot(normed[...], full[...])
        cosine, sine = cos_ref[...], sin_ref[...]
        for i in range(n // size):
            cut = slice(i * size, (i + 1) * size)
            head = pre[:, cut]
            if i < heads + kv_heads:
                head_gain = qg[...] if i < heads else kg[...]
                head = (
                    head
                    * lax.rsqrt(jnp.mean(head * head, axis=1, keepdims=True) + EPS)
                    * head_gain
                )
                head = head * cosine + pltpu.roll(head, size // 2, 1) * sine
            if i < heads:
                ready[:, cut] = head.astype(BF16)
            else:
                kv[:, (i - heads) * size : (i - heads + 1) * size] = head.astype(BF16)

    outs = (
        struct((tokens, width), BF16),
        struct((tokens, n), F32),
        struct((tokens, heads * size), BF16),
        struct((tokens, n - heads * size), BF16),
    )
    ins = (*pieces, *flat_pair(pair), gain, query_gain, key_gain, cosine, sine)
    return pl.pallas_call(
        kernel,
        out_shape=outs,
        in_specs=[SMEM]
        + [whole((tokens, part)) for _ in pieces]
        + [ANY] * len(flat_pair(pair))
        + [whole(a.shape) for a in (gain, query_gain, key_gain, cosine, sine)],
        out_specs=[whole(o.shape) for o in outs],
        scratch_shapes=[full_weight(pair), weight_sems(pair)],
        grid=(1,),
        compiler_params=params(),
        cost_estimate=cost(9e11, 1),
        name="project",
    )(at, *ins)


def attend(ready, own, other, bias, heads, kv_heads, size):
    micro, keys, tok = bias.shape
    group = heads // kv_heads
    outer = own.shape[0]
    scale = 1.0 / math.sqrt(size)

    def kernel(q_ref, k0, k1, v0, v1, bias_ref, out_ref, lse_ref):
        key = jnp.concatenate([r[...].reshape(outer * tok, size) for r in (k0, k1)], axis=0)
        value = jnp.concatenate([r[...].reshape(outer * tok, size) for r in (v0, v1)], axis=0)
        scores = dot_bt(key, q_ref[...]) * scale + bias_ref[0]
        peak = jnp.max(scores, axis=0, keepdims=True)
        powers = jnp.exp(scores - peak)
        total = jnp.sum(powers, axis=0, keepdims=True)
        probs = (powers * (1.0 / total)).astype(BF16)
        out_ref[...] = dot_at(probs, value).astype(BF16)
        lse_ref[0, 0] = peak + jnp.log(total)

    def kv_spec(first):
        return pl.BlockSpec((outer, tok, size), lambda m, h: (0, m, first + h // group))

    head_spec = pl.BlockSpec((tok, size), lambda m, h: (m, h))
    outs = (struct((micro * tok, heads * size), BF16), struct((micro, heads, 1, tok), F32))
    return pl.pallas_call(
        kernel,
        out_shape=outs,
        grid=(micro, heads),
        in_specs=[
            head_spec,
            kv_spec(0),
            kv_spec(0),
            kv_spec(kv_heads),
            kv_spec(kv_heads),
            pl.BlockSpec((1, keys, tok), lambda m, h: (m, 0, 0)),
        ],
        out_specs=[head_spec, pl.BlockSpec((1, 1, 1, tok), lambda m, h: (m, h, 0, 0))],
        compiler_params=params(2),
        cost_estimate=cost(4 * micro * heads * keys * tok * size, nbytes((own, other, bias))),
        name="attend",
    )(ready, own, other, own, other, bias)


def attend_back(ready, own, other, bias, lse, grad, heads, kv_heads, size):
    micro, keys, tok = bias.shape
    group = heads // kv_heads
    outer = own.shape[0]
    scale = 1.0 / math.sqrt(size)
    mid = keys // 2

    def kernel(q_ref, k0, k1, v0, v1, bias_ref, lse_ref, g_ref, gq, mine, theirs, gk, gv):
        head = pl.program_id(1)
        place = head % group
        key = jnp.concatenate([r[...].reshape(outer * tok, size) for r in (k0, k1)], axis=0)
        value = jnp.concatenate([r[...].reshape(outer * tok, size) for r in (v0, v1)], axis=0)
        query, out_grad = q_ref[...], g_ref[...]
        scores = dot_bt(key, query) * scale + bias_ref[0]
        probs = jnp.exp(scores - lse_ref[0, 0])
        back = dot_bt(value, out_grad)
        centre = jnp.sum(probs * back, axis=0, keepdims=True)
        slope = (probs * (back - centre)).astype(BF16)
        gq[...] = dot_at(slope, key) * scale
        key_part = dot(slope, query) * scale
        value_part = dot(probs.astype(BF16), out_grad)

        @pl.when(place == 0)
        def _():
            gk[...] = key_part
            gv[...] = value_part

        @pl.when(place > 0)
        def _():
            gk[...] += key_part
            gv[...] += value_part

        for g in range(kv_heads):

            @pl.when(head == (g + 1) * group - 1)
            def _(g=g):
                for i, ref in enumerate((gk, gv)):
                    at = (i * kv_heads + g) * size
                    cut = slice(at, at + size)
                    mine[:, :, cut] = ref[:mid].reshape(outer, tok, size)
                    theirs[:, :, cut] = ref[mid:].reshape(outer, tok, size).astype(BF16)

    def kv_spec(start):
        return pl.BlockSpec((outer, tok, size), lambda m, h: (0, m, start + h // group))

    head_spec = pl.BlockSpec((tok, size), lambda m, h: (m, h))
    kv_shape = (outer, micro * tok, 2 * kv_heads * size)
    outs = (
        struct((micro * tok, heads * size), F32),
        struct(kv_shape, F32),
        struct(kv_shape, BF16),
    )
    out_spec = pl.BlockSpec((outer, tok, kv_shape[2]), lambda m, h: (0, m, 0))
    return pl.pallas_call(
        kernel,
        out_shape=outs,
        grid=(micro, heads),
        in_specs=[
            head_spec,
            kv_spec(0),
            kv_spec(0),
            kv_spec(kv_heads),
            kv_spec(kv_heads),
            pl.BlockSpec((1, keys, tok), lambda m, h: (m, 0, 0)),
            pl.BlockSpec((1, 1, 1, tok), lambda m, h: (m, h, 0, 0)),
            head_spec,
        ],
        out_specs=[head_spec, out_spec, out_spec],
        scratch_shapes=[pltpu.VMEM((keys, size), F32)] * 2,
        compiler_params=params(2),
        cost_estimate=cost(10 * micro * heads * keys * tok * size, nbytes((own, other, bias))),
        name="attend_back",
    )(ready, own, other, own, other, bias, lse, grad)


def sum_cores(mine, theirs):
    outer, tokens, n = mine.shape

    def kernel(mine, theirs, *outs):
        for j, out in enumerate(outs):
            out[...] = (mine[j] + theirs[j].astype(F32)).astype(BF16)

    outs = [struct((tokens, n), BF16)] * outer
    return pl.pallas_call(
        kernel,
        out_shape=outs,
        grid=(1,),
        in_specs=[whole(mine.shape)] * 2,
        out_specs=[whole(o.shape) for o in outs],
        compiler_params=params(),
        cost_estimate=cost(1, 1),
        name="sum_cores",
    )(mine, theirs)


def expand(at, a, pair, part, parts):
    tokens, n = a.shape
    outs = [struct((tokens, part), F32 if k == 0 else BF16) for k in range(parts)]

    def kernel(at_ref, a_ref, *refs):
        weights, refs = taken(refs, pair)
        outs, (full, sems) = refs[:parts], refs[parts:]
        for copy in weight_copies(at_ref, [weights], [full], sems, parts):
            copy.start()
        for k, out in enumerate(outs):
            weight_wait([weights], [full], sems, parts, k)
            out[...] = dot_bt(a_ref[...], full[k * part : (k + 1) * part]).astype(out.dtype)

    ins = (a, *flat_pair(pair))
    return pl.pallas_call(
        kernel,
        out_shape=outs,
        in_specs=[SMEM, whole(a.shape)] + [ANY] * len(flat_pair(pair)),
        out_specs=[whole(o.shape) for o in outs],
        scratch_shapes=[full_weight(pair, n), weight_sems(pair)],
        grid=(1,),
        compiler_params=params(),
        cost_estimate=cost(2 * tokens * n * part * parts, nbytes(ins)),
        name="expand",
    )(at, *ins)


def contract(at, pieces, pair, n):
    parts = len(pieces)
    tokens, part = pieces[0].shape
    outs = struct((tokens, n), BF16)

    def kernel(at_ref, *refs):
        ins, refs = refs[:parts], refs[parts:]
        weights, (out, full, sems) = taken(refs, pair)
        for copy in weight_copies(at_ref, [weights], [full], sems, parts):
            copy.start()
        total = 0.0
        for k, ref in enumerate(ins):
            weight_wait([weights], [full], sems, parts, k)
            total = total + dot(ref[...], full[k * part : (k + 1) * part])
        out[...] = total.astype(BF16)

    ins = (*pieces, *flat_pair(pair))
    return pl.pallas_call(
        kernel,
        out_shape=outs,
        in_specs=[SMEM] + [whole(a.shape) for a in pieces] + [ANY] * len(flat_pair(pair)),
        out_specs=whole(outs.shape),
        scratch_shapes=[full_weight(pair, n), weight_sems(pair)],
        grid=(1,),
        compiler_params=params(),
        cost_estimate=cost(2 * tokens * n * part * parts, nbytes(ins)),
        name="contract",
    )(at, *ins)


def second_norm(pieces, gain):
    parts = len(pieces)
    tokens, part = pieces[0].shape
    width = parts * part
    out = struct((tokens, width), BF16)

    def kernel(*refs):
        ins, (gain_ref, out_ref) = refs[:parts], refs[parts:]
        values = [ref[...].astype(F32) for ref in ins]
        scale = rms_scale(values, width)
        for k, value in enumerate(values):
            cut = slice(k * part, (k + 1) * part)
            out_ref[:, cut] = (value * scale * gain_ref[:, cut]).astype(BF16)

    return pl.pallas_call(
        kernel,
        out_shape=out,
        in_specs=[whole(a.shape) for a in pieces] + [whole(gain.shape)],
        out_specs=whole(out.shape),
        grid=(1,),
        compiler_params=params(),
        cost_estimate=cost(tokens * width * 4, nbytes((*pieces, out))),
        name="second_norm",
    )(*pieces, gain)


def run_experts(at, tokens_in, grads, spread, pair, router, router_at, parts, by_part):
    count = len(tokens_in)
    tok, width = tokens_in[0].shape
    hidden = flat_pair(pair)[0].shape[-1] // 3
    part = width // parts

    def kernel(at_ref, s_ref, *refs):
        x_refs, refs = refs[:count], refs[count:]
        g_refs, refs = refs[:count], refs[count:]
        weights, refs = taken(refs, pair)
        routers, refs = taken(refs, router)
        weighted, d_high, logit, *refs = refs
        dxs, refs = refs[:count], refs[count:]
        los, (full, r_ref, x_now, g_now, sems, x_sems) = refs[:count], refs[count:]
        pairs, fulls = [weights, routers], [full, r_ref]
        high, low = slice(0, 2 * hidden), slice(2 * hidden, 3 * hidden)
        step = pl.program_id(0)
        arrivals = [
            [
                pltpu.make_async_copy(x_refs[i], x_now.at[i % 2], x_sems.at[0, i % 2]),
                pltpu.make_async_copy(g_refs[i], g_now.at[i % 2], x_sems.at[1, i % 2]),
            ]
            for i in range(count)
        ]

        @pl.when(step == 0)
        def _():
            for copy in arrivals[0]:
                copy.start()
            for copy in weight_copies(at_ref, pairs, fulls, sems, parts, (0, router_at)):
                copy.start()

        for i in range(count):

            @pl.when(step == i)
            def _(i=i):
                for copy in arrivals[i]:
                    copy.wait()
                if i + 1 < count:
                    for copy in arrivals[i + 1]:
                        copy.start()

        slot = lax.rem(step, 2)
        pre, back, logits = 0.0, 0.0, 0.0
        for k in range(parts):

            @pl.when(step == 0)
            def _(k=k):
                weight_wait(pairs, fulls, sems, parts, k)

            cut = slice(k * part, (k + 1) * part)
            x = x_now[slot, :, cut]
            pre = pre + dot(x, full[cut, high])
            back = back + dot(g_now[slot, :, cut], full[cut, low])
            logits = logits + dot(x, r_ref[cut])
        logits = jnp.where(g_now[slot, :, width:] > 0, logits, NEGATIVE)
        peak = jnp.max(logits, axis=1, keepdims=True)
        powers = jnp.exp(logits - peak)
        gate_probs = powers / jnp.sum(powers, axis=1, keepdims=True)
        spread = s_ref[...]
        one, two = two_parts(gate_probs)
        probs_wide = dot(one, spread) + dot(two, spread)
        gate_pre, up_pre = pre[:, :hidden], pre[:, hidden:]
        sigmoid = 0.5 + 0.5 * jnp.tanh(0.5 * gate_pre)
        swish = gate_pre * sigmoid
        active = swish * up_pre
        weighted_now = (probs_wide * active).astype(BF16)
        weighted[...] = weighted_now
        gate_grad = dot_bt((active * back).astype(BF16), spread)
        logit_low = (
            gate_probs * (gate_grad - jnp.sum(gate_probs * gate_grad, axis=1, keepdims=True))
        ).astype(BF16)
        logit[...] = logit_low
        back = probs_wide * back
        d_high[:, :hidden] = (back * up_pre * (sigmoid + swish * (1.0 - sigmoid))).astype(BF16)
        d_high[:, hidden:] = (back * swish).astype(BF16)
        dx = dot_bt(d_high[...], full[:, high]) + dot_bt(logit_low, r_ref[...])
        total = dot_bt(weighted_now, full[:, low])
        for i, ref in enumerate(dxs):

            @pl.when(step == i)
            def _(i=i, ref=ref):
                ref[...] = dx.astype(BF16)
                for k in range(parts if by_part else 0):
                    los[i][at_ref[4] ^ k] = total[:, k * part : (k + 1) * part].astype(BF16)
                if not by_part:
                    los[i][...] = total.astype(BF16)

    def rows(n):
        return pl.BlockSpec((tok, n), lambda i, at_ref: (i, 0))

    outs = [struct((count * tok, n), BF16) for n in (hidden, 2 * hidden, LANES)]
    outs += [struct((tok, width), BF16)] * count
    outs += [struct((parts, tok, part) if by_part else (tok, width), BF16)] * count
    all_weights = flat_pair(pair) + flat_pair(router)
    ins = (spread, *tokens_in, *grads, *all_weights)
    weighted, d_high, logit, *rest = pl.pallas_call(
        kernel,
        out_shape=outs,
        grid_spec=pltpu.PrefetchScalarGridSpec(
            num_scalar_prefetch=1,
            grid=(count,),
            in_specs=[whole(spread.shape)] + [ANY] * (2 * count + len(all_weights)),
            out_specs=[rows(hidden), rows(2 * hidden), rows(LANES)]
            + [whole(o.shape) for o in outs[3:]],
            scratch_shapes=[
                full_weight(pair),
                full_weight(router, LANES),
                pltpu.VMEM((2, tok, width), BF16),
                pltpu.VMEM((2, tok, grads[0].shape[1]), BF16),
                weight_sems(pair, router),
                pltpu.SemaphoreType.DMA((2, 2)),
            ],
        ),
        compiler_params=params(),
        cost_estimate=cost(12 * count * tok * width * hidden, nbytes([*all_weights, *outs])),
        name="run_experts",
    )(at, *ins)
    return weighted, d_high, logit, rest[:count], rest[count:]


def weight_grads(at, place, outer_at, half_at, lefts, rights, parts, blocks, part, add=None, by_device=False, joined=False):
    unit = part * parts // blocks // 2
    stacks = [stack for group in rights for stack in group]
    left_flat = [a if isinstance(a, tuple) else (a, None) for runs in lefts for a in runs]
    if blocks != parts:
        width = part * parts
        totals = []
        for runs, group in zip(lefts, rights):
            runs = [
                lax.dynamic_index_in_dim(a[0], outer_at ^ a[1], 0, keepdims=False)
                if isinstance(a, tuple)
                else a
                for a in runs
            ]
            left = jnp.concatenate([a[:, :width] for a in runs], axis=0)
            left = left.reshape(left.shape[0], parts, 2, -1)[:, :, half_at].reshape(left.shape[0], -1)
            total = jnp.concatenate([dot_at(left, jnp.concatenate(x, axis=0)) for x in group], axis=1)
            total = total.reshape(blocks, unit, -1)
            order = [place ^ j for j in range(blocks)]
            out = jnp.stack([lax.dynamic_index_in_dim(total, i, 0, keepdims=False) for i in order])
            if add is not None and len(add) == 1:
                start = sum(a.shape[2] for a in totals)
                out = out + add[0][:, :, start : start + out.shape[2]].astype(F32)
            elif add is not None:
                out = out + add[len(totals)].astype(F32)
            order = [outer_at ^ j if by_device else j for j in range(blocks)]
            out = [lax.dynamic_index_in_dim(out, i, 0, keepdims=False) for i in order]
            totals.append(jnp.stack(out).astype(BF16))
        return [jnp.concatenate(totals, axis=2)] if joined else totals
    flat = [r for stack in stacks for r in stack]
    tokens = sum(r.shape[0] for r in stacks[0])
    sizes = [sum(stack[0].shape[1] for stack in group) for group in rights]
    n = sum(sizes)
    outs = [struct((blocks, unit, size), BF16) for size in ([n] if joined else sizes)]
    joins = [stack for stack in stacks if len(stack) > 1]
    extra = [] if add is None else add
    counts = [len(runs) for runs in lefts]

    def kernel(at_ref, *refs):
        left_refs, refs = refs[: len(left_flat)], refs[len(left_flat) :]
        right_refs, refs = refs[: len(flat)], refs[len(flat) :]
        added, refs = refs[: len(extra)], refs[len(extra) :]
        out_refs, fulls = refs[: len(outs)], refs[len(outs) :]
        step = pl.program_id(0)
        stacked = []
        for stack in stacks:
            stack_refs, right_refs = right_refs[: len(stack)], right_refs[len(stack) :]
            if len(stack) == 1:
                stacked.append(stack_refs[0])
            else:
                full, fulls = fulls[0], fulls[1:]
                stacked.append(full)

                @pl.when(step == 0)
                def _(full=full, stack_refs=stack_refs):
                    row = 0
                    for ref in stack_refs:
                        full[row : row + ref.shape[0]] = ref[...]
                        row += ref.shape[0]

        column, rest, more = 0, stacked, left_refs
        for i, (count, group) in enumerate(zip(counts, rights)):
            run_refs, more = more[:count], more[count:]
            now, rest = rest[: len(group)], rest[len(group) :]
            left = jnp.concatenate([ref[...].reshape(-1, unit) for ref in run_refs], axis=0).T
            column = column if joined else 0
            own = 0
            for right in now:
                cut = slice(column, column + right.shape[1])
                value = dot(left, right[...])
                if extra:
                    source, start = (added[0], column) if len(extra) == 1 else (added[i], own)
                    value = value + source[0, :, start : start + right.shape[1]].astype(F32)
                out_refs[0 if joined else i][0, :, cut] = value.astype(BF16)
                column, own = cut.stop, own + right.shape[1]

    def left_spec(a, i):
        if a.ndim == 3:
            return pl.BlockSpec(
                (1, a.shape[1], unit),
                lambda j, at_ref: (at_ref[1] ^ i, 0, 2 * (j ^ at_ref[0]) + half_at),
            )
        return pl.BlockSpec((a.shape[0], unit), lambda j, at_ref: (0, 2 * (j ^ at_ref[0]) + half_at))

    ins = (*[a for a, _ in left_flat], *flat, *extra)
    return pl.pallas_call(
        kernel,
        out_shape=outs,
        grid_spec=pltpu.PrefetchScalarGridSpec(
            num_scalar_prefetch=1,
            grid=(blocks,),
            in_specs=[left_spec(a, i) for a, i in left_flat]
            + [whole(a.shape) for a in flat]
            + [pl.BlockSpec((1,) + a.shape[1:], lambda j, at_ref: (j, 0, 0)) for a in extra],
            out_specs=[
                pl.BlockSpec(
                    (1,) + o.shape[1:], lambda j, at_ref: (at_ref[1] ^ j if by_device else j, 0, 0)
                )
                for o in outs
            ],
            scratch_shapes=[
                pltpu.VMEM((sum(a.shape[0] for a in stack), stack[0].shape[1]), BF16)
                for stack in joins
            ],
        ),
        compiler_params=params(),
        cost_estimate=cost(2 * tokens * blocks * unit * n, nbytes(ins)),
        name="weight_grads",
    )(at, *ins)


def by_owner(weights, blocks):
    unit, hidden = weights[0].shape[0], weights[0].shape[1] // blocks
    if hidden % LANES:
        return jnp.concatenate(
            [w.reshape(unit, blocks, hidden).transpose(1, 0, 2) for w in weights], axis=2
        )

    def kernel(*refs):
        for i, ref in enumerate(refs[:-1]):
            refs[-1][0, :, i * hidden : (i + 1) * hidden] = ref[...]

    out = struct((blocks, unit, hidden * len(weights)), BF16)
    return pl.pallas_call(
        kernel,
        out_shape=out,
        grid=(blocks,),
        in_specs=[pl.BlockSpec((unit, hidden), lambda i: (0, i)) for _ in weights],
        out_specs=pl.BlockSpec((1,) + out.shape[1:], lambda i: (i, 0, 0)),
        compiler_params=params(),
        cost_estimate=cost(1, 1),
        name="by_owner",
    )(*weights)


def by_columns(grads, hidden):
    blocks, unit, n = grads.shape
    starts = (0, hidden, 2 * hidden + LANES)
    if hidden % LANES:
        return [
            grads[:, :, start : start + hidden]
            .transpose(1, 0, 2)
            .reshape(unit, blocks * hidden)
            .astype(F32)
            for start in starts
        ]

    def kernel(ref, *outs):
        for start, out in zip(starts, outs):
            out[...] = ref[0, :, start : start + hidden].astype(F32)

    outs = [struct((unit, blocks * hidden), F32) for _ in starts]
    return pl.pallas_call(
        kernel,
        out_shape=outs,
        grid=(blocks,),
        in_specs=[pl.BlockSpec((1, unit, n), lambda i: (i, 0, 0))],
        out_specs=[pl.BlockSpec((unit, hidden), lambda i: (0, i)) for _ in starts],
        compiler_params=params(),
        cost_estimate=cost(0, nbytes([grads, *outs])),
        name="by_columns",
    )(grads)


def norm_back(values, pieces, scale, gain, gain_grad, outs, width):
    part = pieces[0].shape[1]
    cuts = [slice(k * part, (k + 1) * part) for k in range(len(pieces))]
    inner = 0.0
    for value, piece, cut in zip(values, pieces, cuts):
        gain_grad[:, cut] = jnp.sum(value * (piece * scale), axis=0, keepdims=True)
        inner = inner + jnp.sum(value * gain[:, cut] * piece, axis=1, keepdims=True)
    inner = inner * (scale * scale * scale / width)
    for value, piece, cut, out in zip(values, pieces, cuts, outs):
        out[...] = (value * gain[:, cut] * scale - piece * inner).astype(out.dtype)


def second_norm_back(received, pieces, gain):
    parts, blocks = len(pieces), len(received)
    tokens, width = received[0].shape
    part = width // parts
    outs = [struct((tokens, part), F32 if k == 0 else BF16) for k in range(parts)]
    outs.append(struct((1, width), F32))

    def kernel(*refs):
        got, refs = refs[:blocks], refs[blocks:]
        ins, (gain_ref, *outs, gain_grad) = refs[:parts], refs[parts:]
        values = []
        for k in range(parts):
            cut = slice(k * part, (k + 1) * part)
            values.append(sum(ref[:, cut].astype(F32) for ref in got))
        pieces = [ref[...].astype(F32) for ref in ins]
        scale = rms_scale(pieces, width)
        norm_back(values, pieces, scale, gain_ref, gain_grad, outs, width)

    ins = (*received, *pieces, gain)
    return pl.pallas_call(
        kernel,
        out_shape=outs,
        in_specs=[whole(a.shape) for a in ins],
        out_specs=[whole(o.shape) for o in outs],
        grid=(1,),
        compiler_params=params(),
        cost_estimate=cost(tokens * width * 20, nbytes(ins)),
        name="second_norm_back",
    )(*ins)


def project_back(
    at, grad_q, grad_kv, pre, pieces, gain, pair, query_gain, key_gain, cosine, sine, heads, kv_heads, gain_grad_two, router, experts
):
    parts, runs, blocks = len(pieces), len(grad_q), len(grad_kv)
    tokens, n = pre.shape
    width = gain.shape[1]
    part = width // parts
    size = query_gain.shape[1]
    gain_lines = -(-(2 * parts + 1) // 16) * 16
    lines = gain_lines + -(-experts // 16) * 16
    router_rows = router.shape[0]
    outs = [struct((tokens, part), F32)] + [struct((tokens + 2 * lines, part), BF16)] * (parts - 1)
    outs += [struct((tokens, n), BF16), struct((lines, part), F32)]

    def kernel(at_ref, pre_ref, two_ref, router_ref, *refs):
        gq, refs = refs[:runs], refs[runs:]
        gkv, refs = refs[:blocks], refs[blocks:]
        ins, refs = refs[:parts], refs[parts:]
        weights, refs = taken(refs, pair)
        gain_ref, qg, kg, cos_ref, sin_ref, *refs = refs
        outs, (d_wide, sums, gain_grad, full, sems) = refs[:parts], refs[parts:]
        for copy in weight_copies(at_ref, [weights], [full], sems, parts):
            copy.start()
        cosine, sine = cos_ref[...], sin_ref[...]
        totals = [jnp.zeros((1, size), F32), jnp.zeros((1, size), F32)]
        for i in range(n // size):
            cut = slice(i * size, (i + 1) * size)
            if i < heads:
                grad = jnp.concatenate([ref[:, cut] for ref in gq], axis=0)
            else:
                kv_cut = slice((i - heads) * size, (i - heads + 1) * size)
                grad = sum(ref[:, kv_cut].astype(F32) for ref in gkv)
            if i < heads + kv_heads:
                which = 0 if i < heads else 1
                gain_row = (qg, kg)[which][...]
                grad = grad * cosine + pltpu.roll(grad * sine, size // 2, 1)
                head = pre_ref[:, cut]
                scale = lax.rsqrt(jnp.mean(head * head, axis=1, keepdims=True) + EPS)
                unit = head * scale
                totals[which] = totals[which] + jnp.sum(grad * unit, axis=0, keepdims=True)
                grad = grad * gain_row
                grad = scale * (grad - unit * jnp.mean(grad * unit, axis=1, keepdims=True))
            d_wide[:, cut] = grad.astype(BF16)
        weight_wait([weights], [full], sems, parts)
        values = [
            dot_bt(d_wide[...], full[k * part : (k + 1) * part]) for k in range(parts)
        ]
        pieces = [ref[...].astype(F32) for ref in ins]
        scale = rms_scale(pieces, width)
        cut_outs = [outs[0]] + [out.at[:tokens] for out in outs[1:]]
        norm_back(values, pieces, scale, gain_ref, gain_grad, cut_outs, width)
        sums[...] = jnp.zeros_like(sums)
        for i, ref in enumerate((gain_grad, two_ref)):
            for k in range(parts):
                sums[i * parts + k : i * parts + k + 1] = ref[:, k * part : (k + 1) * part]
        for i, total in enumerate(totals):
            sums[2 * parts : 2 * parts + 1, i * size : (i + 1) * size] = total
        sums[gain_lines : gain_lines + experts, :router_rows] = router_ref[...].T[:experts]
        for out in outs[1:]:
            one, two = two_parts(sums[...])
            out[tokens : tokens + lines] = one
            out[tokens + lines :] = two

    ins = (pre, gain_grad_two, router, *grad_q, *grad_kv, *pieces, *flat_pair(pair))
    ins = (*ins, gain, query_gain, key_gain, cosine, sine)
    return pl.pallas_call(
        kernel,
        out_shape=outs,
        in_specs=[SMEM]
        + [whole(a.shape) for a in (pre, gain_grad_two, router, *grad_q, *grad_kv)]
        + [whole((tokens, part)) for _ in pieces]
        + [ANY] * len(flat_pair(pair))
        + [whole(a.shape) for a in (gain, query_gain, key_gain, cosine, sine)],
        out_specs=[whole(o.shape) for o in outs],
        scratch_shapes=[pltpu.VMEM((1, width), F32), full_weight(pair), weight_sems(pair)],
        grid=(1,),
        compiler_params=params(),
        cost_estimate=cost(2 * tokens * width * n, nbytes(ins)),
        name="project_back",
    )(at, *ins)


def sum_blocks(grads, widths, first=0):
    blocks = len(grads)
    unit = grads[0].shape[-2]

    def kernel(*refs):
        ins, outs = refs[:blocks], refs[blocks:]
        start = first
        for out in outs:
            cut = slice(start, start + out.shape[1])
            parts = [ref[:, cut] if len(ref.shape) == 2 else ref[0, :, cut] for ref in ins]
            out[...] = sum(a.astype(F32) for a in parts)
            start = cut.stop

    def spec(i, a):
        if a.ndim == 2:
            return whole(a.shape)
        return pl.BlockSpec((1,) + a.shape[1:], lambda _: (i, 0, 0))

    outs = [struct((unit, width), F32) for width in widths]
    return pl.pallas_call(
        kernel,
        out_shape=outs,
        grid=(1,),
        in_specs=[spec(i, a) for i, a in enumerate(grads)],
        out_specs=[whole(o.shape) for o in outs],
        compiler_params=params(),
        cost_estimate=cost(1, 1),
        name="sum_blocks",
    )(*grads)


def finish(at, residual, own, arrived, own_sums, low, unit_rows, experts):
    others = len(arrived)
    tokens, part = own.shape
    parts, half = others + 1, part // 2
    unit = half // low
    lines = own_sums.shape[0]
    gain_lines = -(-(2 * parts + 1) // 16) * 16

    def kernel(at_ref, residual, own, *refs):
        arrived, refs = refs[:others], refs[others:]
        own_sums, out, sums, router = refs
        even, col = at_ref[3] == 0, at_ref[4]

        def put(ref, rows, value):
            first = jnp.where(even, value[:, :half], value[:, half:])
            second = jnp.where(even, value[:, half:], value[:, :half])
            for i in range(low):
                cut = slice(i * unit, (i + 1) * unit)
                ref[rows, 2 * i * unit : (2 * i + 1) * unit] = first[:, cut].astype(ref.dtype)
                ref[rows, (2 * i + 1) * unit : (2 * i + 2) * unit] = second[:, cut].astype(ref.dtype)

        value = residual[...] + own[...]
        for ref in arrived:
            value = value + ref[:tokens].astype(F32)
        put(out, slice(0, tokens), value)
        got = [ref[tokens : tokens + lines].astype(F32) for ref in arrived]
        got = [a + ref[tokens + lines :].astype(F32) for a, ref in zip(got, arrived)]
        total = own_sums[...]
        for a in got:
            total = total + a
        sums[...] = total[:gain_lines]
        router[...] = total[gain_lines : gain_lines + experts, :unit_rows].T
        for i in range(2):
            for k in range(parts):
                line = own_sums[i * parts + k : i * parts + k + 1]
                for mask, a in enumerate(got, 1):
                    row = i * parts + (k ^ mask)
                    line = line + a[row : row + 1]
                for to in range(parts):

                    @pl.when(col ^ k == to)
                    def _(i=i, to=to, line=line):
                        put(sums, slice(i * parts + to, i * parts + to + 1), line)

    outs = (
        struct((tokens, part), BF16),
        struct((gain_lines, part), F32),
        struct((unit_rows, experts), F32),
    )
    ins = (residual, own, *arrived, own_sums)
    return pl.pallas_call(
        kernel,
        out_shape=outs,
        grid=(1,),
        in_specs=[SMEM] + [whole(a.shape) for a in ins],
        out_specs=[whole(o.shape) for o in outs],
        compiler_params=params(),
        cost_estimate=cost(1, 1),
        name="finish",
    )(at, *ins)


def per_device(
    layer_in,
    out_grad,
    lengths,
    token_order,
    choices,
    norm_gain,
    w_query,
    w_key,
    w_value,
    query_gain,
    key_gain,
    w_out,
    ffn_gain,
    w_router,
    w_gate,
    w_up,
    w_down,
):
    micro, tok, part = layer_in.shape
    outer, cols = lax.axis_size("outer"), lax.axis_size("col")
    rows = 2 * outer
    tokens = micro * tok
    width = part * cols
    outer_at, core_at, col_at = (lax.axis_index(name) for name in ("outer", "core", "col"))
    row_at = outer_at * 2 + core_at
    low = outer // cols
    unit = width // rows
    half = part // 2
    size = query_gain.shape[0]
    heads = w_query.shape[1] // size
    kv_heads = w_key.shape[1] // size
    experts = w_router.shape[1]
    hidden = w_gate.shape[1] // outer
    repeats = hidden // experts

    place = outer_at ^ (col_at * low)
    at = jnp.stack([place, outer_at, col_at * low, core_at, col_at]).astype(jnp.int32)

    def core_swap(a):
        return lax.ppermute(a, "core", [(0, 1), (1, 0)])

    def col_swap(a, mask):
        return lax.ppermute(a, "col", [(i, i ^ mask) for i in range(cols)])

    def exchange(a):
        return lax.all_to_all(a, "outer", 0, 0, tiled=True)

    def col_exchange(a):
        return lax.all_to_all(a, "col", 0, 0, tiled=True)

    def for_all(a):
        return jnp.broadcast_to(a[None], (outer,) + a.shape)

    def after(a, b):
        return lax.optimization_barrier((a, b))[0]

    def to_halves(a):
        blocks = a.reshape(a.shape[:-1] + (low, 2, unit))
        first = blocks[..., 0, :].reshape(a.shape[:-1] + (half,))
        second = blocks[..., 1, :].reshape(a.shape[:-1] + (half,))
        even = core_at == 0
        return jnp.concatenate(
            [jnp.where(even, first, second), jnp.where(even, second, first)], axis=-1
        )

    def from_halves(a):
        even = core_at == 0
        first = jnp.where(even, a[..., :half], a[..., half:]).reshape(a.shape[:-1] + (low, unit))
        second = jnp.where(even, a[..., half:], a[..., :half]).reshape(a.shape[:-1] + (low, unit))
        return jnp.stack([first, second], axis=-2).reshape(a.shape)

    def col_gather(a):
        return [a] + [col_swap(a, k) for k in range(1, cols)]

    def col_total(pieces):
        total = pieces[0]
        for k in range(1, cols):
            total = total + col_swap(pieces[k], k).astype(F32)
        return total

    def swap(a, mask):
        return lax.ppermute(a, "outer", [(i, i ^ mask) for i in range(outer)])

    def gather(a):
        return [a] + [swap(a, j) for j in range(1, outer)]

    def scatter(blocks):
        return [blocks[0]] + [swap(blocks[j], j) for j in range(1, outer)]

    def swap(a, mask):
        return lax.ppermute(a, "outer", [(i, i ^ mask) for i in range(outer)])

    def gather(a):
        return [a] + [swap(a, j) for j in range(1, outer)]

    def scatter(blocks):
        return [blocks[0]] + [swap(blocks[j], j) for j in range(1, outer)]

    def both(*arrays):
        return lax.optimization_barrier(arrays)

    def both_cores(a):
        return a, [core_swap(b) for b in a] if isinstance(a, list) else core_swap(a)

    own_in = to_halves(layer_in).reshape(tokens, part)
    own_grad = to_halves(out_grad).reshape(tokens, part)
    w_in = gather(jnp.concatenate([w_query, w_key, w_value], axis=1))
    arrived = col_gather(own_in)
    w_back = jnp.concatenate([w_out, jnp.pad(w_router, ((0, 0), (0, LANES - experts)))], axis=1)
    w_back = for_all(w_back)
    weights = by_owner([w_gate, w_up, w_down], outer)
    q_gain, k_gain = query_gain[None, :], key_gain[None, :]
    frequency = jnp.exp(jnp.arange(size // 2, dtype=F32) * (-2.0 * math.log(THETA) / size))
    bias, angles, chosen, spread, gain_one, gain_two = prepare(
        at,
        lengths,
        token_order.reshape(micro, rows, tok),
        choices.reshape(tokens, -1),
        jnp.concatenate([frequency, frequency])[None, :],
        jnp.stack([norm_gain, ffn_gain]).reshape(2, cols, part),
        low,
        hidden,
        experts,
    )
    cosine = jnp.cos(angles)
    sine = jnp.sin(angles) * jnp.where(jnp.arange(size) < size // 2, -1.0, 1.0)

    w_back, weights, bias = both(w_back, weights, bias)
    w_back = exchange(w_back)
    w_in, arrived, weights, chosen, bias, cosine, sine, gain_one, gain_two, spread = both(
        w_in, arrived, weights, chosen, bias, cosine, sine, gain_one, gain_two, spread
    )
    own_grads = col_gather(after(own_grad, w_in))
    w_in = both_cores(w_in)
    normed_one, pre, ready, kv = project(
        at, arrived, part, gain_one, w_in, q_gain, k_gain, cosine, sine, heads, kv_heads
    )
    near = [j for j in range(1, outer) if not j & (j - 1)]
    far = [j for j in range(1, outer) if j & (j - 1)]
    far_grads, _ = both(jnp.concatenate([own_grad, chosen], axis=1), w_in[0])
    far_grads = [swap(far_grads, j) for j in far]
    kv_own = jnp.stack(gather(kv))
    kv_own, w_back, far_grads = both(kv_own, w_back, far_grads)
    weights = exchange(after(weights, w_back))
    kv_other = core_swap(kv_own)
    w_back = both_cores(w_back)
    attended, lse = attend(ready, kv_own, kv_other, bias, heads, kv_heads, size)
    attn_parts = expand(at, attended, w_back, part, cols)
    attn_parts, own_grads = both(attn_parts, own_grads)

    grads = [jnp.concatenate(own_grads + [chosen], axis=1)] + [None] * (outer - 1)
    near_grads = [swap(grads[0], j) for j in near]

    residual = own_in.astype(F32) + col_total(attn_parts)
    residual, weights = both(residual, weights)
    full_res = col_gather(residual.astype(BF16))
    full_res, near_grads, weights = both(full_res, near_grads, weights)
    for j, a in zip(near, near_grads):
        grads[j] = a
    weights = both_cores(weights)
    normed_two = second_norm(full_res, gain_two)
    expert_in = gather(normed_two)
    far_grads, _ = both(far_grads, normed_two)
    for j, a in zip(far, far_grads):
        grads[j] = jnp.concatenate(col_gather(a[:, :part]) + [a[:, part:]], axis=1)

    results, dx, lo = [], [None] * outer, [None] * outer
    order = [0] + far + near
    for group in [[0]] + [far[i : i + 4] for i in range(0, len(far), 4)] + [near]:
        *result, dx_now, lo_now = run_experts(
            at,
            [expert_in[j] for j in group],
            [grads[j] for j in group],
            spread,
            weights,
            w_back,
            heads * size,
            cols,
            group != near,
        )
        for j, a, b in zip(group, dx_now, lo_now):
            dx[j], lo[j] = a, b
        if group == [0]:
            expert_in, lo[0] = both(expert_in, lo[0])
        elif group != near:
            for j in group:
                dx[j] = swap(dx[j], j)
            if group[-1] == far[-1]:
                lo_sums = col_exchange(jnp.concatenate([lo[j] for j in [0] + far], axis=1))
        results.append(result)
    far_dx, results[-1] = both([dx[j] for j in far], results[-1])
    weighted, d_high, logit_low = [list(arrays) for arrays in zip(*results)]
    for j in near:
        dx[j] = swap(dx[j], j)
    sizes = (cols, outer, part)
    expert_sides = (
        [[expert_in[j] for j in order], [grads[j] for j in order]],
        [[d_high, logit_low], [weighted]],
    )
    (other,) = weight_grads(at, place, outer_at, 1, *expert_sides, *sizes, joined=True)
    other, near_dx, lo_sums = both(other, [dx[j] for j in near], lo_sums)
    lo_sums = jnp.sum(lo_sums.astype(F32), axis=0)
    lo[0] = lo_sums[:tokens]
    lo_far = [lo_sums[i * tokens : (i + 1) * tokens].astype(BF16) for i in range(1, len(far) + 1)]
    other = core_swap(other)
    *spread_two, gain_grad_two = second_norm_back([dx[0]] + near_dx + far_dx, full_res, gain_two)
    lo_near, _ = both([lo[j] for j in near], spread_two)
    lo_near = [swap(a, j) for j, a in zip(near, lo_near)]
    (expert_grads,) = weight_grads(
        at, place, outer_at, 0, *expert_sides, *sizes, [other], True, True
    )
    spread_two[0], expert_grads = both(spread_two[0], expert_grads)
    grad_residual = own_grad.astype(F32) + col_total(spread_two)
    grad_residual, lo_near, expert_grads = both(grad_residual, lo_near, expert_grads)
    expert_grads = exchange(expert_grads)
    grad_feats = col_gather(grad_residual.astype(BF16))

    lo_near = sum(a.astype(F32) for a in lo_near)
    lo_near = [
        lo_near[:, k * part : (k + 1) * part].astype(F32 if k == 0 else BF16) for k in range(cols)
    ]
    grad_feats, lo_near = both(grad_feats, lo_near)
    back_attended = contract(at, grad_feats, w_back, heads * size)
    lo_near = col_total(after(lo_near, back_attended))
    grad_q, kv_mine, kv_theirs = attend_back(
        ready, kv_own, kv_other, bias, lse, back_attended, heads, kv_heads, size
    )
    kv_theirs, expert_grads, lo_near = both(kv_theirs, expert_grads, lo_near)
    kv_sums = sum_cores(kv_mine, core_swap(kv_theirs))
    grad_kv = scatter(kv_sums)
    router_part = jnp.sum(
        expert_grads[:, :, 2 * hidden : 2 * hidden + LANES].astype(F32), axis=0
    )
    feats, lo_far, _ = both(grad_feats, lo_far, kv_sums)
    lo_far = [swap(a, j) for j, a in zip(far, lo_far)]
    feats = [jnp.concatenate(feats, axis=1)]
    (other,) = weight_grads(at, place, outer_at, 1, [feats], [[[attended]]], *sizes)
    (out_grads,) = weight_grads(
        at, place, outer_at, 0, [feats], [[[attended]]], *sizes, [core_swap(other)], True
    )
    grad_kv, out_grads = both(grad_kv, out_grads)
    out_grads = exchange(out_grads)
    *spread_one, d_wide, sums = project_back(
        at,
        [grad_q],
        grad_kv,
        pre,
        arrived,
        gain_one,
        w_in,
        q_gain,
        k_gain,
        cosine,
        sine,
        heads,
        kv_heads,
        gain_grad_two,
        router_part,
        experts,
    )
    (other,) = weight_grads(at, place, outer_at, 1, [[normed_one]], [[[d_wide]]], *sizes)
    other, expert_grads, lo_far = both(other, expert_grads, lo_far)
    grad_gate_w, grad_up_w, grad_down_w = by_columns(expert_grads, hidden)
    other = jnp.stack([core_swap(other[j]) for j in range(outer)])
    other, grad_gate_w, out_grads = both(other, grad_gate_w, out_grads)
    (wide_grads,) = weight_grads(
        at, place, outer_at, 0, [[normed_one]], [[[d_wide]]], *sizes, [other], True
    )
    spread_one, wide_grads = both(spread_one, wide_grads)
    wide_grads = exchange(wide_grads)

    got = [col_swap(spread_one[k], k) for k in range(1, cols)]
    layer_out = residual + lo[0] + lo_near + sum(a.astype(F32) for a in lo_far)
    layer_out = from_halves(layer_out.astype(BF16)).reshape(micro, tok, part)
    input_grad, sums, grad_router = finish(
        at, grad_residual, spread_one[0], got, sums, low, unit, experts
    )
    input_grad = input_grad.reshape(micro, tok, part)
    sums = sums + core_swap(sums)
    sums = sum(gather(sums))
    (grad_out_w,) = sum_blocks([out_grads] * outer, [heads * size])
    wide_grads, input_grad, layer_out, grad_out_w, sums, grad_router = both(
        wide_grads, input_grad, layer_out, grad_out_w, sums, grad_router
    )
    head_sums = sums[2 * cols, : 2 * size]
    grad_query_w, grad_key_w, grad_value_w = sum_blocks(
        [wide_grads] * outer, [w.shape[1] for w in (w_query, w_key, w_value)]
    )
    return (
        layer_out,
        input_grad,
        sums[:cols].reshape(width),
        grad_query_w,
        grad_key_w,
        grad_value_w,
        head_sums[:size],
        head_sums[size:],
        grad_out_w,
        sums[cols : 2 * cols].reshape(width),
        grad_router,
        grad_gate_w,
        grad_up_w,
        grad_down_w,
    )


def solution(mesh):
    rows, cols = mesh.devices.shape
    split = Mesh(mesh.devices.reshape(rows // 2, 2, cols), ("outer", "core", "col"))
    tokens_placed = P(None, ROW, "col")
    weight_placed = P(ROW, "col")
    return jax.shard_map(
        per_device,
        mesh=split,
        in_specs=(
            tokens_placed,
            tokens_placed,
            P(),
            P(),
            P(None, ROW, None),
            P(),
            weight_placed,
            weight_placed,
            weight_placed,
            P(),
            P(),
            weight_placed,
            P(),
            P(ROW, None),
            weight_placed,
            weight_placed,
            weight_placed,
        ),
        out_specs=(
            tokens_placed,
            tokens_placed,
            P(),
            weight_placed,
            weight_placed,
            weight_placed,
            P(),
            P(),
            weight_placed,
            P(),
            P(ROW, None),
            weight_placed,
            weight_placed,
            weight_placed,
        ),
        check_vma=False,
    )
```

```python
import functools
import math

import jax
import jax.numpy as jnp
from jax import lax
from jax.experimental import pallas as pl
from jax.experimental.pallas import tpu as pltpu
from jax.sharding import Mesh
from jax.sharding import PartitionSpec as P

EPS = 1e-06
THETA = 1000000.0
NEGATIVE = -1e30
F32 = jnp.float32
BF16 = jnp.bfloat16
VMEM_BYTES = 56 * 1024 * 1024
LANES = 128
ROW = ("outer", "core")


def dot(a, b):
    return jnp.dot(a, b, preferred_element_type=F32)


def dot_bt(a, b):
    return lax.dot_general(a, b, (((1,), (1,)), ((), ())), preferred_element_type=F32)


def dot_at(a, b):
    return lax.dot_general(a, b, (((0,), (0,)), ((), ())), preferred_element_type=F32)


def two_parts(a):
    high = a.astype(BF16)
    return high, (a - high.astype(F32)).astype(BF16)


ANY = pl.BlockSpec(memory_space=pl.ANY)
SMEM = pl.BlockSpec(memory_space=pltpu.SMEM)


def whole(shape):
    return pl.BlockSpec(shape, lambda *_: (0,) * len(shape))


def params(steps=1, limit=VMEM_BYTES):
    return pltpu.CompilerParams(
        dimension_semantics=("arbitrary",) * steps, vmem_limit_bytes=limit
    )


def cost(flops, moved):
    return pl.CostEstimate(flops=int(flops) // 64, bytes_accessed=int(moved) // 64, transcendentals=0)


def nbytes(arrays):
    return sum(math.prod(a.shape) * a.dtype.itemsize for a in arrays)


def struct(shape, dtype):
    return jax.ShapeDtypeStruct(shape, dtype)


def block_count(pair):
    return len(pair[0]) if isinstance(pair[0], list) else pair[0].shape[0]


def weight_copies(at_ref, pairs, fulls, sems, parts, firsts=None):
    copies, base = [], 0
    for i, (pair, full) in enumerate(zip(pairs, fulls)):
        first = firsts[i] if firsts else 0
        blocks = block_count(pair)
        low = blocks // parts
        unit = full.shape[0] // blocks // 2
        for h, sources in enumerate(pair):
            listed = isinstance(sources, list)
            for j in range(blocks):
                to = at_ref[0 if listed else 2] ^ j
                source = sources[j] if listed else sources.at[j]
                row = (2 * (to // low) + h) * (low * unit) + lax.rem(to, low) * unit
                copies.append(
                    pltpu.make_async_copy(
                        source.at[:, pl.ds(first, full.shape[1])],
                        full.at[pl.ds(pl.multiple_of(row, unit), unit)],
                        sems.at[base + h * blocks + to],
                    )
                )
        base += 2 * blocks
    return copies


def weight_wait(pairs, fulls, sems, parts, part=None):
    base = 0
    for pair, full in zip(pairs, fulls):
        blocks = block_count(pair)
        low = blocks // parts
        unit = full.shape[0] // blocks // 2
        for h in range(2):
            for to in range(blocks):
                if part is None or to // low == part:
                    row = (2 * (to // low) + h) * (low * unit) + to % low * unit
                    source = pair[h][0] if isinstance(pair[h], list) else pair[h].at[0]
                    pltpu.make_async_copy(
                        source.at[:, pl.ds(0, full.shape[1])],
                        full.at[pl.ds(row, unit)],
                        sems.at[base + h * blocks + to],
                    ).wait()
        base += 2 * blocks


def full_weight(pair, n=None):
    unit, width = (pair[0][0] if isinstance(pair[0], list) else pair[0]).shape[-2:]
    return pltpu.VMEM((2 * block_count(pair) * unit, n or width), BF16)


def weight_sems(*pairs):
    return pltpu.SemaphoreType.DMA((sum(2 * block_count(pair) for pair in pairs),))


def flat_pair(pair):
    return [a for half in pair for a in (half if isinstance(half, list) else [half])]


def taken(refs, pair):
    halves = []
    for half in pair:
        if isinstance(half, list):
            halves.append(list(refs[: len(half)]))
            refs = refs[len(half) :]
        else:
            halves.append(refs[0])
            refs = refs[1:]
    return tuple(halves), refs


def rms_scale(pieces, width):
    total = sum(jnp.sum(piece * piece, axis=1, keepdims=True) for piece in pieces)
    return lax.rsqrt(total / width + EPS)


def prepare(at, lengths, order, choices, frequency, gains, low, hidden, experts):
    micro, rows, tok = order.shape
    tokens, top = choices.shape
    _, cols, part = gains.shape
    unit = part // 2 // low
    outer, seqs, size = rows // 2, lengths.shape[1], frequency.shape[1]

    def kernel(at_ref, len_ref, order_ref, choice_ref, freq_ref, gain_ref, bias, angles, chosen, spread, *ordered):
        outer_at, core, col = at_ref[1], at_ref[3], at_ref[4]
        for b in range(micro):

            def seq_of(value):
                seq, start, end = jnp.zeros_like(value), jnp.zeros_like(value), 0
                for i in range(seqs):
                    end = end + len_ref[b, i]
                    passed = value >= end
                    seq = seq + jnp.where(passed, 1, 0)
                    start = start + jnp.where(passed, len_ref[b, i], 0)
                return seq, start

            def row(at):
                return order_ref[b, pl.ds(at, 1), :]

            own = row(2 * outer_at + core)
            own_seq, own_start = seq_of(own)
            keys = jnp.concatenate(
                [row(2 * (outer_at ^ j) + (core ^ h)) for h in range(2) for j in range(outer)], axis=0
            )
            key_seq, _ = seq_of(keys)
            lines = [keys, key_seq, own - own_start]
            lines.append(jnp.zeros((tok - 2 * rows - 1, tok), jnp.int32))
            turned = jnp.concatenate(lines, axis=0).astype(F32).T
            own, own_seq = own.astype(F32), own_seq.astype(F32)
            for i in range(rows):
                allowed = (turned[:, rows + i : rows + i + 1] == own_seq) & (
                    turned[:, i : i + 1] <= own
                )
                bias[b, i * tok : (i + 1) * tok] = jnp.where(allowed, 0.0, NEGATIVE)
            angles[b * tok : (b + 1) * tok] = turned[:, 2 * rows : 2 * rows + 1] * freq_ref[...]
        lanes = lax.broadcasted_iota(jnp.int32, (tokens, LANES), 1)
        hits = jnp.zeros((tokens, LANES), F32)
        for i in range(top):
            hits = hits + jnp.where(choice_ref[:, i : i + 1] == lanes, 1.0, 0.0)
        chosen[...] = hits.astype(BF16)
        units = lax.broadcasted_iota(jnp.int32, (LANES, hidden), 1)
        owners = lax.broadcasted_iota(jnp.int32, (LANES, hidden), 0)
        spread[...] = jnp.where(lax.rem(units, experts) == owners, 1.0, 0.0).astype(BF16)
        for i, out in enumerate(ordered):
            for k in range(cols):
                line = gain_ref[i, pl.ds(col ^ k, 1), :]
                for n in range(low):
                    first = line[:, 2 * n * unit : (2 * n + 1) * unit]
                    second = line[:, (2 * n + 1) * unit : (2 * n + 2) * unit]
                    start = k * part + n * unit
                    out[:, start : start + unit] = jnp.where(core == 0, first, second)
                    start = start + part // 2
                    out[:, start : start + unit] = jnp.where(core == 0, second, first)

    outs = (
        struct((micro, rows * tok, tok), F32),
        struct((tokens, size), F32),
        struct((tokens, LANES), BF16),
        struct((LANES, hidden), BF16),
        struct((1, cols * part), F32),
        struct((1, cols * part), F32),
    )
    ins = (order, choices, frequency, gains)
    return pl.pallas_call(
        kernel,
        out_shape=outs,
        grid=(1,),
        in_specs=[SMEM, SMEM] + [whole(a.shape) for a in ins],
        out_specs=[whole(o.shape) for o in outs],
        compiler_params=params(),
        cost_estimate=cost(1, 1),
        name="prepare",
    )(at, lengths, *ins)


def project(at, pieces, part, gain, pair, query_gain, key_gain, cosine, sine, heads, kv_heads):
    parts = len(pieces)
    tokens = cosine.shape[0]
    width = parts * part
    n = flat_pair(pair)[0].shape[-1]
    size = query_gain.shape[1]

    def kernel(at_ref, *refs):
        ins, refs = refs[:parts], refs[parts:]
        weights, refs = taken(refs, pair)
        gain_ref, qg, kg, cos_ref, sin_ref, normed, pre, ready, kv, full, sems = refs
        for copy in weight_copies(at_ref, [weights], [full], sems, parts):
            copy.start()
        values = [ref[...].astype(F32) for ref in ins]
        scale = rms_scale(values, width)
        for k, value in enumerate(values):
            cut = slice(k * part, (k + 1) * part)
            normed[:, cut] = (value * scale * gain_ref[:, cut]).astype(BF16)
        weight_wait([weights], [full], sems, parts)
        pre[...] = dot(normed[...], full[...])
        cosine, sine = cos_ref[...], sin_ref[...]
        for i in range(n // size):
            cut = slice(i * size, (i + 1) * size)
            head = pre[:, cut]
            if i < heads + kv_heads:
                head_gain = qg[...] if i < heads else kg[...]
                head = (
                    head
                    * lax.rsqrt(jnp.mean(head * head, axis=1, keepdims=True) + EPS)
                    * head_gain
                )
                head = head * cosine + pltpu.roll(head, size // 2, 1) * sine
            if i < heads:
                ready[:, cut] = head.astype(BF16)
            else:
                kv[:, (i - heads) * size : (i - heads + 1) * size] = head.astype(BF16)

    outs = (
        struct((tokens, width), BF16),
        struct((tokens, n), F32),
        struct((tokens, heads * size), BF16),
        struct((tokens, n - heads * size), BF16),
    )
    ins = (*pieces, *flat_pair(pair), gain, query_gain, key_gain, cosine, sine)
    return pl.pallas_call(
        kernel,
        out_shape=outs,
        in_specs=[SMEM]
        + [whole((tokens, part)) for _ in pieces]
        + [ANY] * len(flat_pair(pair))
        + [whole(a.shape) for a in (gain, query_gain, key_gain, cosine, sine)],
        out_specs=[whole(o.shape) for o in outs],
        scratch_shapes=[full_weight(pair), weight_sems(pair)],
        grid=(1,),
        compiler_params=params(),
        cost_estimate=cost(4.5e11, 1),
        name="project",
    )(at, *ins)


def attend(ready, own, other, bias, heads, kv_heads, size):
    micro, keys, tok = bias.shape
    group = heads // kv_heads
    outer = own.shape[0]
    scale = 1.0 / math.sqrt(size)

    def kernel(q_ref, own_ref, other_ref, bias_ref, out_ref, lse_ref):
        for h in range(heads):
            key, value = (
                jnp.concatenate(
                    [
                        ref[:, :, i * size : (i + 1) * size].reshape(outer * tok, size)
                        for ref in (own_ref, other_ref)
                    ],
                    axis=0,
                )
                for i in (h // group, kv_heads + h // group)
            )
            cut = slice(h * size, (h + 1) * size)
            scores = dot_bt(key, q_ref[:, cut]) * scale + bias_ref[0]
            peak = jnp.max(scores, axis=0, keepdims=True)
            powers = jnp.exp(scores - peak)
            total = jnp.sum(powers, axis=0, keepdims=True)
            probs = (powers * (1.0 / total)).astype(BF16)
            out_ref[:, cut] = dot_at(probs, value).astype(BF16)
            lse_ref[0, h] = peak + jnp.log(total)

    kv_spec = pl.BlockSpec((outer, tok, own.shape[2]), lambda m: (0, m, 0))
    head_spec = pl.BlockSpec((tok, heads * size), lambda m: (m, 0))
    outs = (struct((micro * tok, heads * size), BF16), struct((micro, heads, 1, tok), F32))
    return pl.pallas_call(
        kernel,
        out_shape=outs,
        grid=(micro,),
        in_specs=[
            head_spec,
            kv_spec,
            kv_spec,
            pl.BlockSpec((1, keys, tok), lambda m: (m, 0, 0)),
        ],
        out_specs=[head_spec, pl.BlockSpec((1, heads, 1, tok), lambda m: (m, 0, 0, 0))],
        compiler_params=params(limit=40 * 1024 * 1024),
        cost_estimate=cost(4 * micro * heads * keys * tok * size, nbytes((own, other, bias))),
        name="attend",
    )(ready, own, other, bias)


def attend_back(ready, own, other, bias, lse, grad, heads, kv_heads, size):
    micro, keys, tok = bias.shape
    group = heads // kv_heads
    outer = own.shape[0]
    scale = 1.0 / math.sqrt(size)
    mid = keys // 2

    def kernel(q_ref, own_ref, other_ref, bias_ref, lse_ref, g_ref, gq, mine, theirs, gk, gv):
        for h in range(heads):
            key, value = (
                jnp.concatenate(
                    [
                        ref[:, :, i * size : (i + 1) * size].reshape(outer * tok, size)
                        for ref in (own_ref, other_ref)
                    ],
                    axis=0,
                )
                for i in (h // group, kv_heads + h // group)
            )
            cut = slice(h * size, (h + 1) * size)
            query, out_grad = q_ref[:, cut], g_ref[:, cut]
            scores = dot_bt(key, query) * scale + bias_ref[0]
            probs = jnp.exp(scores - lse_ref[0, h])
            back = dot_bt(value, out_grad)
            centre = jnp.sum(probs * back, axis=0, keepdims=True)
            slope = (probs * (back - centre)).astype(BF16)
            gq[:, cut] = dot_at(slope, key) * scale
            key_part = dot(slope, query) * scale
            value_part = dot(probs.astype(BF16), out_grad)
            if h % group == 0:
                gk[...] = key_part
                gv[...] = value_part
            else:
                gk[...] += key_part
                gv[...] += value_part
            if h % group == group - 1:
                for i, ref in enumerate((gk, gv)):
                    at = (i * kv_heads + h // group) * size
                    cut = slice(at, at + size)
                    mine[:, :, cut] = ref[:mid].reshape(outer, tok, size)
                    theirs[:, :, cut] = ref[mid:].reshape(outer, tok, size).astype(BF16)

    kv_spec = pl.BlockSpec((outer, tok, own.shape[2]), lambda m: (0, m, 0))
    head_spec = pl.BlockSpec((tok, heads * size), lambda m: (m, 0))
    kv_shape = (outer, micro * tok, 2 * kv_heads * size)
    outs = (
        struct((micro * tok, heads * size), F32),
        struct(kv_shape, F32),
        struct(kv_shape, BF16),
    )
    return pl.pallas_call(
        kernel,
        out_shape=outs,
        grid=(micro,),
        in_specs=[
            head_spec,
            kv_spec,
            kv_spec,
            pl.BlockSpec((1, keys, tok), lambda m: (m, 0, 0)),
            pl.BlockSpec((1, heads, 1, tok), lambda m: (m, 0, 0, 0)),
            head_spec,
        ],
        out_specs=[head_spec, kv_spec, kv_spec],
        scratch_shapes=[pltpu.VMEM((keys, size), F32)] * 2,
        compiler_params=params(),
        cost_estimate=cost(10 * micro * heads * keys * tok * size, nbytes((own, other, bias))),
        name="attend_back",
    )(ready, own, other, bias, lse, grad)


def sum_cores(mine, theirs):
    outer, tokens, n = mine.shape

    def kernel(mine, theirs, *outs):
        for j, out in enumerate(outs):
            out[...] = (mine[j] + theirs[j].astype(F32)).astype(BF16)

    outs = [struct((tokens, n), BF16)] * outer
    return pl.pallas_call(
        kernel,
        out_shape=outs,
        grid=(1,),
        in_specs=[whole(mine.shape)] * 2,
        out_specs=[whole(o.shape) for o in outs],
        compiler_params=params(),
        cost_estimate=cost(1, 1),
        name="sum_cores",
    )(mine, theirs)


def expand(at, a, pair, part, parts):
    tokens, n = a.shape
    outs = [struct((tokens, part), F32 if k == 0 else BF16) for k in range(parts)]

    def kernel(at_ref, a_ref, *refs):
        weights, refs = taken(refs, pair)
        outs, (full, sems) = refs[:parts], refs[parts:]
        for copy in weight_copies(at_ref, [weights], [full], sems, parts):
            copy.start()
        for k, out in enumerate(outs):
            weight_wait([weights], [full], sems, parts, k)
            out[...] = dot_bt(a_ref[...], full[k * part : (k + 1) * part]).astype(out.dtype)

    ins = (a, *flat_pair(pair))
    return pl.pallas_call(
        kernel,
        out_shape=outs,
        in_specs=[SMEM, whole(a.shape)] + [ANY] * len(flat_pair(pair)),
        out_specs=[whole(o.shape) for o in outs],
        scratch_shapes=[full_weight(pair, n), weight_sems(pair)],
        grid=(1,),
        compiler_params=params(limit=40 * 1024 * 1024),
        cost_estimate=cost(2 * tokens * n * part * parts, nbytes(ins)),
        name="expand",
    )(at, *ins)


def contract(at, pieces, pair, n):
    parts = len(pieces)
    tokens, part = pieces[0].shape
    outs = (struct((tokens, n), BF16), struct((tokens, part * parts), BF16))

    def kernel(at_ref, *refs):
        ins, refs = refs[:parts], refs[parts:]
        weights, (out, joined, full, sems) = taken(refs, pair)
        for copy in weight_copies(at_ref, [weights], [full], sems, parts):
            copy.start()
        total = 0.0
        for k, ref in enumerate(ins):
            weight_wait([weights], [full], sems, parts, k)
            joined[:, k * part : (k + 1) * part] = ref[...]
            total = total + dot(ref[...], full[k * part : (k + 1) * part])
        out[...] = total.astype(BF16)

    ins = (*pieces, *flat_pair(pair))
    return pl.pallas_call(
        kernel,
        out_shape=outs,
        in_specs=[SMEM] + [whole(a.shape) for a in pieces] + [ANY] * len(flat_pair(pair)),
        out_specs=[whole(o.shape) for o in outs],
        scratch_shapes=[full_weight(pair, n), weight_sems(pair)],
        grid=(1,),
        compiler_params=params(),
        cost_estimate=cost(2 * tokens * n * part * parts, nbytes(ins)),
        name="contract",
    )(at, *ins)


def second_norm(pieces, gain):
    parts = len(pieces)
    tokens, part = pieces[0].shape
    width = parts * part
    out = struct((tokens, width), BF16)

    def kernel(*refs):
        ins, (gain_ref, out_ref) = refs[:parts], refs[parts:]
        values = [ref[...].astype(F32) for ref in ins]
        scale = rms_scale(values, width)
        for k, value in enumerate(values):
            cut = slice(k * part, (k + 1) * part)
            out_ref[:, cut] = (value * scale * gain_ref[:, cut]).astype(BF16)

    return pl.pallas_call(
        kernel,
        out_shape=out,
        in_specs=[whole(a.shape) for a in pieces] + [whole(gain.shape)],
        out_specs=whole(out.shape),
        grid=(1,),
        compiler_params=params(),
        cost_estimate=cost(tokens * width * 4, nbytes((*pieces, out))),
        name="second_norm",
    )(*pieces, gain)


def run_experts(at, tokens_in, grads, spread, pair, router, router_at, parts, by_part):
    count = len(tokens_in)
    tok, width = tokens_in[0].shape
    hidden = flat_pair(pair)[0].shape[-1] // 3
    part = width // parts
    lo_count = parts if by_part else 1

    def kernel(at_ref, s_ref, *refs):
        x_refs, refs = refs[:count], refs[count:]
        g_refs, refs = refs[:count], refs[count:]
        weights, refs = taken(refs, pair)
        routers, refs = taken(refs, router)
        weighted, d_high, logit, *refs = refs
        dxs, refs = refs[:count], refs[count:]
        los, refs = refs[: count * lo_count], refs[count * lo_count :]
        full, r_ref, x_now, g_now, sems, x_sems = refs
        pairs, fulls = [weights, routers], [full, r_ref]
        high, low = slice(0, 2 * hidden), slice(2 * hidden, 3 * hidden)
        step = pl.program_id(0)
        arrivals = [
            [
                pltpu.make_async_copy(x_refs[i], x_now.at[i % 2], x_sems.at[0, i % 2]),
                pltpu.make_async_copy(g_refs[i], g_now.at[i % 2], x_sems.at[1, i % 2]),
            ]
            for i in range(count)
        ]

        @pl.when(step == 0)
        def _():
            for copy in arrivals[0]:
                copy.start()
            for copy in weight_copies(at_ref, pairs, fulls, sems, parts, (0, router_at)):
                copy.start()

        for i in range(count):

            @pl.when(step == i)
            def _(i=i):
                for copy in arrivals[i]:
                    copy.wait()
                if i + 1 < count:
                    for copy in arrivals[i + 1]:
                        copy.start()

        slot = lax.rem(step, 2)
        pre, back, logits = 0.0, 0.0, 0.0
        for k in range(parts):

            @pl.when(step == 0)
            def _(k=k):
                weight_wait(pairs, fulls, sems, parts, k)

            cut = slice(k * part, (k + 1) * part)
            x = x_now[slot, :, cut]
            pre = pre + dot(x, full[cut, high])
            back = back + dot(g_now[slot, :, cut], full[cut, low])
            logits = logits + dot(x, r_ref[cut])
        logits = jnp.where(g_now[slot, :, width:] > 0, logits, NEGATIVE)
        peak = jnp.max(logits, axis=1, keepdims=True)
        powers = jnp.exp(logits - peak)
        gate_probs = powers / jnp.sum(powers, axis=1, keepdims=True)
        spread = s_ref[...]
        one, two = two_parts(gate_probs)
        probs_wide = dot(one, spread) + dot(two, spread)
        gate_pre, up_pre = pre[:, :hidden], pre[:, hidden:]
        sigmoid = 0.5 + 0.5 * jnp.tanh(0.5 * gate_pre)
        swish = gate_pre * sigmoid
        active = swish * up_pre
        weighted_now = (probs_wide * active).astype(BF16)
        weighted[...] = weighted_now
        gate_grad = dot_bt((active * back).astype(BF16), spread)
        logit_low = (
            gate_probs * (gate_grad - jnp.sum(gate_probs * gate_grad, axis=1, keepdims=True))
        ).astype(BF16)
        logit[...] = logit_low
        back = probs_wide * back
        d_high[:, :hidden] = (back * up_pre * (sigmoid + swish * (1.0 - sigmoid))).astype(BF16)
        d_high[:, hidden:] = (back * swish).astype(BF16)
        dx = dot_bt(d_high[...], full[:, high]) + dot_bt(logit_low, r_ref[...])
        total = dot_bt(weighted_now, full[:, low])
        for i, ref in enumerate(dxs):

            @pl.when(step == i)
            def _(i=i, ref=ref):
                ref[...] = dx.astype(BF16)
                n = width // lo_count
                for k, lo in enumerate(los[i * lo_count : (i + 1) * lo_count]):
                    lo[...] = total[:, k * n : (k + 1) * n].astype(BF16)

    def rows(n):
        return pl.BlockSpec((tok, n), lambda i, at_ref: (i, 0))

    outs = [struct((count * tok, n), BF16) for n in (hidden, 2 * hidden, LANES)]
    outs += [struct((tok, width), BF16)] * count
    outs += [struct((tok, width // lo_count), BF16)] * (count * lo_count)
    all_weights = flat_pair(pair) + flat_pair(router)
    ins = (spread, *tokens_in, *grads, *all_weights)
    weighted, d_high, logit, *rest = pl.pallas_call(
        kernel,
        out_shape=outs,
        grid_spec=pltpu.PrefetchScalarGridSpec(
            num_scalar_prefetch=1,
            grid=(count,),
            in_specs=[whole(spread.shape)] + [ANY] * (2 * count + len(all_weights)),
            out_specs=[rows(hidden), rows(2 * hidden), rows(LANES)]
            + [whole(o.shape) for o in outs[3:]],
            scratch_shapes=[
                full_weight(pair),
                full_weight(router, LANES),
                pltpu.VMEM((2, tok, width), BF16),
                pltpu.VMEM((2, tok, grads[0].shape[1]), BF16),
                weight_sems(pair, router),
                pltpu.SemaphoreType.DMA((2, 2)),
            ],
        ),
        compiler_params=params(limit=40 * 1024 * 1024),
        cost_estimate=cost(12 * count * tok * width * hidden, nbytes([*all_weights, *outs])),
        name="run_experts",
    )(at, *ins)
    dx, los = rest[:count], rest[count:]
    if by_part:
        los = [los[i * parts : (i + 1) * parts] for i in range(count)]
    return weighted, d_high, logit, dx, los


def weight_grads(at, place, outer_at, half_at, lefts, rights, parts, blocks, part, add=None, by_device=False, joined=False):
    unit = part * parts // blocks // 2
    stacks = [stack for group in rights for stack in group]
    left_flat = [a if isinstance(a, tuple) else (a, None) for runs in lefts for a in runs]
    if blocks != parts:
        width = part * parts
        totals = []
        for runs, group in zip(lefts, rights):
            runs = [
                lax.dynamic_index_in_dim(a[0], outer_at ^ a[1], 0, keepdims=False)
                if isinstance(a, tuple)
                else a
                for a in runs
            ]
            left = jnp.concatenate([a[:, :width] for a in runs], axis=0)
            left = left.reshape(left.shape[0], parts, 2, -1)[:, :, half_at].reshape(left.shape[0], -1)
            total = jnp.concatenate([dot_at(left, jnp.concatenate(x, axis=0)) for x in group], axis=1)
            total = total.reshape(blocks, unit, -1)
            order = [place ^ j for j in range(blocks)]
            out = jnp.stack([lax.dynamic_index_in_dim(total, i, 0, keepdims=False) for i in order])
            if add is not None and len(add) == 1:
                start = sum(a.shape[2] for a in totals)
                out = out + add[0][:, :, start : start + out.shape[2]].astype(F32)
            elif add is not None:
                out = out + add[len(totals)].astype(F32)
            order = [outer_at ^ j if by_device else j for j in range(blocks)]
            out = [lax.dynamic_index_in_dim(out, i, 0, keepdims=False) for i in order]
            totals.append(jnp.stack(out).astype(BF16))
        return [jnp.concatenate(totals, axis=2)] if joined else totals
    flat = [r for stack in stacks for r in stack]
    tokens = sum(r.shape[0] for r in stacks[0])
    sizes = [sum(stack[0].shape[1] for stack in group) for group in rights]
    n = sum(sizes)
    outs = [struct((blocks, unit, size), BF16) for size in ([n] if joined else sizes)]
    joins = [stack for stack in stacks if len(stack) > 1]
    extra = [] if add is None else add
    counts = [len(runs) for runs in lefts]

    def kernel(at_ref, *refs):
        left_refs, refs = refs[: len(left_flat)], refs[len(left_flat) :]
        right_refs, refs = refs[: len(flat)], refs[len(flat) :]
        added, refs = refs[: len(extra)], refs[len(extra) :]
        out_refs, fulls = refs[: len(outs)], refs[len(outs) :]
        step = pl.program_id(0)
        stacked = []
        for stack in stacks:
            stack_refs, right_refs = right_refs[: len(stack)], right_refs[len(stack) :]
            if len(stack) == 1:
                stacked.append(stack_refs[0])
            else:
                full, fulls = fulls[0], fulls[1:]
                stacked.append(full)

                @pl.when(step == 0)
                def _(full=full, stack_refs=stack_refs):
                    row = 0
                    for ref in stack_refs:
                        full[row : row + ref.shape[0]] = ref[...]
                        row += ref.shape[0]

        column, rest, more = 0, stacked, left_refs
        for i, (count, group) in enumerate(zip(counts, rights)):
            run_refs, more = more[:count], more[count:]
            now, rest = rest[: len(group)], rest[len(group) :]
            left = jnp.concatenate([ref[...].reshape(-1, unit) for ref in run_refs], axis=0).T
            column = column if joined else 0
            own = 0
            for right in now:
                cut = slice(column, column + right.shape[1])
                value = dot(left, right[...])
                if extra:
                    source, start = (added[0], column) if len(extra) == 1 else (added[i], own)
                    value = value + source[0, :, start : start + right.shape[1]].astype(F32)
                out_refs[0 if joined else i][0, :, cut] = value.astype(BF16)
                column, own = cut.stop, own + right.shape[1]

    def left_spec(a, i):
        if a.ndim == 3:
            return pl.BlockSpec(
                (1, a.shape[1], unit),
                lambda j, at_ref: (at_ref[1] ^ i, 0, 2 * (j ^ at_ref[0]) + half_at),
            )
        return pl.BlockSpec((a.shape[0], unit), lambda j, at_ref: (0, 2 * (j ^ at_ref[0]) + half_at))

    ins = (*[a for a, _ in left_flat], *flat, *extra)
    return pl.pallas_call(
        kernel,
        out_shape=outs,
        grid_spec=pltpu.PrefetchScalarGridSpec(
            num_scalar_prefetch=1,
            grid=(blocks,),
            in_specs=[left_spec(a, i) for a, i in left_flat]
            + [whole(a.shape) for a in flat]
            + [pl.BlockSpec((1,) + a.shape[1:], lambda j, at_ref: (j, 0, 0)) for a in extra],
            out_specs=[
                pl.BlockSpec(
                    (1,) + o.shape[1:], lambda j, at_ref: (at_ref[1] ^ j if by_device else j, 0, 0)
                )
                for o in outs
            ],
            scratch_shapes=[
                pltpu.VMEM((sum(a.shape[0] for a in stack), stack[0].shape[1]), BF16)
                for stack in joins
            ],
        ),
        compiler_params=params(limit=40 * 1024 * 1024),
        cost_estimate=cost(2 * tokens * blocks * unit * n, nbytes(ins)),
        name="weight_grads",
    )(at, *ins)


def by_owner(weights, blocks):
    unit, hidden = weights[0].shape[0], weights[0].shape[1] // blocks
    if hidden % LANES:
        return jnp.concatenate(
            [w.reshape(unit, blocks, hidden).transpose(1, 0, 2) for w in weights], axis=2
        )

    def kernel(*refs):
        for i, ref in enumerate(refs[:-1]):
            refs[-1][0, :, i * hidden : (i + 1) * hidden] = ref[...]

    out = struct((blocks, unit, hidden * len(weights)), BF16)
    return pl.pallas_call(
        kernel,
        out_shape=out,
        grid=(blocks,),
        in_specs=[pl.BlockSpec((unit, hidden), lambda i: (0, i)) for _ in weights],
        out_specs=pl.BlockSpec((1,) + out.shape[1:], lambda i: (i, 0, 0)),
        compiler_params=params(),
        cost_estimate=cost(1, 1),
        name="by_owner",
    )(*weights)


def by_columns(grads, hidden):
    blocks, unit, n = grads.shape
    starts = (0, hidden, 2 * hidden + LANES)
    if hidden % LANES:
        return [
            grads[:, :, start : start + hidden]
            .transpose(1, 0, 2)
            .reshape(unit, blocks * hidden)
            .astype(F32)
            for start in starts
        ]

    def kernel(ref, *outs):
        for start, out in zip(starts, outs):
            out[...] = ref[0, :, start : start + hidden].astype(F32)

    outs = [struct((unit, blocks * hidden), F32) for _ in starts]
    return pl.pallas_call(
        kernel,
        out_shape=outs,
        grid=(blocks,),
        in_specs=[pl.BlockSpec((1, unit, n), lambda i: (i, 0, 0))],
        out_specs=[pl.BlockSpec((unit, hidden), lambda i: (0, i)) for _ in starts],
        compiler_params=params(),
        cost_estimate=cost(0, nbytes([grads, *outs])),
        name="by_columns",
    )(grads)


def norm_back(values, pieces, scale, gain, gain_grad, outs, width):
    part = pieces[0].shape[1]
    cuts = [slice(k * part, (k + 1) * part) for k in range(len(pieces))]
    inner = 0.0
    for value, piece, cut in zip(values, pieces, cuts):
        gain_grad[:, cut] = jnp.sum(value * (piece * scale), axis=0, keepdims=True)
        inner = inner + jnp.sum(value * gain[:, cut] * piece, axis=1, keepdims=True)
    inner = inner * (scale * scale * scale / width)
    for value, piece, cut, out in zip(values, pieces, cuts, outs):
        out[...] = (value * gain[:, cut] * scale - piece * inner).astype(out.dtype)


def second_norm_back(received, pieces, gain):
    parts, blocks = len(pieces), len(received)
    tokens, width = received[0].shape
    part = width // parts
    outs = [struct((tokens, part), F32 if k == 0 else BF16) for k in range(parts)]
    outs.append(struct((1, width), F32))

    def kernel(*refs):
        got, refs = refs[:blocks], refs[blocks:]
        ins, (gain_ref, *outs, gain_grad) = refs[:parts], refs[parts:]
        values = []
        for k in range(parts):
            cut = slice(k * part, (k + 1) * part)
            values.append(sum(ref[:, cut].astype(F32) for ref in got))
        pieces = [ref[...].astype(F32) for ref in ins]
        scale = rms_scale(pieces, width)
        norm_back(values, pieces, scale, gain_ref, gain_grad, outs, width)

    ins = (*received, *pieces, gain)
    return pl.pallas_call(
        kernel,
        out_shape=outs,
        in_specs=[whole(a.shape) for a in ins],
        out_specs=[whole(o.shape) for o in outs],
        grid=(1,),
        compiler_params=params(),
        cost_estimate=cost(tokens * width * 20, nbytes(ins)),
        name="second_norm_back",
    )(*ins)


def project_back(
    at, grad_q, grad_kv, pre, pieces, gain, pair, query_gain, key_gain, cosine, sine, heads, kv_heads, gain_grad_two, router, experts
):
    parts, runs, blocks = len(pieces), len(grad_q), len(grad_kv)
    tokens, n = pre.shape
    width = gain.shape[1]
    part = width // parts
    size = query_gain.shape[1]
    gain_lines = -(-(2 * parts + 1) // 16) * 16
    lines = gain_lines + -(-experts // 16) * 16
    router_rows = router.shape[0]
    outs = [struct((tokens, part), F32)] + [struct((tokens + 2 * lines, part), BF16)] * (parts - 1)
    outs += [struct((tokens, n), BF16), struct((lines, part), F32)]

    def kernel(at_ref, pre_ref, two_ref, router_ref, *refs):
        gq, refs = refs[:runs], refs[runs:]
        gkv, refs = refs[:blocks], refs[blocks:]
        ins, refs = refs[:parts], refs[parts:]
        weights, refs = taken(refs, pair)
        gain_ref, qg, kg, cos_ref, sin_ref, *refs = refs
        outs, (d_wide, sums, gain_grad, full, sems) = refs[:parts], refs[parts:]
        for copy in weight_copies(at_ref, [weights], [full], sems, parts):
            copy.start()
        cosine, sine = cos_ref[...], sin_ref[...]
        totals = [jnp.zeros((1, size), F32), jnp.zeros((1, size), F32)]
        for i in range(n // size):
            cut = slice(i * size, (i + 1) * size)
            if i < heads:
                grad = jnp.concatenate([ref[:, cut] for ref in gq], axis=0)
            else:
                kv_cut = slice((i - heads) * size, (i - heads + 1) * size)
                grad = sum(ref[:, kv_cut].astype(F32) for ref in gkv)
            if i < heads + kv_heads:
                which = 0 if i < heads else 1
                gain_row = (qg, kg)[which][...]
                grad = grad * cosine + pltpu.roll(grad * sine, size // 2, 1)
                head = pre_ref[:, cut]
                scale = lax.rsqrt(jnp.mean(head * head, axis=1, keepdims=True) + EPS)
                unit = head * scale
                totals[which] = totals[which] + jnp.sum(grad * unit, axis=0, keepdims=True)
                grad = grad * gain_row
                grad = scale * (grad - unit * jnp.mean(grad * unit, axis=1, keepdims=True))
            d_wide[:, cut] = grad.astype(BF16)
        weight_wait([weights], [full], sems, parts)
        values = [
            dot_bt(d_wide[...], full[k * part : (k + 1) * part]) for k in range(parts)
        ]
        pieces = [ref[...].astype(F32) for ref in ins]
        scale = rms_scale(pieces, width)
        cut_outs = [outs[0]] + [out.at[:tokens] for out in outs[1:]]
        norm_back(values, pieces, scale, gain_ref, gain_grad, cut_outs, width)
        sums[...] = jnp.zeros_like(sums)
        for i, ref in enumerate((gain_grad, two_ref)):
            for k in range(parts):
                sums[i * parts + k : i * parts + k + 1] = ref[:, k * part : (k + 1) * part]
        for i, total in enumerate(totals):
            sums[2 * parts : 2 * parts + 1, i * size : (i + 1) * size] = total
        sums[gain_lines : gain_lines + experts, :router_rows] = router_ref[...].T[:experts]
        for out in outs[1:]:
            one, two = two_parts(sums[...])
            out[tokens : tokens + lines] = one
            out[tokens + lines :] = two

    ins = (pre, gain_grad_two, router, *grad_q, *grad_kv, *pieces, *flat_pair(pair))
    ins = (*ins, gain, query_gain, key_gain, cosine, sine)
    return pl.pallas_call(
        kernel,
        out_shape=outs,
        in_specs=[SMEM]
        + [whole(a.shape) for a in (pre, gain_grad_two, router, *grad_q, *grad_kv)]
        + [whole((tokens, part)) for _ in pieces]
        + [ANY] * len(flat_pair(pair))
        + [whole(a.shape) for a in (gain, query_gain, key_gain, cosine, sine)],
        out_specs=[whole(o.shape) for o in outs],
        scratch_shapes=[pltpu.VMEM((1, width), F32), full_weight(pair), weight_sems(pair)],
        grid=(1,),
        compiler_params=params(),
        cost_estimate=cost(2 * tokens * width * n, nbytes(ins)),
        name="project_back",
    )(at, *ins)


def sum_blocks(grads, widths, first=0):
    blocks = len(grads)
    unit = grads[0].shape[-2]

    def kernel(*refs):
        ins, outs = refs[:blocks], refs[blocks:]
        start = first
        for out in outs:
            cut = slice(start, start + out.shape[1])
            parts = [ref[:, cut] if len(ref.shape) == 2 else ref[0, :, cut] for ref in ins]
            out[...] = sum(a.astype(F32) for a in parts)
            start = cut.stop

    def spec(i, a):
        if a.ndim == 2:
            return whole(a.shape)
        return pl.BlockSpec((1,) + a.shape[1:], lambda _: (i, 0, 0))

    outs = [struct((unit, width), F32) for width in widths]
    return pl.pallas_call(
        kernel,
        out_shape=outs,
        grid=(1,),
        in_specs=[spec(i, a) for i, a in enumerate(grads)],
        out_specs=[whole(o.shape) for o in outs],
        compiler_params=params(),
        cost_estimate=cost(1, 1),
        name="sum_blocks",
    )(*grads)


def finish(at, residual, own, arrived, own_sums, low, unit_rows, experts):
    others = len(arrived)
    tokens, part = own.shape
    parts, half = others + 1, part // 2
    unit = half // low
    lines = own_sums.shape[0]
    gain_lines = -(-(2 * parts + 1) // 16) * 16

    def kernel(at_ref, residual, own, *refs):
        arrived, refs = refs[:others], refs[others:]
        own_sums, out, sums, router = refs
        even, col = at_ref[3] == 0, at_ref[4]

        def put(ref, rows, value):
            first = jnp.where(even, value[:, :half], value[:, half:])
            second = jnp.where(even, value[:, half:], value[:, :half])
            for i in range(low):
                cut = slice(i * unit, (i + 1) * unit)
                ref[rows, 2 * i * unit : (2 * i + 1) * unit] = first[:, cut].astype(ref.dtype)
                ref[rows, (2 * i + 1) * unit : (2 * i + 2) * unit] = second[:, cut].astype(ref.dtype)

        value = residual[...] + own[...]
        for ref in arrived:
            value = value + ref[:tokens].astype(F32)
        put(out, slice(0, tokens), value)
        got = [ref[tokens : tokens + lines].astype(F32) for ref in arrived]
        got = [a + ref[tokens + lines :].astype(F32) for a, ref in zip(got, arrived)]
        total = own_sums[...]
        for a in got:
            total = total + a
        sums[...] = total[:gain_lines]
        router[...] = total[gain_lines : gain_lines + experts, :unit_rows].T
        for i in range(2):
            for k in range(parts):
                line = own_sums[i * parts + k : i * parts + k + 1]
                for mask, a in enumerate(got, 1):
                    row = i * parts + (k ^ mask)
                    line = line + a[row : row + 1]
                for to in range(parts):

                    @pl.when(col ^ k == to)
                    def _(i=i, to=to, line=line):
                        put(sums, slice(i * parts + to, i * parts + to + 1), line)

    outs = (
        struct((tokens, part), BF16),
        struct((gain_lines, part), F32),
        struct((unit_rows, experts), F32),
    )
    ins = (residual, own, *arrived, own_sums)
    return pl.pallas_call(
        kernel,
        out_shape=outs,
        grid=(1,),
        in_specs=[SMEM] + [whole(a.shape) for a in ins],
        out_specs=[whole(o.shape) for o in outs],
        compiler_params=params(),
        cost_estimate=cost(1, 1),
        name="finish",
    )(at, *ins)


def per_device(
    layer_in,
    out_grad,
    lengths,
    token_order,
    choices,
    norm_gain,
    w_query,
    w_key,
    w_value,
    query_gain,
    key_gain,
    w_out,
    ffn_gain,
    w_router,
    w_gate,
    w_up,
    w_down,
):
    micro, tok, part = layer_in.shape
    outer, cols = lax.axis_size("outer"), lax.axis_size("col")
    rows = 2 * outer
    tokens = micro * tok
    width = part * cols
    outer_at, core_at, col_at = (lax.axis_index(name) for name in ("outer", "core", "col"))
    row_at = outer_at * 2 + core_at
    low = outer // cols
    unit = width // rows
    half = part // 2
    size = query_gain.shape[0]
    heads = w_query.shape[1] // size
    kv_heads = w_key.shape[1] // size
    experts = w_router.shape[1]
    hidden = w_gate.shape[1] // outer
    repeats = hidden // experts

    place = outer_at ^ (col_at * low)
    at = jnp.stack([place, outer_at, col_at * low, core_at, col_at]).astype(jnp.int32)

    def core_swap(a):
        return lax.ppermute(a, "core", [(0, 1), (1, 0)])

    def col_swap(a, mask):
        return lax.ppermute(a, "col", [(i, i ^ mask) for i in range(cols)])

    def exchange(a):
        return lax.all_to_all(a, "outer", 0, 0, tiled=True)

    def for_all(a):
        return jnp.broadcast_to(a[None], (outer,) + a.shape)

    def after(a, b):
        return lax.optimization_barrier((a, b))[0]

    def to_halves(a):
        blocks = a.reshape(a.shape[:-1] + (low, 2, unit))
        first = blocks[..., 0, :].reshape(a.shape[:-1] + (half,))
        second = blocks[..., 1, :].reshape(a.shape[:-1] + (half,))
        even = core_at == 0
        return jnp.concatenate(
            [jnp.where(even, first, second), jnp.where(even, second, first)], axis=-1
        )

    def from_halves(a):
        even = core_at == 0
        first = jnp.where(even, a[..., :half], a[..., half:]).reshape(a.shape[:-1] + (low, unit))
        second = jnp.where(even, a[..., half:], a[..., :half]).reshape(a.shape[:-1] + (low, unit))
        return jnp.stack([first, second], axis=-2).reshape(a.shape)

    def col_gather(a):
        return [a] + [col_swap(a, k) for k in range(1, cols)]

    def col_total(pieces):
        total = pieces[0]
        for k in range(1, cols):
            total = total + col_swap(pieces[k], k).astype(F32)
        return total

    def swap(a, mask):
        return lax.ppermute(a, "outer", [(i, i ^ mask) for i in range(outer)])

    def gather(a):
        return [a] + [swap(a, j) for j in range(1, outer)]

    def scatter(blocks):
        return [blocks[0]] + [swap(blocks[j], j) for j in range(1, outer)]

    def swap(a, mask):
        return lax.ppermute(a, "outer", [(i, i ^ mask) for i in range(outer)])

    def gather(a):
        return [a] + [swap(a, j) for j in range(1, outer)]

    def scatter(blocks):
        return [blocks[0]] + [swap(blocks[j], j) for j in range(1, outer)]

    def both(*arrays):
        return lax.optimization_barrier(arrays)

    def both_cores(a):
        return a, [core_swap(b) for b in a] if isinstance(a, list) else core_swap(a)

    own_in = to_halves(layer_in).reshape(tokens, part)
    own_grad = to_halves(out_grad).reshape(tokens, part)
    w_in = gather(jnp.concatenate([w_query, w_key, w_value], axis=1))
    arrived = col_gather(own_in)
    w_back = jnp.concatenate([w_out, jnp.pad(w_router, ((0, 0), (0, LANES - experts)))], axis=1)
    w_back = for_all(w_back)
    weights = by_owner([w_gate, w_up, w_down], outer)
    q_gain, k_gain = query_gain[None, :], key_gain[None, :]
    frequency = jnp.exp(jnp.arange(size // 2, dtype=F32) * (-2.0 * math.log(THETA) / size))
    bias, angles, chosen, spread, gain_one, gain_two = prepare(
        at,
        lengths,
        token_order.reshape(micro, rows, tok),
        choices.reshape(tokens, -1),
        jnp.concatenate([frequency, frequency])[None, :],
        jnp.stack([norm_gain, ffn_gain]).reshape(2, cols, part),
        low,
        hidden,
        experts,
    )
    cosine = jnp.cos(angles)
    sine = jnp.sin(angles) * jnp.where(jnp.arange(size) < size // 2, -1.0, 1.0)

    w_back, weights, bias = both(w_back, weights, bias)
    w_back = exchange(w_back)
    w_in, arrived, weights, chosen, bias, cosine, sine, gain_one, gain_two, spread = both(
        w_in, arrived, weights, chosen, bias, cosine, sine, gain_one, gain_two, spread
    )
    own_grads = col_gather(after(own_grad, w_in))
    w_in = both_cores(w_in)
    normed_one, pre, ready, kv = project(
        at, arrived, part, gain_one, w_in, q_gain, k_gain, cosine, sine, heads, kv_heads
    )
    near = [j for j in range(1, outer) if not j & (j - 1)]
    far = [j for j in range(1, outer) if j & (j - 1)]
    far_grads, _ = both(jnp.concatenate([own_grad, chosen], axis=1), w_in[0])
    far_grads = [swap(far_grads, j) for j in far]
    kv_own = jnp.stack(gather(kv))
    kv_own, w_back, far_grads = both(kv_own, w_back, far_grads)
    weights = exchange(after(weights, w_back))
    kv_other = core_swap(kv_own)
    w_back = both_cores(w_back)
    attended, lse = attend(ready, kv_own, kv_other, bias, heads, kv_heads, size)
    attn_parts = expand(at, attended, w_back, part, cols)
    attn_parts, own_grads = both(attn_parts, own_grads)

    grads = [jnp.concatenate(own_grads + [chosen], axis=1)] + [None] * (outer - 1)
    near_grads = [swap(grads[0], j) for j in near]

    residual = own_in.astype(F32) + col_total(attn_parts)
    residual, weights = both(residual, weights)
    full_res = col_gather(residual.astype(BF16))
    full_res, near_grads, weights = both(full_res, near_grads, weights)
    for j, a in zip(near, near_grads):
        grads[j] = a
    weights = both_cores(weights)
    normed_two = second_norm(full_res, gain_two)
    expert_in = gather(normed_two)
    far_grads, _ = both(far_grads, normed_two)
    for j, a in zip(far, far_grads):
        grads[j] = jnp.concatenate(col_gather(a[:, :part]) + [a[:, part:]], axis=1)

    results, dx, lo_far = [], [None] * outer, []
    order = [0] + far + near
    for group in [[0]] + [far[i : i + 4] for i in range(0, len(far), 4)] + [near]:
        *result, dx_now, lo_now = run_experts(
            at,
            [expert_in[j] for j in group],
            [grads[j] for j in group],
            spread,
            weights,
            w_back,
            heads * size,
            cols,
            group[0] in far,
        )
        for j, a in zip(group, dx_now):
            dx[j] = a
        if group == [0]:
            lo_own = lo_now[0]
            expert_in, lo_own = both(expert_in, lo_own)
        elif group != near:
            lo_far += lo_now
            for j in group:
                dx[j] = swap(dx[j], j)
        else:
            lo_near = lo_now
        results.append(result)
    far_dx, results[-1], lo_far = both([dx[j] for j in far], results[-1], lo_far)
    lo_far = [col_total([a[0].astype(F32), *a[1:]]).astype(BF16) for a in lo_far]
    weighted, d_high, logit_low = [list(arrays) for arrays in zip(*results)]
    near_dx, far_dx = both([dx[j] for j in near], far_dx)
    for j, a in zip(near, near_dx):
        dx[j] = swap(a, j)
    sizes = (cols, outer, part)
    expert_sides = (
        [[expert_in[j] for j in order], [grads[j] for j in order]],
        [[d_high, logit_low], [weighted]],
    )
    (other,) = weight_grads(at, place, outer_at, 1, *expert_sides, *sizes, joined=True)
    other, near_dx, lo_far, lo_near = both(other, [dx[j] for j in near], lo_far, lo_near)
    other = core_swap(other)
    *spread_two, gain_grad_two = second_norm_back([dx[0]] + near_dx + far_dx, full_res, gain_two)
    lo_near = [swap(a, j) for j, a in zip(near, lo_near)]
    (expert_grads,) = weight_grads(
        at, place, outer_at, 0, *expert_sides, *sizes, [other], True, True
    )
    spread_two[0], expert_grads = both(spread_two[0], expert_grads)
    grad_residual = own_grad.astype(F32) + col_total(spread_two)
    grad_residual, lo_near, expert_grads = both(grad_residual, lo_near, expert_grads)
    expert_grads = exchange(expert_grads)
    grad_feats = col_gather(grad_residual.astype(BF16))

    lo_near = lo_own.astype(F32) + sum(a.astype(F32) for a in lo_near)
    lo_near = [
        lo_near[:, k * part : (k + 1) * part].astype(F32 if k == 0 else BF16) for k in range(cols)
    ]
    grad_feats, lo_near = both(grad_feats, lo_near)
    back_attended, feats = contract(at, grad_feats, w_back, heads * size)
    lo_near = col_total(after(lo_near, back_attended))
    grad_q, kv_mine, kv_theirs = attend_back(
        ready, kv_own, kv_other, bias, lse, back_attended, heads, kv_heads, size
    )
    kv_theirs, expert_grads = both(kv_theirs, expert_grads)
    kv_sums = sum_cores(kv_mine, core_swap(kv_theirs))
    grad_kv = scatter(kv_sums)
    router_part = jnp.sum(
        expert_grads[:, :, 2 * hidden : 2 * hidden + LANES].astype(F32), axis=0
    )
    feats, lo_near, _ = both(feats, lo_near, grad_q)
    (other,) = weight_grads(at, place, outer_at, 1, [[feats]], [[[attended]]], *sizes)
    (out_grads,) = weight_grads(
        at, place, outer_at, 0, [[feats]], [[[attended]]], *sizes, [core_swap(other)], True
    )
    grad_kv, out_grads, lo_far = both(grad_kv, out_grads, lo_far)
    lo_far = [swap(a, j) for j, a in zip(far, lo_far)]
    out_grads = exchange(out_grads)
    *spread_one, d_wide, sums = project_back(
        at,
        [grad_q],
        grad_kv,
        pre,
        arrived,
        gain_one,
        w_in,
        q_gain,
        k_gain,
        cosine,
        sine,
        heads,
        kv_heads,
        gain_grad_two,
        router_part,
        experts,
    )
    (other,) = weight_grads(at, place, outer_at, 1, [[normed_one]], [[[d_wide]]], *sizes)
    other, expert_grads, lo_far = both(other, expert_grads, lo_far)
    grad_gate_w, grad_up_w, grad_down_w = by_columns(expert_grads, hidden)
    other = jnp.stack([core_swap(other[j]) for j in range(outer)])
    other, grad_gate_w, out_grads = both(other, grad_gate_w, out_grads)
    (wide_grads,) = weight_grads(
        at, place, outer_at, 0, [[normed_one]], [[[d_wide]]], *sizes, [other], True
    )
    spread_one, wide_grads = both(spread_one, wide_grads)
    wide_grads = exchange(wide_grads)

    got = [col_swap(spread_one[k], k) for k in range(1, cols)]
    layer_out = residual + lo_near + sum(a.astype(F32) for a in lo_far)
    layer_out = from_halves(layer_out.astype(BF16)).reshape(micro, tok, part)
    input_grad, sums, grad_router = finish(
        at, grad_residual, spread_one[0], got, sums, low, unit, experts
    )
    input_grad = input_grad.reshape(micro, tok, part)
    sums = sums + core_swap(sums)
    sums = sum(gather(sums))
    (grad_out_w,) = sum_blocks([out_grads] * outer, [heads * size])
    head_sums = sums[2 * cols, : 2 * size]
    gain_sums = (
        sums[:cols].reshape(width),
        sums[cols : 2 * cols].reshape(width),
        head_sums[:size],
        head_sums[size:],
    )
    wide_grads, input_grad, layer_out, grad_out_w, gain_sums, grad_router = both(
        wide_grads, input_grad, layer_out, grad_out_w, gain_sums, grad_router
    )
    grad_norm_gain, grad_ffn_gain, grad_query_gain, grad_key_gain = gain_sums
    grad_query_w, grad_key_w, grad_value_w = sum_blocks(
        [wide_grads] * outer, [w.shape[1] for w in (w_query, w_key, w_value)]
    )
    return (
        layer_out,
        input_grad,
        grad_norm_gain,
        grad_query_w,
        grad_key_w,
        grad_value_w,
        grad_query_gain,
        grad_key_gain,
        grad_out_w,
        grad_ffn_gain,
        grad_router,
        grad_gate_w,
        grad_up_w,
        grad_down_w,
    )


def solution(mesh):
    rows, cols = mesh.devices.shape
    split = Mesh(mesh.devices.reshape(rows // 2, 2, cols), ("outer", "core", "col"))
    tokens_placed = P(None, ROW, "col")
    weight_placed = P(ROW, "col")
    return jax.shard_map(
        per_device,
        mesh=split,
        in_specs=(
            tokens_placed,
            tokens_placed,
            P(),
            P(),
            P(None, ROW, None),
            P(),
            weight_placed,
            weight_placed,
            weight_placed,
            P(),
            P(),
            weight_placed,
            P(),
            P(ROW, None),
            weight_placed,
            weight_placed,
            weight_placed,
        ),
        out_specs=(
            tokens_placed,
            tokens_placed,
            P(),
            weight_placed,
            weight_placed,
            weight_placed,
            P(),
            P(),
            weight_placed,
            P(),
            P(ROW, None),
            weight_placed,
            weight_placed,
            weight_placed,
        ),
        check_vma=False,
    )
```

```python
import functools
import math

import jax
import jax.numpy as jnp
from jax import lax
from jax.experimental import pallas as pl
from jax.experimental.pallas import tpu as pltpu
from jax.sharding import Mesh
from jax.sharding import PartitionSpec as P

EPS = 1e-06
THETA = 1000000.0
NEGATIVE = -1e30
F32 = jnp.float32
BF16 = jnp.bfloat16
VMEM_BYTES = 56 * 1024 * 1024
LANES = 128
ROW = ("outer", "core")


def dot(a, b):
    return jnp.dot(a, b, preferred_element_type=F32)


def dot_bt(a, b):
    return lax.dot_general(a, b, (((1,), (1,)), ((), ())), preferred_element_type=F32)


def dot_at(a, b):
    return lax.dot_general(a, b, (((0,), (0,)), ((), ())), preferred_element_type=F32)


def two_parts(a):
    high = a.astype(BF16)
    return high, (a - high.astype(F32)).astype(BF16)


ANY = pl.BlockSpec(memory_space=pl.ANY)
SMEM = pl.BlockSpec(memory_space=pltpu.SMEM)


def whole(shape):
    return pl.BlockSpec(shape, lambda *_: (0,) * len(shape))


def params(steps=1, limit=VMEM_BYTES):
    return pltpu.CompilerParams(
        dimension_semantics=("arbitrary",) * steps, vmem_limit_bytes=limit
    )


def cost(flops, moved):
    return pl.CostEstimate(flops=int(flops) // 64, bytes_accessed=int(moved) // 64, transcendentals=0)


def nbytes(arrays):
    return sum(math.prod(a.shape) * a.dtype.itemsize for a in arrays)


def struct(shape, dtype):
    return jax.ShapeDtypeStruct(shape, dtype)


def block_count(pair):
    return len(pair[0]) if isinstance(pair[0], list) else pair[0].shape[0]


def weight_copies(at_ref, pairs, fulls, sems, parts, firsts=None):
    copies, base = [], 0
    for i, (pair, full) in enumerate(zip(pairs, fulls)):
        first = firsts[i] if firsts else 0
        blocks = block_count(pair)
        low = blocks // parts
        unit = full.shape[0] // blocks // 2
        for h, sources in enumerate(pair):
            listed = isinstance(sources, list)
            for j in range(blocks):
                to = at_ref[0 if listed else 2] ^ j
                source = sources[j] if listed else sources.at[j]
                row = (2 * (to // low) + h) * (low * unit) + lax.rem(to, low) * unit
                copies.append(
                    pltpu.make_async_copy(
                        source.at[:, pl.ds(first, full.shape[1])],
                        full.at[pl.ds(pl.multiple_of(row, unit), unit)],
                        sems.at[base + h * blocks + to],
                    )
                )
        base += 2 * blocks
    return copies


def weight_wait(pairs, fulls, sems, parts, part=None):
    base = 0
    for pair, full in zip(pairs, fulls):
        blocks = block_count(pair)
        low = blocks // parts
        unit = full.shape[0] // blocks // 2
        for h in range(2):
            for to in range(blocks):
                if part is None or to // low == part:
                    row = (2 * (to // low) + h) * (low * unit) + to % low * unit
                    source = pair[h][0] if isinstance(pair[h], list) else pair[h].at[0]
                    pltpu.make_async_copy(
                        source.at[:, pl.ds(0, full.shape[1])],
                        full.at[pl.ds(row, unit)],
                        sems.at[base + h * blocks + to],
                    ).wait()
        base += 2 * blocks


def full_weight(pair, n=None):
    unit, width = (pair[0][0] if isinstance(pair[0], list) else pair[0]).shape[-2:]
    return pltpu.VMEM((2 * block_count(pair) * unit, n or width), BF16)


def weight_sems(*pairs):
    return pltpu.SemaphoreType.DMA((sum(2 * block_count(pair) for pair in pairs),))


def flat_pair(pair):
    return [a for half in pair for a in (half if isinstance(half, list) else [half])]


def taken(refs, pair):
    halves = []
    for half in pair:
        if isinstance(half, list):
            halves.append(list(refs[: len(half)]))
            refs = refs[len(half) :]
        else:
            halves.append(refs[0])
            refs = refs[1:]
    return tuple(halves), refs


def rms_scale(pieces, width):
    total = sum(jnp.sum(piece * piece, axis=1, keepdims=True) for piece in pieces)
    return lax.rsqrt(total / width + EPS)


def prepare(at, lengths, order, choices, frequency, gains, low, hidden, experts):
    micro, rows, tok = order.shape
    tokens, top = choices.shape
    _, cols, part = gains.shape
    unit = part // 2 // low
    outer, seqs, size = rows // 2, lengths.shape[1], frequency.shape[1]

    def kernel(at_ref, len_ref, order_ref, choice_ref, freq_ref, gain_ref, bias, angles, chosen, spread, *ordered):
        outer_at, core, col = at_ref[1], at_ref[3], at_ref[4]
        for b in range(micro):

            def seq_of(value):
                seq, start, end = jnp.zeros_like(value), jnp.zeros_like(value), 0
                for i in range(seqs):
                    end = end + len_ref[b, i]
                    passed = value >= end
                    seq = seq + jnp.where(passed, 1, 0)
                    start = start + jnp.where(passed, len_ref[b, i], 0)
                return seq, start

            def row(at):
                return order_ref[b, pl.ds(at, 1), :]

            own = row(2 * outer_at + core)
            own_seq, own_start = seq_of(own)
            keys = jnp.concatenate(
                [row(2 * (outer_at ^ j) + (core ^ h)) for h in range(2) for j in range(outer)], axis=0
            )
            key_seq, _ = seq_of(keys)
            lines = [keys, key_seq, own - own_start]
            lines.append(jnp.zeros((tok - 2 * rows - 1, tok), jnp.int32))
            turned = jnp.concatenate(lines, axis=0).astype(F32).T
            own, own_seq = own.astype(F32), own_seq.astype(F32)
            for i in range(rows):
                allowed = (turned[:, rows + i : rows + i + 1] == own_seq) & (
                    turned[:, i : i + 1] <= own
                )
                bias[b, i * tok : (i + 1) * tok] = jnp.where(allowed, 0.0, NEGATIVE)
            angles[b * tok : (b + 1) * tok] = turned[:, 2 * rows : 2 * rows + 1] * freq_ref[...]
        lanes = lax.broadcasted_iota(jnp.int32, (tokens, LANES), 1)
        hits = jnp.zeros((tokens, LANES), F32)
        for i in range(top):
            hits = hits + jnp.where(choice_ref[:, i : i + 1] == lanes, 1.0, 0.0)
        chosen[...] = hits.astype(BF16)
        units = lax.broadcasted_iota(jnp.int32, (LANES, hidden), 1)
        owners = lax.broadcasted_iota(jnp.int32, (LANES, hidden), 0)
        spread[...] = jnp.where(lax.rem(units, experts) == owners, 1.0, 0.0).astype(BF16)
        for i, out in enumerate(ordered):
            for k in range(cols):
                line = gain_ref[i, pl.ds(col ^ k, 1), :]
                for n in range(low):
                    first = line[:, 2 * n * unit : (2 * n + 1) * unit]
                    second = line[:, (2 * n + 1) * unit : (2 * n + 2) * unit]
                    start = k * part + n * unit
                    out[:, start : start + unit] = jnp.where(core == 0, first, second)
                    start = start + part // 2
                    out[:, start : start + unit] = jnp.where(core == 0, second, first)

    outs = (
        struct((micro, rows * tok, tok), F32),
        struct((tokens, size), F32),
        struct((tokens, LANES), BF16),
        struct((LANES, hidden), BF16),
        struct((1, cols * part), F32),
        struct((1, cols * part), F32),
    )
    ins = (order, choices, frequency, gains)
    return pl.pallas_call(
        kernel,
        out_shape=outs,
        grid=(1,),
        in_specs=[SMEM, SMEM] + [whole(a.shape) for a in ins],
        out_specs=[whole(o.shape) for o in outs],
        compiler_params=params(),
        cost_estimate=cost(1, 1),
        name="prepare",
    )(at, lengths, *ins)


def project(at, pieces, part, gain, pair, query_gain, key_gain, cosine, sine, heads, kv_heads):
    parts = len(pieces)
    tokens = cosine.shape[0]
    width = parts * part
    n = flat_pair(pair)[0].shape[-1]
    size = query_gain.shape[1]

    def kernel(at_ref, *refs):
        ins, refs = refs[:parts], refs[parts:]
        weights, refs = taken(refs, pair)
        gain_ref, qg, kg, cos_ref, sin_ref, normed, pre, ready, kv, full, sems = refs
        for copy in weight_copies(at_ref, [weights], [full], sems, parts):
            copy.start()
        values = [ref[...].astype(F32) for ref in ins]
        scale = rms_scale(values, width)
        for k, value in enumerate(values):
            cut = slice(k * part, (k + 1) * part)
            normed[:, cut] = (value * scale * gain_ref[:, cut]).astype(BF16)
        weight_wait([weights], [full], sems, parts)
        pre[...] = dot(normed[...], full[...])
        cosine, sine = cos_ref[...], sin_ref[...]
        for i in range(n // size):
            cut = slice(i * size, (i + 1) * size)
            head = pre[:, cut]
            if i < heads + kv_heads:
                head_gain = qg[...] if i < heads else kg[...]
                head = (
                    head
                    * lax.rsqrt(jnp.mean(head * head, axis=1, keepdims=True) + EPS)
                    * head_gain
                )
                head = head * cosine + pltpu.roll(head, size // 2, 1) * sine
            if i < heads:
                ready[:, cut] = head.astype(BF16)
            else:
                kv[:, (i - heads) * size : (i - heads + 1) * size] = head.astype(BF16)

    outs = (
        struct((tokens, width), BF16),
        struct((tokens, n), F32),
        struct((tokens, heads * size), BF16),
        struct((tokens, n - heads * size), BF16),
    )
    ins = (*pieces, *flat_pair(pair), gain, query_gain, key_gain, cosine, sine)
    return pl.pallas_call(
        kernel,
        out_shape=outs,
        in_specs=[SMEM]
        + [whole((tokens, part)) for _ in pieces]
        + [ANY] * len(flat_pair(pair))
        + [whole(a.shape) for a in (gain, query_gain, key_gain, cosine, sine)],
        out_specs=[whole(o.shape) for o in outs],
        scratch_shapes=[full_weight(pair), weight_sems(pair)],
        grid=(1,),
        compiler_params=params(),
        cost_estimate=cost(4.5e11, 1),
        name="project",
    )(at, *ins)


def attend(ready, own, other, bias, heads, kv_heads, size):
    micro, keys, tok = bias.shape
    group = heads // kv_heads
    outer = own.shape[0]
    scale = 1.0 / math.sqrt(size)

    def kernel(q_ref, own_ref, other_ref, bias_ref, out_ref, lse_ref):
        for h in range(heads):
            key, value = (
                jnp.concatenate(
                    [
                        ref[:, :, i * size : (i + 1) * size].reshape(outer * tok, size)
                        for ref in (own_ref, other_ref)
                    ],
                    axis=0,
                )
                for i in (h // group, kv_heads + h // group)
            )
            cut = slice(h * size, (h + 1) * size)
            scores = dot_bt(key, q_ref[:, cut]) * scale + bias_ref[0]
            peak = jnp.max(scores, axis=0, keepdims=True)
            powers = jnp.exp(scores - peak)
            total = jnp.sum(powers, axis=0, keepdims=True)
            probs = (powers * (1.0 / total)).astype(BF16)
            out_ref[:, cut] = dot_at(probs, value).astype(BF16)
            lse_ref[0, h] = peak + jnp.log(total)

    kv_spec = pl.BlockSpec((outer, tok, own.shape[2]), lambda m: (0, m, 0))
    head_spec = pl.BlockSpec((tok, heads * size), lambda m: (m, 0))
    outs = (struct((micro * tok, heads * size), BF16), struct((micro, heads, 1, tok), F32))
    return pl.pallas_call(
        kernel,
        out_shape=outs,
        grid=(micro,),
        in_specs=[
            head_spec,
            kv_spec,
            kv_spec,
            pl.BlockSpec((1, keys, tok), lambda m: (m, 0, 0)),
        ],
        out_specs=[head_spec, pl.BlockSpec((1, heads, 1, tok), lambda m: (m, 0, 0, 0))],
        compiler_params=params(limit=40 * 1024 * 1024),
        cost_estimate=cost(4 * micro * heads * keys * tok * size, nbytes((own, other, bias))),
        name="attend",
    )(ready, own, other, bias)


def attend_back(ready, own, other, bias, lse, grad, heads, kv_heads, size):
    micro, keys, tok = bias.shape
    group = heads // kv_heads
    outer = own.shape[0]
    scale = 1.0 / math.sqrt(size)
    mid = keys // 2

    def kernel(q_ref, own_ref, other_ref, bias_ref, lse_ref, g_ref, gq, mine, theirs, gk, gv):
        for h in range(heads):
            key, value = (
                jnp.concatenate(
                    [
                        ref[:, :, i * size : (i + 1) * size].reshape(outer * tok, size)
                        for ref in (own_ref, other_ref)
                    ],
                    axis=0,
                )
                for i in (h // group, kv_heads + h // group)
            )
            cut = slice(h * size, (h + 1) * size)
            query, out_grad = q_ref[:, cut], g_ref[:, cut]
            scores = dot_bt(key, query) * scale + bias_ref[0]
            probs = jnp.exp(scores - lse_ref[0, h])
            back = dot_bt(value, out_grad)
            centre = jnp.sum(probs * back, axis=0, keepdims=True)
            slope = (probs * (back - centre)).astype(BF16)
            gq[:, cut] = dot_at(slope, key) * scale
            key_part = dot(slope, query) * scale
            value_part = dot(probs.astype(BF16), out_grad)
            if h % group == 0:
                gk[...] = key_part
                gv[...] = value_part
            else:
                gk[...] += key_part
                gv[...] += value_part
            if h % group == group - 1:
                for i, ref in enumerate((gk, gv)):
                    at = (i * kv_heads + h // group) * size
                    cut = slice(at, at + size)
                    mine[:, :, cut] = ref[:mid].reshape(outer, tok, size)
                    theirs[:, :, cut] = ref[mid:].reshape(outer, tok, size).astype(BF16)

    kv_spec = pl.BlockSpec((outer, tok, own.shape[2]), lambda m: (0, m, 0))
    head_spec = pl.BlockSpec((tok, heads * size), lambda m: (m, 0))
    kv_shape = (outer, micro * tok, 2 * kv_heads * size)
    outs = (
        struct((micro * tok, heads * size), F32),
        struct(kv_shape, F32),
        struct(kv_shape, BF16),
    )
    return pl.pallas_call(
        kernel,
        out_shape=outs,
        grid=(micro,),
        in_specs=[
            head_spec,
            kv_spec,
            kv_spec,
            pl.BlockSpec((1, keys, tok), lambda m: (m, 0, 0)),
            pl.BlockSpec((1, heads, 1, tok), lambda m: (m, 0, 0, 0)),
            head_spec,
        ],
        out_specs=[head_spec, kv_spec, kv_spec],
        scratch_shapes=[pltpu.VMEM((keys, size), F32)] * 2,
        compiler_params=params(),
        cost_estimate=cost(10 * micro * heads * keys * tok * size, nbytes((own, other, bias))),
        name="attend_back",
    )(ready, own, other, bias, lse, grad)


def sum_cores(mine, theirs):
    outer, tokens, n = mine.shape

    def kernel(mine, theirs, *outs):
        for j, out in enumerate(outs):
            out[...] = (mine[j] + theirs[j].astype(F32)).astype(BF16)

    outs = [struct((tokens, n), BF16)] * outer
    return pl.pallas_call(
        kernel,
        out_shape=outs,
        grid=(1,),
        in_specs=[whole(mine.shape)] * 2,
        out_specs=[whole(o.shape) for o in outs],
        compiler_params=params(limit=24 * 1024 * 1024),
        cost_estimate=cost(1, 1),
        name="sum_cores",
    )(mine, theirs)


def expand(at, a, pair, part, parts):
    tokens, n = a.shape
    outs = [struct((tokens, part), F32 if k == 0 else BF16) for k in range(parts)]

    def kernel(at_ref, a_ref, *refs):
        weights, refs = taken(refs, pair)
        outs, (full, sems) = refs[:parts], refs[parts:]
        for copy in weight_copies(at_ref, [weights], [full], sems, parts):
            copy.start()
        for k, out in enumerate(outs):
            weight_wait([weights], [full], sems, parts, k)
            out[...] = dot_bt(a_ref[...], full[k * part : (k + 1) * part]).astype(out.dtype)

    ins = (a, *flat_pair(pair))
    return pl.pallas_call(
        kernel,
        out_shape=outs,
        in_specs=[SMEM, whole(a.shape)] + [ANY] * len(flat_pair(pair)),
        out_specs=[whole(o.shape) for o in outs],
        scratch_shapes=[full_weight(pair, n), weight_sems(pair)],
        grid=(1,),
        compiler_params=params(limit=40 * 1024 * 1024),
        cost_estimate=cost(2 * tokens * n * part * parts, nbytes(ins)),
        name="expand",
    )(at, *ins)


def contract(at, pieces, pair, n):
    parts = len(pieces)
    tokens, part = pieces[0].shape
    outs = (struct((tokens, n), BF16), struct((tokens, part * parts), BF16))

    def kernel(at_ref, *refs):
        ins, refs = refs[:parts], refs[parts:]
        weights, (out, joined, full, sems) = taken(refs, pair)
        for copy in weight_copies(at_ref, [weights], [full], sems, parts):
            copy.start()
        total = 0.0
        for k, ref in enumerate(ins):
            weight_wait([weights], [full], sems, parts, k)
            joined[:, k * part : (k + 1) * part] = ref[...]
            total = total + dot(ref[...], full[k * part : (k + 1) * part])
        out[...] = total.astype(BF16)

    ins = (*pieces, *flat_pair(pair))
    return pl.pallas_call(
        kernel,
        out_shape=outs,
        in_specs=[SMEM] + [whole(a.shape) for a in pieces] + [ANY] * len(flat_pair(pair)),
        out_specs=[whole(o.shape) for o in outs],
        scratch_shapes=[full_weight(pair, n), weight_sems(pair)],
        grid=(1,),
        compiler_params=params(),
        cost_estimate=cost(2 * tokens * n * part * parts, nbytes(ins)),
        name="contract",
    )(at, *ins)


def second_norm(pieces, gain):
    parts = len(pieces)
    tokens, part = pieces[0].shape
    width = parts * part
    out = struct((tokens, width), BF16)

    def kernel(*refs):
        ins, (gain_ref, out_ref) = refs[:parts], refs[parts:]
        values = [ref[...].astype(F32) for ref in ins]
        scale = rms_scale(values, width)
        for k, value in enumerate(values):
            cut = slice(k * part, (k + 1) * part)
            out_ref[:, cut] = (value * scale * gain_ref[:, cut]).astype(BF16)

    return pl.pallas_call(
        kernel,
        out_shape=out,
        in_specs=[whole(a.shape) for a in pieces] + [whole(gain.shape)],
        out_specs=whole(out.shape),
        grid=(1,),
        compiler_params=params(limit=24 * 1024 * 1024),
        cost_estimate=cost(tokens * width * 4, nbytes((*pieces, out))),
        name="second_norm",
    )(*pieces, gain)


def run_experts(at, tokens_in, grads, spread, pair, router, router_at, parts, by_part):
    count = len(tokens_in)
    tok, width = tokens_in[0].shape
    hidden = flat_pair(pair)[0].shape[-1] // 3
    part = width // parts
    lo_count = parts if by_part else 1

    def kernel(at_ref, s_ref, *refs):
        x_refs, refs = refs[:count], refs[count:]
        g_refs, refs = refs[:count], refs[count:]
        weights, refs = taken(refs, pair)
        routers, refs = taken(refs, router)
        weighted, d_high, logit, *refs = refs
        dxs, refs = refs[:count], refs[count:]
        los, refs = refs[: count * lo_count], refs[count * lo_count :]
        full, r_ref, x_now, g_now, sems, x_sems = refs
        pairs, fulls = [weights, routers], [full, r_ref]
        high, low = slice(0, 2 * hidden), slice(2 * hidden, 3 * hidden)
        step = pl.program_id(0)
        arrivals = [
            [
                pltpu.make_async_copy(x_refs[i], x_now.at[i % 2], x_sems.at[0, i % 2]),
                pltpu.make_async_copy(g_refs[i], g_now.at[i % 2], x_sems.at[1, i % 2]),
            ]
            for i in range(count)
        ]

        @pl.when(step == 0)
        def _():
            for copy in arrivals[0]:
                copy.start()
            for copy in weight_copies(at_ref, pairs, fulls, sems, parts, (0, router_at)):
                copy.start()

        for i in range(count):

            @pl.when(step == i)
            def _(i=i):
                for copy in arrivals[i]:
                    copy.wait()
                if i + 1 < count:
                    for copy in arrivals[i + 1]:
                        copy.start()

        slot = lax.rem(step, 2)
        pre, back, logits = 0.0, 0.0, 0.0
        for k in range(parts):

            @pl.when(step == 0)
            def _(k=k):
                weight_wait(pairs, fulls, sems, parts, k)

            cut = slice(k * part, (k + 1) * part)
            x = x_now[slot, :, cut]
            pre = pre + dot(x, full[cut, high])
            back = back + dot(g_now[slot, :, cut], full[cut, low])
            logits = logits + dot(x, r_ref[cut])
        logits = jnp.where(g_now[slot, :, width:] > 0, logits, NEGATIVE)
        peak = jnp.max(logits, axis=1, keepdims=True)
        powers = jnp.exp(logits - peak)
        gate_probs = powers / jnp.sum(powers, axis=1, keepdims=True)
        spread = s_ref[...]
        one, two = two_parts(gate_probs)
        probs_wide = dot(one, spread) + dot(two, spread)
        gate_pre, up_pre = pre[:, :hidden], pre[:, hidden:]
        sigmoid = 0.5 + 0.5 * jnp.tanh(0.5 * gate_pre)
        swish = gate_pre * sigmoid
        active = swish * up_pre
        weighted_now = (probs_wide * active).astype(BF16)
        weighted[...] = weighted_now
        gate_grad = dot_bt((active * back).astype(BF16), spread)
        logit_low = (
            gate_probs * (gate_grad - jnp.sum(gate_probs * gate_grad, axis=1, keepdims=True))
        ).astype(BF16)
        logit[...] = logit_low
        back = probs_wide * back
        d_high[:, :hidden] = (back * up_pre * (sigmoid + swish * (1.0 - sigmoid))).astype(BF16)
        d_high[:, hidden:] = (back * swish).astype(BF16)
        dx = dot_bt(d_high[...], full[:, high]) + dot_bt(logit_low, r_ref[...])
        total = dot_bt(weighted_now, full[:, low])
        for i, ref in enumerate(dxs):

            @pl.when(step == i)
            def _(i=i, ref=ref):
                ref[...] = dx.astype(BF16)
                n = width // lo_count
                for k, lo in enumerate(los[i * lo_count : (i + 1) * lo_count]):
                    lo[...] = total[:, k * n : (k + 1) * n].astype(BF16)

    def rows(n):
        return pl.BlockSpec((tok, n), lambda i, at_ref: (i, 0))

    outs = [struct((count * tok, n), BF16) for n in (hidden, 2 * hidden, LANES)]
    outs += [struct((tok, width), BF16)] * count
    outs += [struct((tok, width // lo_count), BF16)] * (count * lo_count)
    all_weights = flat_pair(pair) + flat_pair(router)
    ins = (spread, *tokens_in, *grads, *all_weights)
    weighted, d_high, logit, *rest = pl.pallas_call(
        kernel,
        out_shape=outs,
        grid_spec=pltpu.PrefetchScalarGridSpec(
            num_scalar_prefetch=1,
            grid=(count,),
            in_specs=[whole(spread.shape)] + [ANY] * (2 * count + len(all_weights)),
            out_specs=[rows(hidden), rows(2 * hidden), rows(LANES)]
            + [whole(o.shape) for o in outs[3:]],
            scratch_shapes=[
                full_weight(pair),
                full_weight(router, LANES),
                pltpu.VMEM((2, tok, width), BF16),
                pltpu.VMEM((2, tok, grads[0].shape[1]), BF16),
                weight_sems(pair, router),
                pltpu.SemaphoreType.DMA((2, 2)),
            ],
        ),
        compiler_params=params(limit=32 * 1024 * 1024),
        cost_estimate=cost(12 * count * tok * width * hidden, nbytes([*all_weights, *outs])),
        name="run_experts",
    )(at, *ins)
    dx, los = rest[:count], rest[count:]
    if by_part:
        los = [los[i * parts : (i + 1) * parts] for i in range(count)]
    return weighted, d_high, logit, dx, los


def weight_grads(at, place, outer_at, half_at, lefts, rights, parts, blocks, part, add=None, by_device=False, joined=False):
    unit = part * parts // blocks // 2
    stacks = [stack for group in rights for stack in group]
    left_flat = [a if isinstance(a, tuple) else (a, None) for runs in lefts for a in runs]
    if blocks != parts:
        width = part * parts
        totals = []
        for runs, group in zip(lefts, rights):
            runs = [
                lax.dynamic_index_in_dim(a[0], outer_at ^ a[1], 0, keepdims=False)
                if isinstance(a, tuple)
                else a
                for a in runs
            ]
            left = jnp.concatenate([a[:, :width] for a in runs], axis=0)
            left = left.reshape(left.shape[0], parts, 2, -1)[:, :, half_at].reshape(left.shape[0], -1)
            total = jnp.concatenate([dot_at(left, jnp.concatenate(x, axis=0)) for x in group], axis=1)
            total = total.reshape(blocks, unit, -1)
            order = [place ^ j for j in range(blocks)]
            out = jnp.stack([lax.dynamic_index_in_dim(total, i, 0, keepdims=False) for i in order])
            if add is not None and len(add) == 1:
                start = sum(a.shape[2] for a in totals)
                out = out + add[0][:, :, start : start + out.shape[2]].astype(F32)
            elif add is not None:
                out = out + add[len(totals)].astype(F32)
            order = [outer_at ^ j if by_device else j for j in range(blocks)]
            out = [lax.dynamic_index_in_dim(out, i, 0, keepdims=False) for i in order]
            totals.append(jnp.stack(out).astype(BF16))
        return [jnp.concatenate(totals, axis=2)] if joined else totals
    flat = [r for stack in stacks for r in stack]
    tokens = sum(r.shape[0] for r in stacks[0])
    sizes = [sum(stack[0].shape[1] for stack in group) for group in rights]
    n = sum(sizes)
    outs = [struct((blocks, unit, size), BF16) for size in ([n] if joined else sizes)]
    joins = [stack for stack in stacks if len(stack) > 1]
    extra = [] if add is None else add
    counts = [len(runs) for runs in lefts]

    def kernel(at_ref, *refs):
        left_refs, refs = refs[: len(left_flat)], refs[len(left_flat) :]
        right_refs, refs = refs[: len(flat)], refs[len(flat) :]
        added, refs = refs[: len(extra)], refs[len(extra) :]
        out_refs, fulls = refs[: len(outs)], refs[len(outs) :]
        step = pl.program_id(0)
        stacked = []
        for stack in stacks:
            stack_refs, right_refs = right_refs[: len(stack)], right_refs[len(stack) :]
            if len(stack) == 1:
                stacked.append(stack_refs[0])
            else:
                full, fulls = fulls[0], fulls[1:]
                stacked.append(full)

                @pl.when(step == 0)
                def _(full=full, stack_refs=stack_refs):
                    row = 0
                    for ref in stack_refs:
                        full[row : row + ref.shape[0]] = ref[...]
                        row += ref.shape[0]

        column, rest, more = 0, stacked, left_refs
        for i, (count, group) in enumerate(zip(counts, rights)):
            run_refs, more = more[:count], more[count:]
            now, rest = rest[: len(group)], rest[len(group) :]
            left = jnp.concatenate([ref[...].reshape(-1, unit) for ref in run_refs], axis=0).T
            column = column if joined else 0
            own = 0
            for right in now:
                cut = slice(column, column + right.shape[1])
                value = dot(left, right[...])
                if extra:
                    source, start = (added[0], column) if len(extra) == 1 else (added[i], own)
                    value = value + source[0, :, start : start + right.shape[1]].astype(F32)
                out_refs[0 if joined else i][0, :, cut] = value.astype(BF16)
                column, own = cut.stop, own + right.shape[1]

    def left_spec(a, i):
        if a.ndim == 3:
            return pl.BlockSpec(
                (1, a.shape[1], unit),
                lambda j, at_ref: (at_ref[1] ^ i, 0, 2 * (j ^ at_ref[0]) + half_at),
            )
        return pl.BlockSpec((a.shape[0], unit), lambda j, at_ref: (0, 2 * (j ^ at_ref[0]) + half_at))

    ins = (*[a for a, _ in left_flat], *flat, *extra)
    return pl.pallas_call(
        kernel,
        out_shape=outs,
        grid_spec=pltpu.PrefetchScalarGridSpec(
            num_scalar_prefetch=1,
            grid=(blocks,),
            in_specs=[left_spec(a, i) for a, i in left_flat]
            + [whole(a.shape) for a in flat]
            + [pl.BlockSpec((1,) + a.shape[1:], lambda j, at_ref: (j, 0, 0)) for a in extra],
            out_specs=[
                pl.BlockSpec(
                    (1,) + o.shape[1:], lambda j, at_ref: (at_ref[1] ^ j if by_device else j, 0, 0)
                )
                for o in outs
            ],
            scratch_shapes=[
                pltpu.VMEM((sum(a.shape[0] for a in stack), stack[0].shape[1]), BF16)
                for stack in joins
            ],
        ),
        compiler_params=params(limit=40 * 1024 * 1024),
        cost_estimate=cost(2 * tokens * blocks * unit * n, nbytes(ins)),
        name="weight_grads",
    )(at, *ins)


def by_owner(weights, blocks):
    unit, hidden = weights[0].shape[0], weights[0].shape[1] // blocks
    if hidden % LANES:
        return jnp.concatenate(
            [w.reshape(unit, blocks, hidden).transpose(1, 0, 2) for w in weights], axis=2
        )

    def kernel(*refs):
        for i, ref in enumerate(refs[:-1]):
            refs[-1][0, :, i * hidden : (i + 1) * hidden] = ref[...]

    out = struct((blocks, unit, hidden * len(weights)), BF16)
    return pl.pallas_call(
        kernel,
        out_shape=out,
        grid=(blocks,),
        in_specs=[pl.BlockSpec((unit, hidden), lambda i: (0, i)) for _ in weights],
        out_specs=pl.BlockSpec((1,) + out.shape[1:], lambda i: (i, 0, 0)),
        compiler_params=params(),
        cost_estimate=cost(1, 1),
        name="by_owner",
    )(*weights)


def by_columns(grads, hidden):
    blocks, unit, n = grads.shape
    starts = (0, hidden, 2 * hidden + LANES)
    if hidden % LANES:
        return [
            grads[:, :, start : start + hidden]
            .transpose(1, 0, 2)
            .reshape(unit, blocks * hidden)
            .astype(F32)
            for start in starts
        ]

    def kernel(ref, *outs):
        for start, out in zip(starts, outs):
            out[...] = ref[0, :, start : start + hidden].astype(F32)

    outs = [struct((unit, blocks * hidden), F32) for _ in starts]
    return pl.pallas_call(
        kernel,
        out_shape=outs,
        grid=(blocks,),
        in_specs=[pl.BlockSpec((1, unit, n), lambda i: (i, 0, 0))],
        out_specs=[pl.BlockSpec((unit, hidden), lambda i: (0, i)) for _ in starts],
        compiler_params=params(limit=24 * 1024 * 1024),
        cost_estimate=cost(0, nbytes([grads, *outs])),
        name="by_columns",
    )(grads)


def norm_back(values, pieces, scale, gain, gain_grad, outs, width):
    part = pieces[0].shape[1]
    cuts = [slice(k * part, (k + 1) * part) for k in range(len(pieces))]
    inner = 0.0
    for value, piece, cut in zip(values, pieces, cuts):
        gain_grad[:, cut] = jnp.sum(value * (piece * scale), axis=0, keepdims=True)
        inner = inner + jnp.sum(value * gain[:, cut] * piece, axis=1, keepdims=True)
    inner = inner * (scale * scale * scale / width)
    for value, piece, cut, out in zip(values, pieces, cuts, outs):
        out[...] = (value * gain[:, cut] * scale - piece * inner).astype(out.dtype)


def second_norm_back(received, pieces, gain):
    parts, blocks = len(pieces), len(received)
    tokens, width = received[0].shape
    part = width // parts
    outs = [struct((tokens, part), F32 if k == 0 else BF16) for k in range(parts)]
    outs.append(struct((1, width), F32))

    def kernel(*refs):
        got, refs = refs[:blocks], refs[blocks:]
        ins, (gain_ref, *outs, gain_grad) = refs[:parts], refs[parts:]
        values = []
        for k in range(parts):
            cut = slice(k * part, (k + 1) * part)
            values.append(sum(ref[:, cut].astype(F32) for ref in got))
        pieces = [ref[...].astype(F32) for ref in ins]
        scale = rms_scale(pieces, width)
        norm_back(values, pieces, scale, gain_ref, gain_grad, outs, width)

    ins = (*received, *pieces, gain)
    return pl.pallas_call(
        kernel,
        out_shape=outs,
        in_specs=[whole(a.shape) for a in ins],
        out_specs=[whole(o.shape) for o in outs],
        grid=(1,),
        compiler_params=params(limit=24 * 1024 * 1024),
        cost_estimate=cost(tokens * width * 20, nbytes(ins)),
        name="second_norm_back",
    )(*ins)


def project_back(
    at, grad_q, grad_kv, pre, pieces, gain, pair, query_gain, key_gain, cosine, sine, heads, kv_heads, gain_grad_two, router, experts
):
    parts, runs, blocks = len(pieces), len(grad_q), len(grad_kv)
    tokens, n = pre.shape
    width = gain.shape[1]
    part = width // parts
    size = query_gain.shape[1]
    gain_lines = -(-(2 * parts + 1) // 16) * 16
    lines = gain_lines + -(-experts // 16) * 16
    router_rows = router.shape[0]
    outs = [struct((tokens, part), F32)] + [struct((tokens + lines, part), BF16)] * (parts - 1)
    outs += [struct((tokens, n), BF16), struct((lines, part), F32)]

    def kernel(at_ref, pre_ref, two_ref, router_ref, *refs):
        gq, refs = refs[:runs], refs[runs:]
        gkv, refs = refs[:blocks], refs[blocks:]
        ins, refs = refs[:parts], refs[parts:]
        weights, refs = taken(refs, pair)
        gain_ref, qg, kg, cos_ref, sin_ref, *refs = refs
        outs, (d_wide, sums, gain_grad, full, sems) = refs[:parts], refs[parts:]
        for copy in weight_copies(at_ref, [weights], [full], sems, parts):
            copy.start()
        cosine, sine = cos_ref[...], sin_ref[...]
        totals = [jnp.zeros((1, size), F32), jnp.zeros((1, size), F32)]
        for i in range(n // size):
            cut = slice(i * size, (i + 1) * size)
            if i < heads:
                grad = jnp.concatenate([ref[:, cut] for ref in gq], axis=0)
            else:
                kv_cut = slice((i - heads) * size, (i - heads + 1) * size)
                grad = sum(ref[:, kv_cut].astype(F32) for ref in gkv)
            if i < heads + kv_heads:
                which = 0 if i < heads else 1
                gain_row = (qg, kg)[which][...]
                grad = grad * cosine + pltpu.roll(grad * sine, size // 2, 1)
                head = pre_ref[:, cut]
                scale = lax.rsqrt(jnp.mean(head * head, axis=1, keepdims=True) + EPS)
                unit = head * scale
                totals[which] = totals[which] + jnp.sum(grad * unit, axis=0, keepdims=True)
                grad = grad * gain_row
                grad = scale * (grad - unit * jnp.mean(grad * unit, axis=1, keepdims=True))
            d_wide[:, cut] = grad.astype(BF16)
        weight_wait([weights], [full], sems, parts)
        values = [
            dot_bt(d_wide[...], full[k * part : (k + 1) * part]) for k in range(parts)
        ]
        pieces = [ref[...].astype(F32) for ref in ins]
        scale = rms_scale(pieces, width)
        cut_outs = [outs[0]] + [out.at[:tokens] for out in outs[1:]]
        norm_back(values, pieces, scale, gain_ref, gain_grad, cut_outs, width)
        sums[...] = jnp.zeros_like(sums)
        for i, ref in enumerate((gain_grad, two_ref)):
            for k in range(parts):
                sums[i * parts + k : i * parts + k + 1] = ref[:, k * part : (k + 1) * part]
        for i, total in enumerate(totals):
            sums[2 * parts : 2 * parts + 1, i * size : (i + 1) * size] = total
        sums[gain_lines : gain_lines + experts, :router_rows] = router_ref[...].T[:experts]
        for out in outs[1:]:
            out[tokens:] = sums[...].astype(BF16)

    ins = (pre, gain_grad_two, router, *grad_q, *grad_kv, *pieces, *flat_pair(pair))
    ins = (*ins, gain, query_gain, key_gain, cosine, sine)
    return pl.pallas_call(
        kernel,
        out_shape=outs,
        in_specs=[SMEM]
        + [whole(a.shape) for a in (pre, gain_grad_two, router, *grad_q, *grad_kv)]
        + [whole((tokens, part)) for _ in pieces]
        + [ANY] * len(flat_pair(pair))
        + [whole(a.shape) for a in (gain, query_gain, key_gain, cosine, sine)],
        out_specs=[whole(o.shape) for o in outs],
        scratch_shapes=[pltpu.VMEM((1, width), F32), full_weight(pair), weight_sems(pair)],
        grid=(1,),
        compiler_params=params(),
        cost_estimate=cost(2 * tokens * width * n, nbytes(ins)),
        name="project_back",
    )(at, *ins)


def sum_blocks(grads, widths, first=0):
    blocks = len(grads)
    unit = grads[0].shape[-2]

    def kernel(*refs):
        ins, outs = refs[:blocks], refs[blocks:]
        start = first
        for out in outs:
            cut = slice(start, start + out.shape[1])
            parts = [ref[:, cut] if len(ref.shape) == 2 else ref[0, :, cut] for ref in ins]
            out[...] = sum(a.astype(F32) for a in parts)
            start = cut.stop

    def spec(i, a):
        if a.ndim == 2:
            return whole(a.shape)
        return pl.BlockSpec((1,) + a.shape[1:], lambda _: (i, 0, 0))

    outs = [struct((unit, width), F32) for width in widths]
    return pl.pallas_call(
        kernel,
        out_shape=outs,
        grid=(1,),
        in_specs=[spec(i, a) for i, a in enumerate(grads)],
        out_specs=[whole(o.shape) for o in outs],
        compiler_params=params(limit=24 * 1024 * 1024),
        cost_estimate=cost(1, 1),
        name="sum_blocks",
    )(*grads)


def finish(at, residual, own, arrived, own_sums, low, unit_rows, experts):
    others = len(arrived)
    tokens, part = own.shape
    parts, half = others + 1, part // 2
    unit = half // low
    lines = own_sums.shape[0]
    gain_lines = -(-(2 * parts + 1) // 16) * 16

    def kernel(at_ref, residual, own, *refs):
        arrived, refs = refs[:others], refs[others:]
        own_sums, out, sums, router = refs
        even, col = at_ref[3] == 0, at_ref[4]

        def put(ref, rows, value):
            first = jnp.where(even, value[:, :half], value[:, half:])
            second = jnp.where(even, value[:, half:], value[:, :half])
            for i in range(low):
                cut = slice(i * unit, (i + 1) * unit)
                ref[rows, 2 * i * unit : (2 * i + 1) * unit] = first[:, cut].astype(ref.dtype)
                ref[rows, (2 * i + 1) * unit : (2 * i + 2) * unit] = second[:, cut].astype(ref.dtype)

        value = residual[...] + own[...]
        for ref in arrived:
            value = value + ref[:tokens].astype(F32)
        put(out, slice(0, tokens), value)
        got = [ref[tokens:].astype(F32) for ref in arrived]
        total = own_sums[...]
        for a in got:
            total = total + a
        sums[...] = total[:gain_lines]
        router[...] = total[gain_lines : gain_lines + experts, :unit_rows].T
        for i in range(2):
            for k in range(parts):
                line = own_sums[i * parts + k : i * parts + k + 1]
                for mask, a in enumerate(got, 1):
                    row = i * parts + (k ^ mask)
                    line = line + a[row : row + 1]
                for to in range(parts):

                    @pl.when(col ^ k == to)
                    def _(i=i, to=to, line=line):
                        put(sums, slice(i * parts + to, i * parts + to + 1), line)

    outs = (
        struct((tokens, part), BF16),
        struct((gain_lines, part), F32),
        struct((unit_rows, experts), F32),
    )
    ins = (residual, own, *arrived, own_sums)
    return pl.pallas_call(
        kernel,
        out_shape=outs,
        grid=(1,),
        in_specs=[SMEM] + [whole(a.shape) for a in ins],
        out_specs=[whole(o.shape) for o in outs],
        compiler_params=params(limit=24 * 1024 * 1024),
        cost_estimate=cost(1, 1),
        name="finish",
    )(at, *ins)


def per_device(
    layer_in,
    out_grad,
    lengths,
    token_order,
    choices,
    norm_gain,
    w_query,
    w_key,
    w_value,
    query_gain,
    key_gain,
    w_out,
    ffn_gain,
    w_router,
    w_gate,
    w_up,
    w_down,
):
    micro, tok, part = layer_in.shape
    outer, cols = lax.axis_size("outer"), lax.axis_size("col")
    rows = 2 * outer
    tokens = micro * tok
    width = part * cols
    outer_at, core_at, col_at = (lax.axis_index(name) for name in ("outer", "core", "col"))
    row_at = outer_at * 2 + core_at
    low = outer // cols
    unit = width // rows
    half = part // 2
    size = query_gain.shape[0]
    heads = w_query.shape[1] // size
    kv_heads = w_key.shape[1] // size
    experts = w_router.shape[1]
    hidden = w_gate.shape[1] // outer
    repeats = hidden // experts

    place = outer_at ^ (col_at * low)
    at = jnp.stack([place, outer_at, col_at * low, core_at, col_at]).astype(jnp.int32)

    def core_swap(a):
        return lax.ppermute(a, "core", [(0, 1), (1, 0)])

    def col_swap(a, mask):
        return lax.ppermute(a, "col", [(i, i ^ mask) for i in range(cols)])

    def exchange(a):
        return lax.all_to_all(a, "outer", 0, 0, tiled=True)

    def for_all(a):
        return jnp.broadcast_to(a[None], (outer,) + a.shape)

    def after(a, b):
        return lax.optimization_barrier((a, b))[0]

    def to_halves(a):
        blocks = a.reshape(a.shape[:-1] + (low, 2, unit))
        first = blocks[..., 0, :].reshape(a.shape[:-1] + (half,))
        second = blocks[..., 1, :].reshape(a.shape[:-1] + (half,))
        even = core_at == 0
        return jnp.concatenate(
            [jnp.where(even, first, second), jnp.where(even, second, first)], axis=-1
        )

    def from_halves(a):
        even = core_at == 0
        first = jnp.where(even, a[..., :half], a[..., half:]).reshape(a.shape[:-1] + (low, unit))
        second = jnp.where(even, a[..., half:], a[..., :half]).reshape(a.shape[:-1] + (low, unit))
        return jnp.stack([first, second], axis=-2).reshape(a.shape)

    def col_gather(a):
        return [a] + [col_swap(a, k) for k in range(1, cols)]

    def col_total(pieces):
        total = pieces[0]
        for k in range(1, cols):
            total = total + col_swap(pieces[k], k).astype(F32)
        return total

    def swap(a, mask):
        return lax.ppermute(a, "outer", [(i, i ^ mask) for i in range(outer)])

    def gather(a):
        return [a] + [swap(a, j) for j in range(1, outer)]

    def scatter(blocks):
        return [blocks[0]] + [swap(blocks[j], j) for j in range(1, outer)]

    def swap(a, mask):
        return lax.ppermute(a, "outer", [(i, i ^ mask) for i in range(outer)])

    def gather(a):
        return [a] + [swap(a, j) for j in range(1, outer)]

    def scatter(blocks):
        return [blocks[0]] + [swap(blocks[j], j) for j in range(1, outer)]

    def both(*arrays):
        return lax.optimization_barrier(arrays)

    def both_cores(a):
        return a, [core_swap(b) for b in a] if isinstance(a, list) else core_swap(a)

    own_in = to_halves(layer_in).reshape(tokens, part)
    own_grad = to_halves(out_grad).reshape(tokens, part)
    w_in = gather(jnp.concatenate([w_query, w_key, w_value], axis=1))
    arrived = col_gather(own_in)
    w_back = jnp.concatenate([w_out, jnp.pad(w_router, ((0, 0), (0, LANES - experts)))], axis=1)
    w_back = for_all(w_back)
    weights = by_owner([w_gate, w_up, w_down], outer)
    q_gain, k_gain = query_gain[None, :], key_gain[None, :]
    frequency = jnp.exp(jnp.arange(size // 2, dtype=F32) * (-2.0 * math.log(THETA) / size))
    bias, angles, chosen, spread, gain_one, gain_two = prepare(
        at,
        lengths,
        token_order.reshape(micro, rows, tok),
        choices.reshape(tokens, -1),
        jnp.concatenate([frequency, frequency])[None, :],
        jnp.stack([norm_gain, ffn_gain]).reshape(2, cols, part),
        low,
        hidden,
        experts,
    )
    cosine = jnp.cos(angles)
    sine = jnp.sin(angles) * jnp.where(jnp.arange(size) < size // 2, -1.0, 1.0)

    w_back, weights, bias = both(w_back, weights, bias)
    w_back = exchange(w_back)
    w_in, arrived, weights, chosen, bias, cosine, sine, gain_one, gain_two, spread = both(
        w_in, arrived, weights, chosen, bias, cosine, sine, gain_one, gain_two, spread
    )
    own_grads = col_gather(after(own_grad, w_in))
    w_in = both_cores(w_in)
    normed_one, pre, ready, kv = project(
        at, arrived, part, gain_one, w_in, q_gain, k_gain, cosine, sine, heads, kv_heads
    )
    near = [j for j in range(1, outer) if not j & (j - 1)]
    far = [j for j in range(1, outer) if j & (j - 1)]
    far_grads, _ = both(jnp.concatenate([own_grad, chosen], axis=1), kv)
    far_grads = [swap(far_grads, j) for j in far]
    kv_own = jnp.stack(gather(kv))
    kv_own, w_back = both(kv_own, w_back)
    weights, far_grads, _ = both(weights, far_grads, w_back)
    weights = exchange(weights)
    kv_other = core_swap(kv_own)
    w_back = both_cores(w_back)
    attended, lse = attend(ready, kv_own, kv_other, bias, heads, kv_heads, size)
    attn_parts = expand(at, attended, w_back, part, cols)
    attn_parts, own_grads = both(attn_parts, own_grads)

    grads = [jnp.concatenate(own_grads + [chosen], axis=1)] + [None] * (outer - 1)
    near_grads = [swap(grads[0], j) for j in near]

    residual = own_in.astype(F32) + col_total(attn_parts)
    residual, weights = both(residual, weights)
    full_res = col_gather(residual.astype(BF16))
    full_res, near_grads, weights = both(full_res, near_grads, weights)
    for j, a in zip(near, near_grads):
        grads[j] = a
    weights = both_cores(weights)
    normed_two = second_norm(full_res, gain_two)
    expert_in = gather(normed_two)
    far_grads, _ = both(far_grads, normed_two)
    for j, a in zip(far, far_grads):
        grads[j] = jnp.concatenate(col_gather(a[:, :part]) + [a[:, part:]], axis=1)

    results, dx, lo_far = [], [None] * outer, []
    order = [0] + far + near
    for group in [[0]] + [far[i : i + 4] for i in range(0, len(far), 4)] + [near]:
        *result, dx_now, lo_now = run_experts(
            at,
            [expert_in[j] for j in group],
            [grads[j] for j in group],
            spread,
            weights,
            w_back,
            heads * size,
            cols,
            group[0] in far,
        )
        for j, a in zip(group, dx_now):
            dx[j] = a
        if group == [0]:
            lo_own = lo_now[0]
            expert_in, lo_own = both(expert_in, lo_own)
        elif group != near:
            lo_far += lo_now
            for j in group:
                dx[j] = swap(dx[j], j)
        else:
            lo_near = lo_now
        results.append(result)
    far_dx, results[-1], lo_far = both([dx[j] for j in far], results[-1], lo_far)
    lo_far = [col_total([a[0].astype(F32), *a[1:]]).astype(BF16) for a in lo_far]
    weighted, d_high, logit_low = [list(arrays) for arrays in zip(*results)]
    near_dx, far_dx = both([dx[j] for j in near], far_dx)
    for j, a in zip(near, near_dx):
        dx[j] = swap(a, j)
    sizes = (cols, outer, part)
    expert_sides = (
        [[expert_in[j] for j in order], [grads[j] for j in order]],
        [[d_high, logit_low], [weighted]],
    )
    (other,) = weight_grads(at, place, outer_at, 1, *expert_sides, *sizes, joined=True)
    other, near_dx, lo_far, lo_near = both(other, [dx[j] for j in near], lo_far, lo_near)
    other = core_swap(other)
    *spread_two, gain_grad_two = second_norm_back([dx[0]] + near_dx + far_dx, full_res, gain_two)
    lo_near = [swap(a, j) for j, a in zip(near, lo_near)]
    (expert_grads,) = weight_grads(
        at, place, outer_at, 0, *expert_sides, *sizes, [other], True, True
    )
    spread_two[0], expert_grads = both(spread_two[0], expert_grads)
    grad_residual = own_grad.astype(F32) + col_total(spread_two)
    grad_residual, lo_near, expert_grads = both(grad_residual, lo_near, expert_grads)
    expert_grads = exchange(expert_grads)
    grad_feats = col_gather(grad_residual.astype(BF16))

    lo_near = lo_own.astype(F32) + sum(a.astype(F32) for a in lo_near)
    lo_near = [
        lo_near[:, k * part : (k + 1) * part].astype(F32 if k == 0 else BF16) for k in range(cols)
    ]
    grad_feats, lo_near = both(grad_feats, lo_near)
    back_attended, feats = contract(at, grad_feats, w_back, heads * size)
    lo_near = col_total(after(lo_near, back_attended))
    grad_q, kv_mine, kv_theirs = attend_back(
        ready, kv_own, kv_other, bias, lse, back_attended, heads, kv_heads, size
    )
    kv_theirs, expert_grads = both(kv_theirs, expert_grads)
    kv_sums = sum_cores(kv_mine, core_swap(kv_theirs))
    grad_kv = scatter(kv_sums)
    router_part = jnp.sum(
        expert_grads[:, :, 2 * hidden : 2 * hidden + LANES].astype(F32), axis=0
    )
    feats, lo_near, _ = both(feats, lo_near, grad_q)
    (other,) = weight_grads(at, place, outer_at, 1, [[feats]], [[[attended]]], *sizes)
    (out_grads,) = weight_grads(
        at, place, outer_at, 0, [[feats]], [[[attended]]], *sizes, [core_swap(other)], True
    )
    grad_kv, out_grads, lo_far = both(grad_kv, out_grads, lo_far)
    lo_far = [swap(a, j) for j, a in zip(far, lo_far)]
    out_grads = exchange(out_grads)
    *spread_one, d_wide, sums = project_back(
        at,
        [grad_q],
        grad_kv,
        pre,
        arrived,
        gain_one,
        w_in,
        q_gain,
        k_gain,
        cosine,
        sine,
        heads,
        kv_heads,
        gain_grad_two,
        router_part,
        experts,
    )
    (other,) = weight_grads(at, place, outer_at, 1, [[normed_one]], [[[d_wide]]], *sizes)
    other, expert_grads, lo_far = both(other, expert_grads, lo_far)
    grad_gate_w, grad_up_w, grad_down_w = by_columns(expert_grads, hidden)
    other = jnp.stack([core_swap(other[j]) for j in range(outer)])
    other, grad_gate_w = both(other, grad_gate_w)
    (wide_grads,) = weight_grads(
        at, place, outer_at, 0, [[normed_one]], [[[d_wide]]], *sizes, [other], True
    )
    spread_one, wide_grads, out_grads = both(spread_one, wide_grads, out_grads)
    wide_grads = exchange(wide_grads)

    got = [col_swap(spread_one[k], k) for k in range(1, cols)]
    layer_out = residual + lo_near + sum(a.astype(F32) for a in lo_far)
    layer_out = from_halves(layer_out.astype(BF16)).reshape(micro, tok, part)
    (grad_out_w,) = sum_blocks([out_grads] * outer, [heads * size])
    got, grad_out_w, layer_out = both(got, grad_out_w, layer_out)
    input_grad, sums, grad_router = finish(
        at, grad_residual, spread_one[0], got, sums, low, unit, experts
    )
    input_grad = input_grad.reshape(micro, tok, part)
    sums = sums + core_swap(sums)
    sums = gather(sums)
    wide_grads, input_grad, layer_out, grad_out_w, grad_router = both(
        wide_grads, input_grad, layer_out, grad_out_w, grad_router
    )
    grad_query_w, grad_key_w, grad_value_w = sum_blocks(
        [wide_grads] * outer, [w.shape[1] for w in (w_query, w_key, w_value)]
    )
    sums, _ = both(sums, grad_query_w)
    sums = sum(sums)
    head_sums = sums[2 * cols, : 2 * size]
    grad_norm_gain, grad_ffn_gain = sums[:cols].reshape(width), sums[cols : 2 * cols].reshape(width)
    grad_query_gain, grad_key_gain = head_sums[:size], head_sums[size:]
    return (
        layer_out,
        input_grad,
        grad_norm_gain,
        grad_query_w,
        grad_key_w,
        grad_value_w,
        grad_query_gain,
        grad_key_gain,
        grad_out_w,
        grad_ffn_gain,
        grad_router,
        grad_gate_w,
        grad_up_w,
        grad_down_w,
    )


def solution(mesh):
    rows, cols = mesh.devices.shape
    split = Mesh(mesh.devices.reshape(rows // 2, 2, cols), ("outer", "core", "col"))
    tokens_placed = P(None, ROW, "col")
    weight_placed = P(ROW, "col")
    return jax.shard_map(
        per_device,
        mesh=split,
        in_specs=(
            tokens_placed,
            tokens_placed,
            P(),
            P(),
            P(None, ROW, None),
            P(),
            weight_placed,
            weight_placed,
            weight_placed,
            P(),
            P(),
            weight_placed,
            P(),
            P(ROW, None),
            weight_placed,
            weight_placed,
            weight_placed,
        ),
        out_specs=(
            tokens_placed,
            tokens_placed,
            P(),
            weight_placed,
            weight_placed,
            weight_placed,
            P(),
            P(),
            weight_placed,
            P(),
            P(ROW, None),
            weight_placed,
            weight_placed,
            weight_placed,
        ),
        check_vma=False,
    )
```

```python
import functools
import math

import jax
import jax.numpy as jnp
from jax import lax
from jax.experimental import pallas as pl
from jax.experimental.pallas import tpu as pltpu
from jax.sharding import Mesh
from jax.sharding import PartitionSpec as P

EPS = 1e-06
THETA = 1000000.0
NEGATIVE = -1e30
F32 = jnp.float32
BF16 = jnp.bfloat16
VMEM_BYTES = 56 * 1024 * 1024
LANES = 128
ROW = ("outer", "core")


def dot(a, b):
    return jnp.dot(a, b, preferred_element_type=F32)


def dot_bt(a, b):
    return lax.dot_general(a, b, (((1,), (1,)), ((), ())), preferred_element_type=F32)


def dot_at(a, b):
    return lax.dot_general(a, b, (((0,), (0,)), ((), ())), preferred_element_type=F32)


def two_parts(a):
    high = a.astype(BF16)
    return high, (a - high.astype(F32)).astype(BF16)


ANY = pl.BlockSpec(memory_space=pl.ANY)
SMEM = pl.BlockSpec(memory_space=pltpu.SMEM)


def whole(shape):
    return pl.BlockSpec(shape, lambda *_: (0,) * len(shape))


def params(steps=1, limit=VMEM_BYTES):
    return pltpu.CompilerParams(
        dimension_semantics=("arbitrary",) * steps, vmem_limit_bytes=limit
    )


def cost(flops, moved):
    return pl.CostEstimate(flops=int(flops) // 64, bytes_accessed=int(moved) // 64, transcendentals=0)


def nbytes(arrays):
    return sum(math.prod(a.shape) * a.dtype.itemsize for a in arrays)


def struct(shape, dtype):
    return jax.ShapeDtypeStruct(shape, dtype)


def block_count(pair):
    return len(pair[0]) if isinstance(pair[0], list) else pair[0].shape[0]


def weight_copies(at_ref, pairs, fulls, sems, parts, firsts=None):
    copies, base = [], 0
    for i, (pair, full) in enumerate(zip(pairs, fulls)):
        first = firsts[i] if firsts else 0
        blocks = block_count(pair)
        low = blocks // parts
        unit = full.shape[0] // blocks // 2
        for h, sources in enumerate(pair):
            listed = isinstance(sources, list)
            for j in range(blocks):
                to = at_ref[0 if listed else 2] ^ j
                source = sources[j] if listed else sources.at[j]
                row = (2 * (to // low) + h) * (low * unit) + lax.rem(to, low) * unit
                copies.append(
                    pltpu.make_async_copy(
                        source.at[:, pl.ds(first, full.shape[1])],
                        full.at[pl.ds(pl.multiple_of(row, unit), unit)],
                        sems.at[base + h * blocks + to],
                    )
                )
        base += 2 * blocks
    return copies


def weight_wait(pairs, fulls, sems, parts, part=None):
    base = 0
    for pair, full in zip(pairs, fulls):
        blocks = block_count(pair)
        low = blocks // parts
        unit = full.shape[0] // blocks // 2
        for h in range(2):
            for to in range(blocks):
                if part is None or to // low == part:
                    row = (2 * (to // low) + h) * (low * unit) + to % low * unit
                    source = pair[h][0] if isinstance(pair[h], list) else pair[h].at[0]
                    pltpu.make_async_copy(
                        source.at[:, pl.ds(0, full.shape[1])],
                        full.at[pl.ds(row, unit)],
                        sems.at[base + h * blocks + to],
                    ).wait()
        base += 2 * blocks


def full_weight(pair, n=None):
    unit, width = (pair[0][0] if isinstance(pair[0], list) else pair[0]).shape[-2:]
    return pltpu.VMEM((2 * block_count(pair) * unit, n or width), BF16)


def weight_sems(*pairs):
    return pltpu.SemaphoreType.DMA((sum(2 * block_count(pair) for pair in pairs),))


def flat_pair(pair):
    return [a for half in pair for a in (half if isinstance(half, list) else [half])]


def taken(refs, pair):
    halves = []
    for half in pair:
        if isinstance(half, list):
            halves.append(list(refs[: len(half)]))
            refs = refs[len(half) :]
        else:
            halves.append(refs[0])
            refs = refs[1:]
    return tuple(halves), refs


def rms_scale(pieces, width):
    total = sum(jnp.sum(piece * piece, axis=1, keepdims=True) for piece in pieces)
    return lax.rsqrt(total / width + EPS)


def prepare(at, lengths, order, choices, frequency, gains, low, hidden, experts):
    micro, rows, tok = order.shape
    tokens, top = choices.shape
    _, cols, part = gains.shape
    unit = part // 2 // low
    outer, seqs, size = rows // 2, lengths.shape[1], frequency.shape[1]

    def kernel(at_ref, len_ref, order_ref, choice_ref, freq_ref, gain_ref, bias, angles, chosen, spread, *ordered):
        outer_at, core, col = at_ref[1], at_ref[3], at_ref[4]
        for b in range(micro):

            def seq_of(value):
                seq, start, end = jnp.zeros_like(value), jnp.zeros_like(value), 0
                for i in range(seqs):
                    end = end + len_ref[b, i]
                    passed = value >= end
                    seq = seq + jnp.where(passed, 1, 0)
                    start = start + jnp.where(passed, len_ref[b, i], 0)
                return seq, start

            def row(at):
                return order_ref[b, pl.ds(at, 1), :]

            own = row(2 * outer_at + core)
            own_seq, own_start = seq_of(own)
            keys = jnp.concatenate(
                [row(2 * (outer_at ^ j) + (core ^ h)) for h in range(2) for j in range(outer)], axis=0
            )
            key_seq, _ = seq_of(keys)
            lines = [keys, key_seq, own - own_start]
            lines.append(jnp.zeros((tok - 2 * rows - 1, tok), jnp.int32))
            turned = jnp.concatenate(lines, axis=0).astype(F32).T
            own, own_seq = own.astype(F32), own_seq.astype(F32)
            for i in range(rows):
                allowed = (turned[:, rows + i : rows + i + 1] == own_seq) & (
                    turned[:, i : i + 1] <= own
                )
                bias[b, i * tok : (i + 1) * tok] = jnp.where(allowed, 0.0, NEGATIVE)
            angles[b * tok : (b + 1) * tok] = turned[:, 2 * rows : 2 * rows + 1] * freq_ref[...]
        lanes = lax.broadcasted_iota(jnp.int32, (tokens, LANES), 1)
        hits = jnp.zeros((tokens, LANES), F32)
        for i in range(top):
            hits = hits + jnp.where(choice_ref[:, i : i + 1] == lanes, 1.0, 0.0)
        chosen[...] = hits.astype(BF16)
        units = lax.broadcasted_iota(jnp.int32, (LANES, hidden), 1)
        owners = lax.broadcasted_iota(jnp.int32, (LANES, hidden), 0)
        spread[...] = jnp.where(lax.rem(units, experts) == owners, 1.0, 0.0).astype(BF16)
        for i, out in enumerate(ordered):
            for k in range(cols):
                line = gain_ref[i, pl.ds(col ^ k, 1), :]
                for n in range(low):
                    first = line[:, 2 * n * unit : (2 * n + 1) * unit]
                    second = line[:, (2 * n + 1) * unit : (2 * n + 2) * unit]
                    start = k * part + n * unit
                    out[:, start : start + unit] = jnp.where(core == 0, first, second)
                    start = start + part // 2
                    out[:, start : start + unit] = jnp.where(core == 0, second, first)

    outs = (
        struct((micro, rows * tok, tok), F32),
        struct((tokens, size), F32),
        struct((tokens, LANES), BF16),
        struct((LANES, hidden), BF16),
        struct((1, cols * part), F32),
        struct((1, cols * part), F32),
    )
    ins = (order, choices, frequency, gains)
    return pl.pallas_call(
        kernel,
        out_shape=outs,
        grid=(1,),
        in_specs=[SMEM, SMEM] + [whole(a.shape) for a in ins],
        out_specs=[whole(o.shape) for o in outs],
        compiler_params=params(),
        cost_estimate=cost(1, 1),
        name="prepare",
    )(at, lengths, *ins)


def project(at, pieces, part, gain, pair, query_gain, key_gain, cosine, sine, heads, kv_heads):
    parts = len(pieces)
    tokens = cosine.shape[0]
    width = parts * part
    n = flat_pair(pair)[0].shape[-1]
    size = query_gain.shape[1]

    def kernel(at_ref, *refs):
        ins, refs = refs[:parts], refs[parts:]
        weights, refs = taken(refs, pair)
        gain_ref, qg, kg, cos_ref, sin_ref, normed, pre, ready, kv, full, sems = refs
        for copy in weight_copies(at_ref, [weights], [full], sems, parts):
            copy.start()
        values = [ref[...].astype(F32) for ref in ins]
        scale = rms_scale(values, width)
        for k, value in enumerate(values):
            cut = slice(k * part, (k + 1) * part)
            normed[:, cut] = (value * scale * gain_ref[:, cut]).astype(BF16)
        weight_wait([weights], [full], sems, parts)
        pre[...] = dot(normed[...], full[...])
        cosine, sine = cos_ref[...], sin_ref[...]
        for i in range(n // size):
            cut = slice(i * size, (i + 1) * size)
            head = pre[:, cut]
            if i < heads + kv_heads:
                head_gain = qg[...] if i < heads else kg[...]
                head = (
                    head
                    * lax.rsqrt(jnp.mean(head * head, axis=1, keepdims=True) + EPS)
                    * head_gain
                )
                head = head * cosine + pltpu.roll(head, size // 2, 1) * sine
            if i < heads:
                ready[:, cut] = head.astype(BF16)
            else:
                kv[:, (i - heads) * size : (i - heads + 1) * size] = head.astype(BF16)

    outs = (
        struct((tokens, width), BF16),
        struct((tokens, n), F32),
        struct((tokens, heads * size), BF16),
        struct((tokens, n - heads * size), BF16),
    )
    ins = (*pieces, *flat_pair(pair), gain, query_gain, key_gain, cosine, sine)
    return pl.pallas_call(
        kernel,
        out_shape=outs,
        in_specs=[SMEM]
        + [whole((tokens, part)) for _ in pieces]
        + [ANY] * len(flat_pair(pair))
        + [whole(a.shape) for a in (gain, query_gain, key_gain, cosine, sine)],
        out_specs=[whole(o.shape) for o in outs],
        scratch_shapes=[full_weight(pair), weight_sems(pair)],
        grid=(1,),
        compiler_params=params(limit=32 * 1024 * 1024),
        cost_estimate=cost(4.5e11, 1),
        name="project",
    )(at, *ins)


def attend(ready, own, other, bias, heads, kv_heads, size):
    micro, keys, tok = bias.shape
    group = heads // kv_heads
    outer = own.shape[0]
    scale = 1.0 / math.sqrt(size)

    def kernel(q_ref, own_ref, other_ref, bias_ref, out_ref, lse_ref):
        for h in range(heads):
            key, value = (
                jnp.concatenate(
                    [
                        ref[:, :, i * size : (i + 1) * size].reshape(outer * tok, size)
                        for ref in (own_ref, other_ref)
                    ],
                    axis=0,
                )
                for i in (h // group, kv_heads + h // group)
            )
            cut = slice(h * size, (h + 1) * size)
            scores = dot_bt(key, q_ref[:, cut]) * scale + bias_ref[0]
            peak = jnp.max(scores, axis=0, keepdims=True)
            powers = jnp.exp(scores - peak)
            total = jnp.sum(powers, axis=0, keepdims=True)
            probs = (powers * (1.0 / total)).astype(BF16)
            out_ref[:, cut] = dot_at(probs, value).astype(BF16)
            lse_ref[0, h] = peak + jnp.log(total)

    kv_spec = pl.BlockSpec((outer, tok, own.shape[2]), lambda m: (0, m, 0))
    head_spec = pl.BlockSpec((tok, heads * size), lambda m: (m, 0))
    outs = (struct((micro * tok, heads * size), BF16), struct((micro, heads, 1, tok), F32))
    return pl.pallas_call(
        kernel,
        out_shape=outs,
        grid=(micro,),
        in_specs=[
            head_spec,
            kv_spec,
            kv_spec,
            pl.BlockSpec((1, keys, tok), lambda m: (m, 0, 0)),
        ],
        out_specs=[head_spec, pl.BlockSpec((1, heads, 1, tok), lambda m: (m, 0, 0, 0))],
        compiler_params=params(limit=32 * 1024 * 1024),
        cost_estimate=cost(4 * micro * heads * keys * tok * size, nbytes((own, other, bias))),
        name="attend",
    )(ready, own, other, bias)


def attend_back(ready, own, other, bias, lse, grad, heads, kv_heads, size):
    micro, keys, tok = bias.shape
    group = heads // kv_heads
    outer = own.shape[0]
    scale = 1.0 / math.sqrt(size)
    mid = keys // 2

    def kernel(q_ref, own_ref, other_ref, bias_ref, lse_ref, g_ref, gq, mine, theirs, gk, gv):
        for h in range(heads):
            key, value = (
                jnp.concatenate(
                    [
                        ref[:, :, i * size : (i + 1) * size].reshape(outer * tok, size)
                        for ref in (own_ref, other_ref)
                    ],
                    axis=0,
                )
                for i in (h // group, kv_heads + h // group)
            )
            cut = slice(h * size, (h + 1) * size)
            query, out_grad = q_ref[:, cut], g_ref[:, cut]
            scores = dot_bt(key, query) * scale + bias_ref[0]
            probs = jnp.exp(scores - lse_ref[0, h])
            back = dot_bt(value, out_grad)
            centre = jnp.sum(probs * back, axis=0, keepdims=True)
            slope = (probs * (back - centre)).astype(BF16)
            gq[:, cut] = dot_at(slope, key) * scale
            key_part = dot(slope, query) * scale
            value_part = dot(probs.astype(BF16), out_grad)
            if h % group == 0:
                gk[...] = key_part
                gv[...] = value_part
            else:
                gk[...] += key_part
                gv[...] += value_part
            if h % group == group - 1:
                for i, ref in enumerate((gk, gv)):
                    at = (i * kv_heads + h // group) * size
                    cut = slice(at, at + size)
                    mine[:, :, cut] = ref[:mid].reshape(outer, tok, size)
                    theirs[:, :, cut] = ref[mid:].reshape(outer, tok, size).astype(BF16)

    kv_spec = pl.BlockSpec((outer, tok, own.shape[2]), lambda m: (0, m, 0))
    head_spec = pl.BlockSpec((tok, heads * size), lambda m: (m, 0))
    kv_shape = (outer, micro * tok, 2 * kv_heads * size)
    outs = (
        struct((micro * tok, heads * size), F32),
        struct(kv_shape, F32),
        struct(kv_shape, BF16),
    )
    return pl.pallas_call(
        kernel,
        out_shape=outs,
        grid=(micro,),
        in_specs=[
            head_spec,
            kv_spec,
            kv_spec,
            pl.BlockSpec((1, keys, tok), lambda m: (m, 0, 0)),
            pl.BlockSpec((1, heads, 1, tok), lambda m: (m, 0, 0, 0)),
            head_spec,
        ],
        out_specs=[head_spec, kv_spec, kv_spec],
        scratch_shapes=[pltpu.VMEM((keys, size), F32)] * 2,
        compiler_params=params(),
        cost_estimate=cost(10 * micro * heads * keys * tok * size, nbytes((own, other, bias))),
        name="attend_back",
    )(ready, own, other, bias, lse, grad)


def sum_cores(mine, theirs):
    outer, tokens, n = mine.shape

    def kernel(mine, theirs, *outs):
        for j, out in enumerate(outs):
            out[...] = (mine[j] + theirs[j].astype(F32)).astype(BF16)

    outs = [struct((tokens, n), BF16)] * outer
    return pl.pallas_call(
        kernel,
        out_shape=outs,
        grid=(1,),
        in_specs=[whole(mine.shape)] * 2,
        out_specs=[whole(o.shape) for o in outs],
        compiler_params=params(limit=24 * 1024 * 1024),
        cost_estimate=cost(1, 1),
        name="sum_cores",
    )(mine, theirs)


def expand(at, a, pair, part, parts):
    tokens, n = a.shape
    outs = [struct((tokens, part), F32 if k == 0 else BF16) for k in range(parts)]

    def kernel(at_ref, a_ref, *refs):
        weights, refs = taken(refs, pair)
        outs, (full, sems) = refs[:parts], refs[parts:]
        for copy in weight_copies(at_ref, [weights], [full], sems, parts):
            copy.start()
        for k, out in enumerate(outs):
            weight_wait([weights], [full], sems, parts, k)
            out[...] = dot_bt(a_ref[...], full[k * part : (k + 1) * part]).astype(out.dtype)

    ins = (a, *flat_pair(pair))
    return pl.pallas_call(
        kernel,
        out_shape=outs,
        in_specs=[SMEM, whole(a.shape)] + [ANY] * len(flat_pair(pair)),
        out_specs=[whole(o.shape) for o in outs],
        scratch_shapes=[full_weight(pair, n), weight_sems(pair)],
        grid=(1,),
        compiler_params=params(limit=32 * 1024 * 1024),
        cost_estimate=cost(2 * tokens * n * part * parts, nbytes(ins)),
        name="expand",
    )(at, *ins)


def contract(at, pieces, pair, n):
    parts = len(pieces)
    tokens, part = pieces[0].shape
    outs = (struct((tokens, n), BF16), struct((tokens, part * parts), BF16))

    def kernel(at_ref, *refs):
        ins, refs = refs[:parts], refs[parts:]
        weights, (out, joined, full, sems) = taken(refs, pair)
        for copy in weight_copies(at_ref, [weights], [full], sems, parts):
            copy.start()
        total = 0.0
        for k, ref in enumerate(ins):
            weight_wait([weights], [full], sems, parts, k)
            joined[:, k * part : (k + 1) * part] = ref[...]
            total = total + dot(ref[...], full[k * part : (k + 1) * part])
        out[...] = total.astype(BF16)

    ins = (*pieces, *flat_pair(pair))
    return pl.pallas_call(
        kernel,
        out_shape=outs,
        in_specs=[SMEM] + [whole(a.shape) for a in pieces] + [ANY] * len(flat_pair(pair)),
        out_specs=[whole(o.shape) for o in outs],
        scratch_shapes=[full_weight(pair, n), weight_sems(pair)],
        grid=(1,),
        compiler_params=params(),
        cost_estimate=cost(2 * tokens * n * part * parts, nbytes(ins)),
        name="contract",
    )(at, *ins)


def second_norm(pieces, gain):
    parts = len(pieces)
    tokens, part = pieces[0].shape
    width = parts * part
    out = struct((tokens, width), BF16)

    def kernel(*refs):
        ins, (gain_ref, out_ref) = refs[:parts], refs[parts:]
        values = [ref[...].astype(F32) for ref in ins]
        scale = rms_scale(values, width)
        for k, value in enumerate(values):
            cut = slice(k * part, (k + 1) * part)
            out_ref[:, cut] = (value * scale * gain_ref[:, cut]).astype(BF16)

    return pl.pallas_call(
        kernel,
        out_shape=out,
        in_specs=[whole(a.shape) for a in pieces] + [whole(gain.shape)],
        out_specs=whole(out.shape),
        grid=(1,),
        compiler_params=params(limit=24 * 1024 * 1024),
        cost_estimate=cost(tokens * width * 4, nbytes((*pieces, out))),
        name="second_norm",
    )(*pieces, gain)


def run_experts(at, tokens_in, grads, spread, pair, router, router_at, parts, by_part):
    count = len(tokens_in)
    tok, width = tokens_in[0].shape
    hidden = flat_pair(pair)[0].shape[-1] // 3
    part = width // parts
    lo_count = parts if by_part else 1

    def kernel(at_ref, s_ref, *refs):
        x_refs, refs = refs[:count], refs[count:]
        g_refs, refs = refs[:count], refs[count:]
        weights, refs = taken(refs, pair)
        routers, refs = taken(refs, router)
        weighted, d_high, logit, *refs = refs
        dxs, refs = refs[:count], refs[count:]
        los, refs = refs[: count * lo_count], refs[count * lo_count :]
        full, r_ref, x_now, g_now, sems, x_sems = refs
        pairs, fulls = [weights, routers], [full, r_ref]
        high, low = slice(0, 2 * hidden), slice(2 * hidden, 3 * hidden)
        step = pl.program_id(0)
        arrivals = [
            [
                pltpu.make_async_copy(x_refs[i], x_now.at[i % 2], x_sems.at[0, i % 2]),
                pltpu.make_async_copy(g_refs[i], g_now.at[i % 2], x_sems.at[1, i % 2]),
            ]
            for i in range(count)
        ]

        @pl.when(step == 0)
        def _():
            for copy in arrivals[0]:
                copy.start()
            for copy in weight_copies(at_ref, pairs, fulls, sems, parts, (0, router_at)):
                copy.start()

        for i in range(count):

            @pl.when(step == i)
            def _(i=i):
                for copy in arrivals[i]:
                    copy.wait()
                if i + 1 < count:
                    for copy in arrivals[i + 1]:
                        copy.start()

        slot = lax.rem(step, 2)
        pre, back, logits = 0.0, 0.0, 0.0
        for k in range(parts):

            @pl.when(step == 0)
            def _(k=k):
                weight_wait(pairs, fulls, sems, parts, k)

            cut = slice(k * part, (k + 1) * part)
            x = x_now[slot, :, cut]
            pre = pre + dot(x, full[cut, high])
            back = back + dot(g_now[slot, :, cut], full[cut, low])
            logits = logits + dot(x, r_ref[cut])
        logits = jnp.where(g_now[slot, :, width:] > 0, logits, NEGATIVE)
        peak = jnp.max(logits, axis=1, keepdims=True)
        powers = jnp.exp(logits - peak)
        gate_probs = powers / jnp.sum(powers, axis=1, keepdims=True)
        spread = s_ref[...]
        one, two = two_parts(gate_probs)
        probs_wide = dot(one, spread) + dot(two, spread)
        gate_pre, up_pre = pre[:, :hidden], pre[:, hidden:]
        sigmoid = 0.5 + 0.5 * jnp.tanh(0.5 * gate_pre)
        swish = gate_pre * sigmoid
        active = swish * up_pre
        weighted_now = (probs_wide * active).astype(BF16)
        weighted[...] = weighted_now
        gate_grad = dot_bt((active * back).astype(BF16), spread)
        logit_low = (
            gate_probs * (gate_grad - jnp.sum(gate_probs * gate_grad, axis=1, keepdims=True))
        ).astype(BF16)
        logit[...] = logit_low
        back = probs_wide * back
        d_high[:, :hidden] = (back * up_pre * (sigmoid + swish * (1.0 - sigmoid))).astype(BF16)
        d_high[:, hidden:] = (back * swish).astype(BF16)
        dx = dot_bt(d_high[...], full[:, high]) + dot_bt(logit_low, r_ref[...])
        total = dot_bt(weighted_now, full[:, low])
        for i, ref in enumerate(dxs):

            @pl.when(step == i)
            def _(i=i, ref=ref):
                ref[...] = dx.astype(BF16)
                n = width // lo_count
                for k, lo in enumerate(los[i * lo_count : (i + 1) * lo_count]):
                    lo[...] = total[:, k * n : (k + 1) * n].astype(BF16)

    def rows(n):
        return pl.BlockSpec((tok, n), lambda i, at_ref: (i, 0))

    outs = [struct((count * tok, n), BF16) for n in (hidden, 2 * hidden, LANES)]
    outs += [struct((tok, width), BF16)] * count
    outs += [struct((tok, width // lo_count), BF16)] * (count * lo_count)
    all_weights = flat_pair(pair) + flat_pair(router)
    ins = (spread, *tokens_in, *grads, *all_weights)
    weighted, d_high, logit, *rest = pl.pallas_call(
        kernel,
        out_shape=outs,
        grid_spec=pltpu.PrefetchScalarGridSpec(
            num_scalar_prefetch=1,
            grid=(count,),
            in_specs=[whole(spread.shape)] + [ANY] * (2 * count + len(all_weights)),
            out_specs=[rows(hidden), rows(2 * hidden), rows(LANES)]
            + [whole(o.shape) for o in outs[3:]],
            scratch_shapes=[
                full_weight(pair),
                full_weight(router, LANES),
                pltpu.VMEM((2, tok, width), BF16),
                pltpu.VMEM((2, tok, grads[0].shape[1]), BF16),
                weight_sems(pair, router),
                pltpu.SemaphoreType.DMA((2, 2)),
            ],
        ),
        compiler_params=params(limit=32 * 1024 * 1024),
        cost_estimate=cost(12 * count * tok * width * hidden, nbytes([*all_weights, *outs])),
        name="run_experts",
    )(at, *ins)
    dx, los = rest[:count], rest[count:]
    if by_part:
        los = [los[i * parts : (i + 1) * parts] for i in range(count)]
    return weighted, d_high, logit, dx, los


def weight_grads(at, place, outer_at, half_at, lefts, rights, parts, blocks, part, add=None, by_device=False, joined=False):
    unit = part * parts // blocks // 2
    stacks = [stack for group in rights for stack in group]
    left_flat = [a if isinstance(a, tuple) else (a, None) for runs in lefts for a in runs]
    if blocks != parts:
        width = part * parts
        totals = []
        for runs, group in zip(lefts, rights):
            runs = [
                lax.dynamic_index_in_dim(a[0], outer_at ^ a[1], 0, keepdims=False)
                if isinstance(a, tuple)
                else a
                for a in runs
            ]
            left = jnp.concatenate([a[:, :width] for a in runs], axis=0)
            left = left.reshape(left.shape[0], parts, 2, -1)[:, :, half_at].reshape(left.shape[0], -1)
            total = jnp.concatenate([dot_at(left, jnp.concatenate(x, axis=0)) for x in group], axis=1)
            total = total.reshape(blocks, unit, -1)
            order = [place ^ j for j in range(blocks)]
            out = jnp.stack([lax.dynamic_index_in_dim(total, i, 0, keepdims=False) for i in order])
            if add is not None and len(add) == 1:
                start = sum(a.shape[2] for a in totals)
                out = out + add[0][:, :, start : start + out.shape[2]].astype(F32)
            elif add is not None:
                out = out + add[len(totals)].astype(F32)
            order = [outer_at ^ j if by_device else j for j in range(blocks)]
            out = [lax.dynamic_index_in_dim(out, i, 0, keepdims=False) for i in order]
            totals.append(jnp.stack(out).astype(BF16))
        return [jnp.concatenate(totals, axis=2)] if joined else totals
    flat = [r for stack in stacks for r in stack]
    tokens = sum(r.shape[0] for r in stacks[0])
    sizes = [sum(stack[0].shape[1] for stack in group) for group in rights]
    n = sum(sizes)
    outs = [struct((blocks, unit, size), BF16) for size in ([n] if joined else sizes)]
    joins = [stack for stack in stacks if len(stack) > 1]
    extra = [] if add is None else add
    counts = [len(runs) for runs in lefts]

    def kernel(at_ref, *refs):
        left_refs, refs = refs[: len(left_flat)], refs[len(left_flat) :]
        right_refs, refs = refs[: len(flat)], refs[len(flat) :]
        added, refs = refs[: len(extra)], refs[len(extra) :]
        out_refs, fulls = refs[: len(outs)], refs[len(outs) :]
        step = pl.program_id(0)
        stacked = []
        for stack in stacks:
            stack_refs, right_refs = right_refs[: len(stack)], right_refs[len(stack) :]
            if len(stack) == 1:
                stacked.append(stack_refs[0])
            else:
                full, fulls = fulls[0], fulls[1:]
                stacked.append(full)

                @pl.when(step == 0)
                def _(full=full, stack_refs=stack_refs):
                    row = 0
                    for ref in stack_refs:
                        full[row : row + ref.shape[0]] = ref[...]
                        row += ref.shape[0]

        column, rest, more = 0, stacked, left_refs
        for i, (count, group) in enumerate(zip(counts, rights)):
            run_refs, more = more[:count], more[count:]
            now, rest = rest[: len(group)], rest[len(group) :]
            left = jnp.concatenate([ref[...].reshape(-1, unit) for ref in run_refs], axis=0).T
            column = column if joined else 0
            own = 0
            for right in now:
                cut = slice(column, column + right.shape[1])
                value = dot(left, right[...])
                if extra:
                    source, start = (added[0], column) if len(extra) == 1 else (added[i], own)
                    value = value + source[0, :, start : start + right.shape[1]].astype(F32)
                out_refs[0 if joined else i][0, :, cut] = value.astype(BF16)
                column, own = cut.stop, own + right.shape[1]

    def left_spec(a, i):
        if a.ndim == 3:
            return pl.BlockSpec(
                (1, a.shape[1], unit),
                lambda j, at_ref: (at_ref[1] ^ i, 0, 2 * (j ^ at_ref[0]) + half_at),
            )
        return pl.BlockSpec((a.shape[0], unit), lambda j, at_ref: (0, 2 * (j ^ at_ref[0]) + half_at))

    ins = (*[a for a, _ in left_flat], *flat, *extra)
    return pl.pallas_call(
        kernel,
        out_shape=outs,
        grid_spec=pltpu.PrefetchScalarGridSpec(
            num_scalar_prefetch=1,
            grid=(blocks,),
            in_specs=[left_spec(a, i) for a, i in left_flat]
            + [whole(a.shape) for a in flat]
            + [pl.BlockSpec((1,) + a.shape[1:], lambda j, at_ref: (j, 0, 0)) for a in extra],
            out_specs=[
                pl.BlockSpec(
                    (1,) + o.shape[1:], lambda j, at_ref: (at_ref[1] ^ j if by_device else j, 0, 0)
                )
                for o in outs
            ],
            scratch_shapes=[
                pltpu.VMEM((sum(a.shape[0] for a in stack), stack[0].shape[1]), BF16)
                for stack in joins
            ],
        ),
        compiler_params=params(limit=40 * 1024 * 1024),
        cost_estimate=cost(2 * tokens * blocks * unit * n, nbytes(ins)),
        name="weight_grads",
    )(at, *ins)


def by_owner(weights, blocks):
    unit, hidden = weights[0].shape[0], weights[0].shape[1] // blocks
    if hidden % LANES:
        return jnp.concatenate(
            [w.reshape(unit, blocks, hidden).transpose(1, 0, 2) for w in weights], axis=2
        )

    def kernel(*refs):
        for i, ref in enumerate(refs[:-1]):
            refs[-1][0, :, i * hidden : (i + 1) * hidden] = ref[...]

    out = struct((blocks, unit, hidden * len(weights)), BF16)
    return pl.pallas_call(
        kernel,
        out_shape=out,
        grid=(blocks,),
        in_specs=[pl.BlockSpec((unit, hidden), lambda i: (0, i)) for _ in weights],
        out_specs=pl.BlockSpec((1,) + out.shape[1:], lambda i: (i, 0, 0)),
        compiler_params=params(),
        cost_estimate=cost(1, 1),
        name="by_owner",
    )(*weights)


def by_columns(grads, hidden):
    blocks, unit, n = grads.shape
    starts = (0, hidden, 2 * hidden + LANES)
    if hidden % LANES:
        return [
            grads[:, :, start : start + hidden]
            .transpose(1, 0, 2)
            .reshape(unit, blocks * hidden)
            .astype(F32)
            for start in starts
        ]

    def kernel(ref, *outs):
        for start, out in zip(starts, outs):
            out[...] = ref[0, :, start : start + hidden].astype(F32)

    outs = [struct((unit, blocks * hidden), F32) for _ in starts]
    return pl.pallas_call(
        kernel,
        out_shape=outs,
        grid=(blocks,),
        in_specs=[pl.BlockSpec((1, unit, n), lambda i: (i, 0, 0))],
        out_specs=[pl.BlockSpec((unit, hidden), lambda i: (0, i)) for _ in starts],
        compiler_params=params(limit=24 * 1024 * 1024),
        cost_estimate=cost(0, nbytes([grads, *outs])),
        name="by_columns",
    )(grads)


def norm_back(values, pieces, scale, gain, gain_grad, outs, width):
    part = pieces[0].shape[1]
    cuts = [slice(k * part, (k + 1) * part) for k in range(len(pieces))]
    inner = 0.0
    for value, piece, cut in zip(values, pieces, cuts):
        gain_grad[:, cut] = jnp.sum(value * (piece * scale), axis=0, keepdims=True)
        inner = inner + jnp.sum(value * gain[:, cut] * piece, axis=1, keepdims=True)
    inner = inner * (scale * scale * scale / width)
    for value, piece, cut, out in zip(values, pieces, cuts, outs):
        out[...] = (value * gain[:, cut] * scale - piece * inner).astype(out.dtype)


def second_norm_back(received, pieces, gain):
    parts, blocks = len(pieces), len(received)
    tokens, width = received[0].shape
    part = width // parts
    outs = [struct((tokens, part), F32 if k == 0 else BF16) for k in range(parts)]
    outs.append(struct((1, width), F32))

    def kernel(*refs):
        got, refs = refs[:blocks], refs[blocks:]
        ins, (gain_ref, *outs, gain_grad) = refs[:parts], refs[parts:]
        values = []
        for k in range(parts):
            cut = slice(k * part, (k + 1) * part)
            values.append(sum(ref[:, cut].astype(F32) for ref in got))
        pieces = [ref[...].astype(F32) for ref in ins]
        scale = rms_scale(pieces, width)
        norm_back(values, pieces, scale, gain_ref, gain_grad, outs, width)

    ins = (*received, *pieces, gain)
    return pl.pallas_call(
        kernel,
        out_shape=outs,
        in_specs=[whole(a.shape) for a in ins],
        out_specs=[whole(o.shape) for o in outs],
        grid=(1,),
        compiler_params=params(limit=24 * 1024 * 1024),
        cost_estimate=cost(tokens * width * 20, nbytes(ins)),
        name="second_norm_back",
    )(*ins)


def project_back(
    at, grad_q, grad_kv, pre, pieces, gain, pair, query_gain, key_gain, cosine, sine, heads, kv_heads, gain_grad_two, router, experts
):
    parts, runs, blocks = len(pieces), len(grad_q), len(grad_kv)
    tokens, n = pre.shape
    width = gain.shape[1]
    part = width // parts
    size = query_gain.shape[1]
    gain_lines = -(-(2 * parts + 1) // 16) * 16
    lines = gain_lines + -(-experts // 16) * 16
    router_rows = router.shape[0]
    outs = [struct((tokens, part), F32)] + [struct((tokens + lines, part), BF16)] * (parts - 1)
    outs += [struct((tokens, n), BF16), struct((lines, part), F32)]

    def kernel(at_ref, pre_ref, two_ref, router_ref, *refs):
        gq, refs = refs[:runs], refs[runs:]
        gkv, refs = refs[:blocks], refs[blocks:]
        ins, refs = refs[:parts], refs[parts:]
        weights, refs = taken(refs, pair)
        gain_ref, qg, kg, cos_ref, sin_ref, *refs = refs
        outs, (d_wide, sums, gain_grad, full, sems) = refs[:parts], refs[parts:]
        for copy in weight_copies(at_ref, [weights], [full], sems, parts):
            copy.start()
        cosine, sine = cos_ref[...], sin_ref[...]
        totals = [jnp.zeros((1, size), F32), jnp.zeros((1, size), F32)]
        for i in range(n // size):
            cut = slice(i * size, (i + 1) * size)
            if i < heads:
                grad = jnp.concatenate([ref[:, cut] for ref in gq], axis=0)
            else:
                kv_cut = slice((i - heads) * size, (i - heads + 1) * size)
                grad = sum(ref[:, kv_cut].astype(F32) for ref in gkv)
            if i < heads + kv_heads:
                which = 0 if i < heads else 1
                gain_row = (qg, kg)[which][...]
                grad = grad * cosine + pltpu.roll(grad * sine, size // 2, 1)
                head = pre_ref[:, cut]
                scale = lax.rsqrt(jnp.mean(head * head, axis=1, keepdims=True) + EPS)
                unit = head * scale
                totals[which] = totals[which] + jnp.sum(grad * unit, axis=0, keepdims=True)
                grad = grad * gain_row
                grad = scale * (grad - unit * jnp.mean(grad * unit, axis=1, keepdims=True))
            d_wide[:, cut] = grad.astype(BF16)
        weight_wait([weights], [full], sems, parts)
        values = [
            dot_bt(d_wide[...], full[k * part : (k + 1) * part]) for k in range(parts)
        ]
        pieces = [ref[...].astype(F32) for ref in ins]
        scale = rms_scale(pieces, width)
        cut_outs = [outs[0]] + [out.at[:tokens] for out in outs[1:]]
        norm_back(values, pieces, scale, gain_ref, gain_grad, cut_outs, width)
        sums[...] = jnp.zeros_like(sums)
        for i, ref in enumerate((gain_grad, two_ref)):
            for k in range(parts):
                sums[i * parts + k : i * parts + k + 1] = ref[:, k * part : (k + 1) * part]
        for i, total in enumerate(totals):
            sums[2 * parts : 2 * parts + 1, i * size : (i + 1) * size] = total
        sums[gain_lines : gain_lines + experts, :router_rows] = router_ref[...].T[:experts]
        for out in outs[1:]:
            out[tokens:] = sums[...].astype(BF16)

    ins = (pre, gain_grad_two, router, *grad_q, *grad_kv, *pieces, *flat_pair(pair))
    ins = (*ins, gain, query_gain, key_gain, cosine, sine)
    return pl.pallas_call(
        kernel,
        out_shape=outs,
        in_specs=[SMEM]
        + [whole(a.shape) for a in (pre, gain_grad_two, router, *grad_q, *grad_kv)]
        + [whole((tokens, part)) for _ in pieces]
        + [ANY] * len(flat_pair(pair))
        + [whole(a.shape) for a in (gain, query_gain, key_gain, cosine, sine)],
        out_specs=[whole(o.shape) for o in outs],
        scratch_shapes=[pltpu.VMEM((1, width), F32), full_weight(pair), weight_sems(pair)],
        grid=(1,),
        compiler_params=params(),
        cost_estimate=cost(2 * tokens * width * n, nbytes(ins)),
        name="project_back",
    )(at, *ins)


def sum_blocks(grads, widths, first=0):
    blocks = len(grads)
    unit = grads[0].shape[-2]

    def kernel(*refs):
        ins, outs = refs[:blocks], refs[blocks:]
        start = first
        for out in outs:
            cut = slice(start, start + out.shape[1])
            parts = [ref[:, cut] if len(ref.shape) == 2 else ref[0, :, cut] for ref in ins]
            out[...] = sum(a.astype(F32) for a in parts)
            start = cut.stop

    def spec(i, a):
        if a.ndim == 2:
            return whole(a.shape)
        return pl.BlockSpec((1,) + a.shape[1:], lambda _: (i, 0, 0))

    outs = [struct((unit, width), F32) for width in widths]
    return pl.pallas_call(
        kernel,
        out_shape=outs,
        grid=(1,),
        in_specs=[spec(i, a) for i, a in enumerate(grads)],
        out_specs=[whole(o.shape) for o in outs],
        compiler_params=params(limit=24 * 1024 * 1024),
        cost_estimate=cost(1, 1),
        name="sum_blocks",
    )(*grads)


def finish(at, residual, own, arrived, own_sums, low, unit_rows, experts):
    others = len(arrived)
    tokens, part = own.shape
    parts, half = others + 1, part // 2
    unit = half // low
    lines = own_sums.shape[0]
    gain_lines = -(-(2 * parts + 1) // 16) * 16

    def kernel(at_ref, residual, own, *refs):
        arrived, refs = refs[:others], refs[others:]
        own_sums, out, sums, router = refs
        even, col = at_ref[3] == 0, at_ref[4]

        def put(ref, rows, value):
            first = jnp.where(even, value[:, :half], value[:, half:])
            second = jnp.where(even, value[:, half:], value[:, :half])
            for i in range(low):
                cut = slice(i * unit, (i + 1) * unit)
                ref[rows, 2 * i * unit : (2 * i + 1) * unit] = first[:, cut].astype(ref.dtype)
                ref[rows, (2 * i + 1) * unit : (2 * i + 2) * unit] = second[:, cut].astype(ref.dtype)

        value = residual[...] + own[...]
        for ref in arrived:
            value = value + ref[:tokens].astype(F32)
        put(out, slice(0, tokens), value)
        got = [ref[tokens:].astype(F32) for ref in arrived]
        total = own_sums[...]
        for a in got:
            total = total + a
        sums[...] = total[:gain_lines]
        router[...] = total[gain_lines : gain_lines + experts, :unit_rows].T
        for i in range(2):
            for k in range(parts):
                line = own_sums[i * parts + k : i * parts + k + 1]
                for mask, a in enumerate(got, 1):
                    row = i * parts + (k ^ mask)
                    line = line + a[row : row + 1]
                for to in range(parts):

                    @pl.when(col ^ k == to)
                    def _(i=i, to=to, line=line):
                        put(sums, slice(i * parts + to, i * parts + to + 1), line)

    outs = (
        struct((tokens, part), BF16),
        struct((gain_lines, part), F32),
        struct((unit_rows, experts), F32),
    )
    ins = (residual, own, *arrived, own_sums)
    return pl.pallas_call(
        kernel,
        out_shape=outs,
        grid=(1,),
        in_specs=[SMEM] + [whole(a.shape) for a in ins],
        out_specs=[whole(o.shape) for o in outs],
        compiler_params=params(limit=24 * 1024 * 1024),
        cost_estimate=cost(1, 1),
        name="finish",
    )(at, *ins)


def per_device(
    layer_in,
    out_grad,
    lengths,
    token_order,
    choices,
    norm_gain,
    w_query,
    w_key,
    w_value,
    query_gain,
    key_gain,
    w_out,
    ffn_gain,
    w_router,
    w_gate,
    w_up,
    w_down,
):
    micro, tok, part = layer_in.shape
    outer, cols = lax.axis_size("outer"), lax.axis_size("col")
    rows = 2 * outer
    tokens = micro * tok
    width = part * cols
    outer_at, core_at, col_at = (lax.axis_index(name) for name in ("outer", "core", "col"))
    row_at = outer_at * 2 + core_at
    low = outer // cols
    unit = width // rows
    half = part // 2
    size = query_gain.shape[0]
    heads = w_query.shape[1] // size
    kv_heads = w_key.shape[1] // size
    experts = w_router.shape[1]
    hidden = w_gate.shape[1] // outer
    repeats = hidden // experts

    place = outer_at ^ (col_at * low)
    at = jnp.stack([place, outer_at, col_at * low, core_at, col_at]).astype(jnp.int32)

    def core_swap(a):
        return lax.ppermute(a, "core", [(0, 1), (1, 0)])

    def col_swap(a, mask):
        return lax.ppermute(a, "col", [(i, i ^ mask) for i in range(cols)])

    def exchange(a):
        return lax.all_to_all(a, "outer", 0, 0, tiled=True)

    def for_all(a):
        return jnp.broadcast_to(a[None], (outer,) + a.shape)

    def after(a, b):
        return lax.optimization_barrier((a, b))[0]

    def to_halves(a):
        blocks = a.reshape(a.shape[:-1] + (low, 2, unit))
        first = blocks[..., 0, :].reshape(a.shape[:-1] + (half,))
        second = blocks[..., 1, :].reshape(a.shape[:-1] + (half,))
        even = core_at == 0
        return jnp.concatenate(
            [jnp.where(even, first, second), jnp.where(even, second, first)], axis=-1
        )

    def from_halves(a):
        even = core_at == 0
        first = jnp.where(even, a[..., :half], a[..., half:]).reshape(a.shape[:-1] + (low, unit))
        second = jnp.where(even, a[..., half:], a[..., :half]).reshape(a.shape[:-1] + (low, unit))
        return jnp.stack([first, second], axis=-2).reshape(a.shape)

    def col_gather(a):
        return [a] + [col_swap(a, k) for k in range(1, cols)]

    def col_total(pieces):
        total = pieces[0]
        for k in range(1, cols):
            total = total + col_swap(pieces[k], k).astype(F32)
        return total

    def swap(a, mask):
        return lax.ppermute(a, "outer", [(i, i ^ mask) for i in range(outer)])

    def gather(a):
        return [a] + [swap(a, j) for j in range(1, outer)]

    def scatter(blocks):
        return [blocks[0]] + [swap(blocks[j], j) for j in range(1, outer)]

    def swap(a, mask):
        return lax.ppermute(a, "outer", [(i, i ^ mask) for i in range(outer)])

    def gather(a):
        return [a] + [swap(a, j) for j in range(1, outer)]

    def scatter(blocks):
        return [blocks[0]] + [swap(blocks[j], j) for j in range(1, outer)]

    def both(*arrays):
        return lax.optimization_barrier(arrays)

    def both_cores(a):
        return a, [core_swap(b) for b in a] if isinstance(a, list) else core_swap(a)

    own_in = to_halves(layer_in).reshape(tokens, part)
    own_grad = to_halves(out_grad).reshape(tokens, part)
    w_in = gather(jnp.concatenate([w_query, w_key, w_value], axis=1))
    arrived = col_gather(own_in)
    w_back = jnp.concatenate([w_out, jnp.pad(w_router, ((0, 0), (0, LANES - experts)))], axis=1)
    w_back = for_all(w_back)
    weights = by_owner([w_gate, w_up, w_down], outer)
    q_gain, k_gain = query_gain[None, :], key_gain[None, :]
    frequency = jnp.exp(jnp.arange(size // 2, dtype=F32) * (-2.0 * math.log(THETA) / size))
    bias, angles, chosen, spread, gain_one, gain_two = prepare(
        at,
        lengths,
        token_order.reshape(micro, rows, tok),
        choices.reshape(tokens, -1),
        jnp.concatenate([frequency, frequency])[None, :],
        jnp.stack([norm_gain, ffn_gain]).reshape(2, cols, part),
        low,
        hidden,
        experts,
    )
    cosine = jnp.cos(angles)
    sine = jnp.sin(angles) * jnp.where(jnp.arange(size) < size // 2, -1.0, 1.0)

    w_back, weights, bias = both(w_back, weights, bias)
    w_back = exchange(w_back)
    w_in, arrived, weights, chosen, bias, cosine, sine, gain_one, gain_two, spread = both(
        w_in, arrived, weights, chosen, bias, cosine, sine, gain_one, gain_two, spread
    )
    own_grads = col_gather(after(own_grad, w_in))
    w_in = both_cores(w_in)
    normed_one, pre, ready, kv = project(
        at, arrived, part, gain_one, w_in, q_gain, k_gain, cosine, sine, heads, kv_heads
    )
    near = [j for j in range(1, outer) if not j & (j - 1)]
    far = [j for j in range(1, outer) if j & (j - 1)]
    far_grads, _ = both(jnp.concatenate([own_grad, chosen], axis=1), kv)
    far_grads = [swap(far_grads, j) for j in far]
    kv_own = jnp.stack(gather(kv))
    kv_own, w_back = both(kv_own, w_back)
    weights, far_grads, _ = both(weights, far_grads, w_back)
    weights = exchange(weights)
    kv_other = core_swap(kv_own)
    w_back = both_cores(w_back)
    attended, lse = attend(ready, kv_own, kv_other, bias, heads, kv_heads, size)
    attn_parts = expand(at, attended, w_back, part, cols)
    attn_parts, own_grads = both(attn_parts, own_grads)

    grads = [jnp.concatenate(own_grads + [chosen], axis=1)] + [None] * (outer - 1)
    near_grads = [swap(grads[0], j) for j in near]

    residual = own_in.astype(F32) + col_total(attn_parts)
    residual, weights = both(residual, weights)
    full_res = col_gather(residual.astype(BF16))
    full_res, near_grads, weights = both(full_res, near_grads, weights)
    for j, a in zip(near, near_grads):
        grads[j] = a
    weights = both_cores(weights)
    normed_two = second_norm(full_res, gain_two)
    expert_in = gather(normed_two)
    far_grads, _ = both(far_grads, normed_two)
    for j, a in zip(far, far_grads):
        grads[j] = jnp.concatenate(col_gather(a[:, :part]) + [a[:, part:]], axis=1)

    results, dx, lo_far = [], [None] * outer, []
    order = [0] + far + near
    for group in [[0]] + [far[i : i + 4] for i in range(0, len(far), 4)] + [near]:
        *result, dx_now, lo_now = run_experts(
            at,
            [expert_in[j] for j in group],
            [grads[j] for j in group],
            spread,
            weights,
            w_back,
            heads * size,
            cols,
            group[0] in far,
        )
        for j, a in zip(group, dx_now):
            dx[j] = a
        if group == [0]:
            lo_own = lo_now[0]
            expert_in, lo_own = both(expert_in, lo_own)
        elif group != near:
            lo_far += lo_now
            for j in group:
                dx[j] = swap(dx[j], j)
        else:
            lo_near = lo_now
        results.append(result)
    far_dx, results[-1], lo_far = both([dx[j] for j in far], results[-1], lo_far)
    lo_far = [col_total([a[0].astype(F32), *a[1:]]).astype(BF16) for a in lo_far]
    weighted, d_high, logit_low = [list(arrays) for arrays in zip(*results)]
    near_dx, far_dx = both([dx[j] for j in near], far_dx)
    for j, a in zip(near, near_dx):
        dx[j] = swap(a, j)
    sizes = (cols, outer, part)
    expert_sides = (
        [[expert_in[j] for j in order], [grads[j] for j in order]],
        [[d_high, logit_low], [weighted]],
    )
    (other,) = weight_grads(at, place, outer_at, 1, *expert_sides, *sizes, joined=True)
    other, near_dx, lo_far, lo_near = both(other, [dx[j] for j in near], lo_far, lo_near)
    other = core_swap(other)
    *spread_two, gain_grad_two = second_norm_back([dx[0]] + near_dx + far_dx, full_res, gain_two)
    lo_near = [swap(a, j) for j, a in zip(near, lo_near)]
    (expert_grads,) = weight_grads(
        at, place, outer_at, 0, *expert_sides, *sizes, [other], True, True
    )
    spread_two[0], expert_grads = both(spread_two[0], expert_grads)
    grad_residual = own_grad.astype(F32) + col_total(spread_two)
    grad_residual, lo_near, expert_grads = both(grad_residual, lo_near, expert_grads)
    expert_grads = exchange(expert_grads)
    grad_feats = col_gather(grad_residual.astype(BF16))

    lo_near = lo_own.astype(F32) + sum(a.astype(F32) for a in lo_near)
    lo_near = [
        lo_near[:, k * part : (k + 1) * part].astype(F32 if k == 0 else BF16) for k in range(cols)
    ]
    grad_feats, lo_near = both(grad_feats, lo_near)
    back_attended, feats = contract(at, grad_feats, w_back, heads * size)
    lo_near = col_total(after(lo_near, back_attended))
    grad_q, kv_mine, kv_theirs = attend_back(
        ready, kv_own, kv_other, bias, lse, back_attended, heads, kv_heads, size
    )
    kv_theirs, expert_grads = both(kv_theirs, expert_grads)
    kv_sums = sum_cores(kv_mine, core_swap(kv_theirs))
    grad_kv = scatter(kv_sums)
    router_part = jnp.sum(
        expert_grads[:, :, 2 * hidden : 2 * hidden + LANES].astype(F32), axis=0
    )
    feats, lo_near, _ = both(feats, lo_near, grad_q)
    (other,) = weight_grads(at, place, outer_at, 1, [[feats]], [[[attended]]], *sizes)
    (out_grads,) = weight_grads(
        at, place, outer_at, 0, [[feats]], [[[attended]]], *sizes, [core_swap(other)], True
    )
    grad_kv, out_grads, lo_far = both(grad_kv, out_grads, lo_far)
    lo_far = [swap(a, j) for j, a in zip(far, lo_far)]
    out_grads = exchange(out_grads)
    *spread_one, d_wide, sums = project_back(
        at,
        [grad_q],
        grad_kv,
        pre,
        arrived,
        gain_one,
        w_in,
        q_gain,
        k_gain,
        cosine,
        sine,
        heads,
        kv_heads,
        gain_grad_two,
        router_part,
        experts,
    )
    (other,) = weight_grads(at, place, outer_at, 1, [[normed_one]], [[[d_wide]]], *sizes)
    other, expert_grads, lo_far = both(other, expert_grads, lo_far)
    grad_gate_w, grad_up_w, grad_down_w = by_columns(expert_grads, hidden)
    other = jnp.stack([core_swap(other[j]) for j in range(outer)])
    other, grad_gate_w = both(other, grad_gate_w)
    (wide_grads,) = weight_grads(
        at, place, outer_at, 0, [[normed_one]], [[[d_wide]]], *sizes, [other], True
    )
    spread_one, wide_grads, out_grads = both(spread_one, wide_grads, out_grads)
    wide_grads = exchange(wide_grads)

    got = [col_swap(spread_one[k], k) for k in range(1, cols)]
    layer_out = residual + lo_near + sum(a.astype(F32) for a in lo_far)
    layer_out = from_halves(layer_out.astype(BF16)).reshape(micro, tok, part)
    (grad_out_w,) = sum_blocks([out_grads] * outer, [heads * size])
    got, grad_out_w, layer_out = both(got, grad_out_w, layer_out)
    input_grad, sums, grad_router = finish(
        at, grad_residual, spread_one[0], got, sums, low, unit, experts
    )
    input_grad = input_grad.reshape(micro, tok, part)
    sums = sums + core_swap(sums)
    sums = gather(sums)
    wide_grads, input_grad, layer_out, grad_out_w, grad_router = both(
        wide_grads, input_grad, layer_out, grad_out_w, grad_router
    )
    grad_query_w, grad_key_w, grad_value_w = sum_blocks(
        [wide_grads] * outer, [w.shape[1] for w in (w_query, w_key, w_value)]
    )
    sums, _ = both(sums, grad_query_w)
    sums = sum(sums)
    head_sums = sums[2 * cols, : 2 * size]
    grad_norm_gain, grad_ffn_gain = sums[:cols].reshape(width), sums[cols : 2 * cols].reshape(width)
    grad_query_gain, grad_key_gain = head_sums[:size], head_sums[size:]
    return (
        layer_out,
        input_grad,
        grad_norm_gain,
        grad_query_w,
        grad_key_w,
        grad_value_w,
        grad_query_gain,
        grad_key_gain,
        grad_out_w,
        grad_ffn_gain,
        grad_router,
        grad_gate_w,
        grad_up_w,
        grad_down_w,
    )


def solution(mesh):
    rows, cols = mesh.devices.shape
    split = Mesh(mesh.devices.reshape(rows // 2, 2, cols), ("outer", "core", "col"))
    tokens_placed = P(None, ROW, "col")
    weight_placed = P(ROW, "col")
    return jax.shard_map(
        per_device,
        mesh=split,
        in_specs=(
            tokens_placed,
            tokens_placed,
            P(),
            P(),
            P(None, ROW, None),
            P(),
            weight_placed,
            weight_placed,
            weight_placed,
            P(),
            P(),
            weight_placed,
            P(),
            P(ROW, None),
            weight_placed,
            weight_placed,
            weight_placed,
        ),
        out_specs=(
            tokens_placed,
            tokens_placed,
            P(),
            weight_placed,
            weight_placed,
            weight_placed,
            P(),
            P(),
            weight_placed,
            P(),
            P(ROW, None),
            weight_placed,
            weight_placed,
            weight_placed,
        ),
        check_vma=False,
    )
```
